512 devices in a mesh: chan: 8 (over x, z_hi), bl: 64 (over y, z_lo, core).
Axes of the slice: x: 4, y: 4, z: 16 (z_hi: 2, z_lo: 8; z = z_hi * 8 + z_lo), core: 2. Of those that a mesh axis runs over, the one named last changes fastest.
Arguments:
- measured_correlations: float32 [8, 4, 64, 32768], P(None, None, 'chan', 'bl'), may hold values from -6 to 6
- model_visibility: float32 [8, 4, 64, 32768], P(None, None, 'chan', 'bl'), may hold values from -6 to 6
- sample_importances: float32 [4, 64, 32768], P(None, 'chan', 'bl'), may hold values from 0.2 to 2
- rejected_frequency_tally: int32 [8, 32768], P('chan', 'bl'), may hold values from 0 to 4
- antenna_one: int32 [32768], P('bl'), may hold values from 0 to 511, as said below
- antenna_two: int32 [32768], P('bl'), may hold values from 0 to 511, as said below
- station_gains: float32 [8, 4, 64, 512], P(None, None, 'chan', 'bl'), may hold values from -3 to 3
- tv_weight: float32 [64, 512], P('chan', 'bl'), may hold values from 0.3 to 3
Outputs:
- updated_gains: float32 [8, 4, 64, 512], P(None, None, 'chan', 'bl')
- weighted_residual: float32 [8, 4, 64, 32768], P(None, None, 'chan', 'bl')
The draws below stay inside these ranges and needn't reach their ends.
Inputs may be any that keep to these rules, and one draw needn't show every extreme that they name: `antenna_one`: station index of each baseline's first station. `antenna_two`: station index of each baseline's second station, never equal to antenna_one on the same baseline.
All inputs are finite; a program needn't handle non-finite values.
Results may differ from the reference program's by a relative error of at most 0.000098.
Values sent between devices are 32-bit elements; how exact they have to be, the bound alone decides.
A program may use at most 128 MiB of HBM per device.

```python
import math
import jax
import jax.numpy as jnp
from jax import lax

STATION_COUNT = 512
TIME_INTERVALS = 4
BLOCK_CHANNELS = 8
CHANNEL_COUNT = 64
BASELINE_COUNT = 32768
CHANNEL_BLOCKS = 8


def station_pairs(key):
    leading_entry = jax.random.randint(jax.random.fold_in(key, 11), (BASELINE_COUNT,), 0, STATION_COUNT)
    channel_offset = jax.random.randint(jax.random.fold_in(key, 12), (BASELINE_COUNT,), 1, STATION_COUNT)
    second = (leading_entry + channel_offset) % STATION_COUNT
    return (leading_entry, second)


def draw_antenna_one(key, part):
    leading_entry, second = station_pairs(key)
    return leading_entry.astype(jnp.int32)


def draw_antenna_two(key, part):
    leading_entry, second = station_pairs(key)
    return second.astype(jnp.int32)


def place_ends(entries, rng, low, top_value):
    shape = entries.shape
    place = [jax.random.randint(jax.random.fold_in(rng, axis), (), 0, shape[axis]) for axis in range(len(shape))]
    entries = entries.at[tuple(place)].set(low)
    longest = shape.index(max(shape))
    place[longest] = (place[longest] + 1) % shape[longest]
    return entries.at[tuple(place)].set(top_value)


def steps_of(stream_key, dims, shards, smallest, high):
    def one(dim, shards_of):
        steps = jax.random.uniform(jax.random.fold_in(jax.random.fold_in(stream_key, 6), dim), (shards_of,), jnp.float32, smallest / len(shards), high / len(shards))
        return jnp.repeat(jnp.exp(steps), dims[dim] // shards_of).reshape((-1,) + (1,) * (len(dims) - dim - 1))

    loudness = one(*shards[0])
    for cut in shards[1:]:
        loudness = loudness * one(*cut)
    return loudness


def gaussian(rng, extent, scale, most, split=(), kind=jnp.bfloat16):
    drawn = jax.random.normal(rng, extent, jnp.float32) * scale
    if len(split) > 0:
        drawn = steps_of(rng, extent, split, -0.22, 0.18) * drawn
    return jnp.clip(drawn, min=-most, max=most).astype(kind)


def setup_inputs(seed: int = 0) -> dict:
    keys = jax.random.split(jax.random.key(seed), 9)
    measured_correlations = gaussian(keys[0], (8, TIME_INTERVALS, CHANNEL_COUNT, BASELINE_COUNT), 1.0, 6.0, ((2, 8), (3, 64)), jnp.float32)
    model_visibility = gaussian(keys[1], (8, TIME_INTERVALS, CHANNEL_COUNT, BASELINE_COUNT), 1.0, 6.0, ((2, 8), (3, 64)), jnp.float32)
    sample_importances = jnp.clip(jnp.exp(math.log(2.0) - 2.3025851 * jax.random.uniform(keys[2], (TIME_INTERVALS, CHANNEL_COUNT, BASELINE_COUNT), jnp.float32) ** steps_of(keys[2], (TIME_INTERVALS, CHANNEL_COUNT, BASELINE_COUNT), ((1, 8), (2, 64)), -0.2, 0.2)), 0.2, 2.0)
    rejected_frequency_tally = place_ends(jax.random.randint(keys[3], (CHANNEL_BLOCKS, BASELINE_COUNT), 0, BLOCK_CHANNELS // 2 + 1), jax.random.fold_in(keys[3], 1), 0, (BLOCK_CHANNELS // 2 + 1) - 1).astype(jnp.int32)
    antenna_one = draw_antenna_one(jax.random.fold_in(keys[8], 71), 0)
    antenna_two = draw_antenna_two(jax.random.fold_in(keys[8], 71), 0)
    station_gains = gaussian(keys[6], (8, TIME_INTERVALS, CHANNEL_COUNT, STATION_COUNT), 0.5, 3.0, ((2, 8), (3, 64)), jnp.float32)
    tv_weight = jnp.clip(jnp.exp(math.log(3.0) - 2.3025851 * jax.random.uniform(keys[7], (CHANNEL_COUNT, STATION_COUNT), jnp.float32) ** steps_of(keys[7], (CHANNEL_COUNT, STATION_COUNT), ((0, 8), (1, 64)), -0.2, 0.2)), 0.3, 3.0)
    return dict(measured_correlations=measured_correlations, model_visibility=model_visibility, sample_importances=sample_importances, rejected_frequency_tally=rejected_frequency_tally, antenna_one=antenna_one, antenna_two=antenna_two, station_gains=station_gains, tv_weight=tv_weight)


smooth_eps = 0.01
tv_scale = 2.0

def complex_product(left, right):
    real_parts = []
    imag_parts = []
    for left_idx in range(2):
        for right_idx in range(2):
            leading_entry = 2 * left_idx
            second = 2 * left_idx + 1
            real_parts.append(left[leading_entry] * right[right_idx] - left[leading_entry + 4] * right[right_idx + 4] + left[second] * right[right_idx + 2] - left[second + 4] * right[right_idx + 6])
            imag_parts.append(left[leading_entry] * right[right_idx + 4] + left[leading_entry + 4] * right[right_idx] + left[second] * right[right_idx + 6] + left[second + 4] * right[right_idx + 2])
    return jnp.stack(real_parts + imag_parts)

def adjoint(matrix):
    return jnp.stack([matrix[0], matrix[2], matrix[1], matrix[3], -matrix[4], -matrix[6], -matrix[5], -matrix[7]])

def predicted(gain_first, model_part, gain_second):
    return complex_product(complex_product(gain_first, model_part), adjoint(gain_second))

def smoothness(gains, tv_weight):
    chan_step = gains[:, :, 1:] - gains[:, :, :-1]
    chan_term = jnp.sum(tv_weight[1:] * jnp.sqrt(lax.optimization_barrier(jnp.sum(chan_step * chan_step, axis=0)) + smooth_eps))
    time_step = gains[:, 1:] - gains[:, :-1]
    time_term = jnp.sum(tv_weight * jnp.sqrt(lax.optimization_barrier(jnp.sum(time_step * time_step, axis=0)) + smooth_eps))
    return chan_term + time_term

def reference(measured_correlations, model_visibility, sample_importances, rejected_frequency_tally, antenna_one, antenna_two, station_gains, tv_weight):
    frequency_index_within = (jnp.arange(CHANNEL_COUNT, dtype=jnp.int32) % BLOCK_CHANNELS)[:, None]
    limit = BLOCK_CHANNELS - jnp.repeat(rejected_frequency_tally, BLOCK_CHANNELS, axis=0)
    nonzero_importance = sample_importances * (frequency_index_within < limit).astype(jnp.float32)[None]

    def per_interval(items):
        vis_part, model_part, weight_part, gain_part = items
        gain_first = jnp.take(gain_part, antenna_one, axis=2)
        gain_second = jnp.take(gain_part, antenna_two, axis=2)

        def data_loss(leading_entry, second):
            diff = vis_part - predicted(leading_entry, model_part, second)
            return 0.5 * jnp.sum(weight_part[None] * diff * diff)
        residual = weight_part[None] * (vis_part - predicted(gain_first, model_part, gain_second))
        value, pullback = jax.vjp(data_loss, gain_first, gain_second)
        grad_first, grad_second = pullback(jnp.ones_like(value))
        blank = jnp.zeros(gain_part.shape, jnp.float32)
        grad_table = blank.at[:, :, antenna_one].add(grad_first).at[:, :, antenna_two].add(grad_second)
        return (residual, grad_table)
    residuals, grad_tables = lax.map(per_interval, (measured_correlations.transpose(1, 0, 2, 3), model_visibility.transpose(1, 0, 2, 3), nonzero_importance, station_gains.transpose(1, 0, 2, 3)))
    weighted_residual = residuals.transpose(1, 0, 2, 3)
    data_grad = grad_tables.transpose(1, 0, 2, 3)
    smooth_grad = jax.grad(smoothness)(station_gains, tv_weight)
    descent_scale = 2.0 * STATION_COUNT / BASELINE_COUNT
    updated_gains = station_gains - descent_scale * (data_grad + tv_scale * smooth_grad)
    return (updated_gains, weighted_residual)
```

```python
import jax
import jax.numpy as jnp
from jax import lax
from jax.experimental import pallas as pl
from jax.experimental.pallas import tpu as pltpu
from jax.sharding import PartitionSpec as P

MESH = pl.DeviceIdType.MESH
STATIONS = 512
BASELINES = 32768
TIMES = 4
CHANNELS = 8
PAIRS = 512
LANES = 8 * TIMES * CHANNELS
NY, NZ, NC = 4, 8, 2
SMOOTH_EPS = 0.01
TV_SCALE = 2.0
STEP = 2.0 * STATIONS / BASELINES
F32 = jnp.float32
BF16 = jnp.bfloat16


def cmul_add(terms):
    real, imag = None, None
    for (ar, ai), (br, bi), conj in terms:
        if conj:
            r, i = ar * br + ai * bi, ai * br - ar * bi
        else:
            r, i = ar * br - ai * bi, ar * bi + ai * br
        real = r if real is None else real + r
        imag = i if imag is None else imag + i
    return real, imag


def halves(x):
    high = x.astype(BF16)
    return high, (x - high.astype(F32)).astype(BF16)


def split_index():
    bl = lax.axis_index("bl")
    return lax.div(bl, NZ * NC), lax.rem(lax.div(bl, NC), NZ), lax.rem(bl, NC)


def join_index(y, z, core):
    return (y * NZ + z) * NC + core


def row_of(y, z, core):
    return pl.multiple_of(((core * NY + y) * NZ + z) * 8, 8)


def kernel(
    meas_h, model_h, imp_h, tally_h, one_h, two_h, gains_h, tvw_h,
    upd_ref, res_h,
    meas, model, imp, tally, one, two, gains, tvw,
    table, hot1, hot2, gp, gq, res, part, got_core, got_y, got_z, halo, halo_got, smooth, own_x,
    in_sem, out_sem, zs, zr, ys, yr, cs, cr, hs, hr, rcs, rcr, rys, ryr, rzs, rzr,
):
    chan = lax.axis_index("chan")
    y, z, core = split_index()
    n_chan = lax.axis_size("chan")

    def to_bl(src, dst, send, recv, peer):
        return pltpu.make_async_remote_copy(
            src_ref=src, dst_ref=dst, send_sem=send, recv_sem=recv,
            device_id={"bl": peer}, device_id_type=MESH,
        )

    z_peer = [None] + [join_index(y, lax.rem(z + k, NZ), core) for k in range(1, NZ)]
    y_peer = [None] + [join_index(lax.rem(y + k, NY), z, core) for k in range(1, NY)]
    other = join_index(y, z, 1 - core)
    chan_next = lax.rem(chan + 1, n_chan)
    chan_prev = lax.rem(chan + n_chan - 1, n_chan)

    loads = [
        pltpu.make_async_copy(src, dst, in_sem.at[i])
        for i, (src, dst) in enumerate(
            [(gains_h, gains), (one_h, one), (two_h, two), (tvw_h, tvw), (tally_h, tally),
             (imp_h, imp), (meas_h, meas), (model_h, model)]
        )
    ]
    loads[0].start()
    barrier = pltpu.get_barrier_semaphore()
    for peer in z_peer[1:] + y_peer[1:] + [other]:
        pl.semaphore_signal(barrier, inc=1, device_id={"bl": peer}, device_id_type=MESH)
    for peer in (chan_next, chan_prev):
        pl.semaphore_signal(barrier, inc=1, device_id={"chan": peer}, device_id_type=MESH)
    for load in loads[1:]:
        load.start()

    own_row = row_of(y, z, core)
    loads[0].wait()
    own = jnp.transpose(gains[...].reshape(LANES, 8))
    own_x[...] = own
    table[pl.ds(own_row, 8), :] = own
    pl.semaphore_wait(barrier, NZ + NY + 1)

    z_sends = []
    for k in range(1, NZ):
        rows = table.at[pl.ds(own_row, 8)]
        copy = to_bl(rows, rows, zs.at[k], zr.at[k], z_peer[k])
        copy.start()
        z_sends.append(copy)

    loads[1].wait()
    loads[2].wait()

    def to_row(ant):
        return (
            (lax.shift_right_logical(ant, 3) & 1) * 256
            + lax.shift_right_logical(ant, 7) * 64
            + (lax.shift_right_logical(ant, 4) & 7) * 8
            + (ant & 7)
        )

    row1, row2 = to_row(one[...]), to_row(two[...])

    def hot_body(i, carry):
        base = pl.multiple_of(i * 32, 32)
        index = lax.broadcasted_iota(jnp.int32, (32, PAIRS), 0) + base
        hot1[pl.ds(base, 32), :] = jnp.where(index == row1, 1.0, 0.0).astype(BF16)
        hot2[pl.ds(base, 32), :] = jnp.where(index == row2, 1.0, 0.0).astype(BF16)
        return carry

    lax.fori_loop(0, 8, hot_body, 0)

    for k in range(1, NZ):
        rows = table.at[pl.ds(row_of(y, lax.rem(z + NZ - k, NZ), core), 8)]
        to_bl(rows, rows, zs.at[k], zr.at[k], z_peer[k]).wait_recv()

    column = table.at[pl.ds(row_of(y, 0, core), 64)]
    y_sends = []
    for k in range(1, NY):
        copy = to_bl(column, column, ys.at[k], yr.at[k], y_peer[k])
        copy.start()
        y_sends.append(copy)
    c_sends = [to_bl(column, column, cs.at[0], cr.at[0], other)]
    c_sends[0].start()

    loads[3].wait()
    lane = lax.broadcasted_iota(jnp.int32, (8, LANES), 1)
    freq, time = lane & 7, lax.shift_right_logical(lane, 3) & 3
    weight = jnp.transpose(
        jnp.broadcast_to(tvw[...][None], (8 * TIMES, CHANNELS, 8)).reshape(LANES, 8)
    )
    low, high = own[:, :128], own[:, 128:]
    freq_h = freq[:, :128]
    halo[...] = jnp.where(
        freq_h == 0, low,
        jnp.where(
            freq_h == 1, pltpu.roll(high, 1, 1),
            jnp.where(
                freq_h == 7, low,
                jnp.where(freq_h == 6, pltpu.roll(high, 127, 1), pltpu.roll(weight[:, :128], 2, 1)),
            ),
        ),
    )
    h_sends = []
    for k, peer in enumerate((chan_next, chan_prev)):
        copy = pltpu.make_async_remote_copy(
            src_ref=halo, dst_ref=halo_got.at[k], send_sem=hs.at[k], recv_sem=hr.at[k],
            device_id={"chan": peer}, device_id_type=MESH,
        )
        copy.start()
        h_sends.append(copy)

    lax.fori_loop(8, 16, hot_body, 0)

    for k in range(1, NY):
        rows = table.at[pl.ds(row_of(lax.rem(y + NY - k, NY), 0, core), 64)]
        to_bl(rows, rows, ys.at[k], yr.at[k], y_peer[k]).wait_recv()
        copy = to_bl(rows, rows, cs.at[k], cr.at[k], other)
        copy.start()
        c_sends.append(copy)

    loads[4].wait()
    loads[5].wait()
    keep = lax.broadcasted_iota(jnp.int32, (CHANNELS, PAIRS), 0) < CHANNELS - tally[...]
    for t in range(TIMES):
        imp[t] = jnp.where(keep, imp[t], 0.0)

    for k in range(NY):
        rows = table.at[pl.ds(row_of(lax.rem(y + NY - k, NY), 0, 1 - core), 64)]
        to_bl(rows, rows, cs.at[k], cr.at[k], other).wait_recv()

    flipped = jnp.transpose(table[...])
    g_high, g_low = halves(flipped)
    for hot, dst in ((hot1, gp), (hot2, gq)):
        picked = jnp.dot(g_high, hot[...], preferred_element_type=F32) + jnp.dot(
            g_low, hot[...], preferred_element_type=F32
        )
        dst[...] = picked.reshape(8, TIMES, CHANNELS, PAIRS)
    loads[6].wait()
    loads[7].wait()

    def compute(i, carry):
        t = lax.div(i, 4)
        at = pl.ds(pl.multiple_of(lax.rem(i, 4) * 128, 128), 128)

        def matrix(ref):
            return [(ref[c, t, :, at], ref[c + 4, t, :, at]) for c in range(4)]

        jp, jq, m, d = matrix(gp), matrix(gq), matrix(model), matrix(meas)
        w = imp[t, :, at]
        a = [
            cmul_add([(jp[2 * r], m[c], False), (jp[2 * r + 1], m[c + 2], False)])
            for r in range(2) for c in range(2)
        ]
        v = [
            cmul_add([(a[2 * r], jq[2 * c], True), (a[2 * r + 1], jq[2 * c + 1], True)])
            for r in range(2) for c in range(2)
        ]
        e = [(w * (d[k][0] - v[k][0]), w * (d[k][1] - v[k][1])) for k in range(4)]
        for k in range(4):
            res[k, t, :, at] = e[k][0]
            res[k + 4, t, :, at] = e[k][1]
        b = [
            cmul_add([(jq[2 * r], m[2 * c], True), (jq[2 * r + 1], m[2 * c + 1], True)])
            for r in range(2) for c in range(2)
        ]
        first = [
            cmul_add([(e[2 * r], b[c], False), (e[2 * r + 1], b[c + 2], False)])
            for r in range(2) for c in range(2)
        ]
        second = [
            cmul_add([(a[c], e[r], True), (a[c + 2], e[r + 2], True)])
            for r in range(2) for c in range(2)
        ]
        for k in range(4):
            gp[k, t, :, at] = first[k][0]
            gp[k + 4, t, :, at] = first[k][1]
            gq[k, t, :, at] = second[k][0]
            gq[k + 4, t, :, at] = second[k][1]
        return carry

    lax.fori_loop(0, 16, compute, 0)
    store = pltpu.make_async_copy(res, res_h, out_sem.at[0])
    store.start()

    p_high, p_low = halves(gp[...].reshape(LANES, PAIRS))
    q_high, q_low = halves(gq[...].reshape(LANES, PAIRS))
    nt = (((1,), (1,)), ((), ()))

    def add_up(rows):
        h1, h2 = hot1[rows, :], hot2[rows, :]
        total = lax.dot_general(h1, p_high, nt, preferred_element_type=F32)
        total += lax.dot_general(h1, p_low, nt, preferred_element_type=F32)
        total += lax.dot_general(h2, q_high, nt, preferred_element_type=F32)
        total += lax.dot_general(h2, q_low, nt, preferred_element_type=F32)
        part[rows, :] = total

    theirs = pl.multiple_of((1 - core) * 256, 256)
    mine = pl.multiple_of(core * 256, 256)
    add_up(pl.ds(theirs, 256))
    rc_sends = []
    for k in (1, 2, 3, 0):
        y_to = lax.rem(y + k, NY)
        copy = to_bl(
            part.at[pl.ds(row_of(y_to, 0, 1 - core), 64)], got_core.at[k],
            rcs.at[k], rcr.at[k], other,
        )
        copy.start()
        rc_sends.append(copy)
    add_up(pl.ds(mine, 256))
    ry_sends = []
    for k in (1, 2, 3, 0):
        at = pl.ds(row_of(lax.rem(y + k, NY), 0, core), 64)
        to_bl(part.at[at], got_core.at[k], rcs.at[k], rcr.at[k], other).wait_recv()
        part[at, :] = part[at, :] + got_core[k]
        if k:
            copy = to_bl(part.at[at], got_y.at[k], rys.at[k], ryr.at[k], y_peer[k])
            copy.start()
            ry_sends.append(copy)

    for k in range(2):
        pltpu.make_async_remote_copy(
            src_ref=halo, dst_ref=halo_got.at[k], send_sem=hs.at[k], recv_sem=hr.at[k],
            device_id={"chan": (chan_next, chan_prev)[k]}, device_id_type=MESH,
        ).wait_recv()
    from_prev, from_next = halo_got[0], halo_got[1]
    x = own_x[...]

    def shift(v, by):
        return pltpu.roll(v, by % LANES, 1)

    prev_edge = jnp.concatenate([pltpu.roll(from_prev, 121, 1), pltpu.roll(from_prev, 122, 1)], axis=1)
    next_edge = jnp.concatenate([pltpu.roll(from_next, 7, 1), pltpu.roll(from_next, 6, 1)], axis=1)
    next_weight = jnp.concatenate([pltpu.roll(from_next, 5, 1)] * 2, axis=1)
    is_first, is_last = freq == 0, freq == CHANNELS - 1
    not_low = jnp.where(chan > 0, 1.0, 0.0).astype(F32)
    not_high = jnp.where(chan < n_chan - 1, 1.0, 0.0).astype(F32)

    def slope(w, step):
        square = step * step
        for by in (128, 64, 32):
            square = square + shift(square, by)
        return w * step / jnp.sqrt(square + SMOOTH_EPS)

    grad = slope(
        jnp.where(is_first, weight * not_low, weight), x - jnp.where(is_first, prev_edge, shift(x, 1))
    )
    grad -= slope(
        jnp.where(is_last, next_weight * not_high, shift(weight, -1)),
        jnp.where(is_last, next_edge, shift(x, -1)) - x,
    )
    grad += slope(jnp.where(time > 0, weight, 0.0), x - shift(x, 8))
    grad -= slope(jnp.where(time < TIMES - 1, weight, 0.0), shift(x, -8) - x)
    smooth[...] = x - (STEP * TV_SCALE) * grad

    at = pl.ds(row_of(y, 0, core), 64)
    total = part[at, :]
    for k in range(1, NY):
        to_bl(part.at[at], got_y.at[k], rys.at[k], ryr.at[k], y_peer[k]).wait_recv()
        total = total + got_y[k]
    part[at, :] = total
    rz_sends = []
    for k in range(1, NZ):
        copy = to_bl(
            part.at[pl.ds(row_of(y, lax.rem(z + k, NZ), core), 8)], got_z.at[k],
            rzs.at[k], rzr.at[k], z_peer[k],
        )
        copy.start()
        rz_sends.append(copy)
    total = part[pl.ds(own_row, 8), :]
    for k in range(1, NZ):
        to_bl(part.at[pl.ds(own_row, 8)], got_z.at[k], rzs.at[k], rzr.at[k], z_peer[k]).wait_recv()
        total = total + got_z[k]
    updated = smooth[...] + STEP * total
    upd_ref[...] = jnp.transpose(updated).reshape(8, TIMES, CHANNELS, 8)

    for copy in z_sends + y_sends + c_sends + h_sends + rc_sends + ry_sends + rz_sends:
        copy.wait_send()
    store.wait()


def local(meas, model, imp, tally, one, two, gains, tvw):
    big = (8, TIMES, CHANNELS, PAIRS)
    vmem = pltpu.VMEM
    dma = pltpu.SemaphoreType.DMA
    any_spec = pl.BlockSpec(memory_space=pl.ANY)
    return pl.pallas_call(
        kernel,
        out_shape=(
            jax.ShapeDtypeStruct((8, TIMES, CHANNELS, 8), F32),
            jax.ShapeDtypeStruct(big, F32),
        ),
        in_specs=[any_spec] * 8,
        out_specs=(pl.BlockSpec(memory_space=pltpu.VMEM), any_spec),
        scratch_shapes=[
            vmem(big, F32), vmem(big, F32), vmem((TIMES, CHANNELS, PAIRS), F32),
            vmem((1, PAIRS), jnp.int32), vmem((1, PAIRS), jnp.int32), vmem((1, PAIRS), jnp.int32),
            vmem((8, TIMES, CHANNELS, 8), F32), vmem((CHANNELS, 8), F32),
            vmem((STATIONS, LANES), F32), vmem((STATIONS, PAIRS), BF16), vmem((STATIONS, PAIRS), BF16),
            vmem(big, F32), vmem(big, F32), vmem(big, F32), vmem((STATIONS, LANES), F32),
            vmem((NY, 64, LANES), F32), vmem((NY, 64, LANES), F32), vmem((NZ, 8, LANES), F32),
            vmem((8, 128), F32), vmem((2, 8, 128), F32), vmem((8, LANES), F32), vmem((8, LANES), F32),
            dma((8,)), dma((1,)),
            dma((NZ,)), dma((NZ,)), dma((NY,)), dma((NY,)), dma((NY,)), dma((NY,)), dma((2,)), dma((2,)),
            dma((NY,)), dma((NY,)), dma((NY,)), dma((NY,)), dma((NZ,)), dma((NZ,)),
        ],
        compiler_params=pltpu.CompilerParams(
            collective_id=0, has_side_effects=True, vmem_limit_bytes=40 * 1024 * 1024
        ),
    )(meas, model, imp, tally, one.reshape(1, PAIRS), two.reshape(1, PAIRS), gains, tvw)


def solution(mesh):
    placed = (
        P(None, None, "chan", "bl"),
        P(None, None, "chan", "bl"),
        P(None, "chan", "bl"),
        P("chan", "bl"),
        P("bl"),
        P("bl"),
        P(None, None, "chan", "bl"),
        P("chan", "bl"),
    )
    return jax.shard_map(
        local,
        mesh=mesh,
        in_specs=placed,
        out_specs=(P(None, None, "chan", "bl"), P(None, None, "chan", "bl")),
        check_vma=False,
    )
```

```python
import jax
import jax.numpy as jnp
from jax import lax
from jax.experimental import pallas as pl
from jax.experimental.pallas import tpu as pltpu
from jax.sharding import PartitionSpec as P

MESH = pl.DeviceIdType.MESH
STATIONS = 512
BASELINES = 32768
TIMES = 4
CHANNELS = 8
PAIRS = 512
LANES = 8 * TIMES * CHANNELS
NY, NZ, NC = 4, 8, 2
SMOOTH_EPS = 0.01
TV_SCALE = 2.0
STEP = 2.0 * STATIONS / BASELINES
F32 = jnp.float32
BF16 = jnp.bfloat16


def cmul_add(terms):
    real, imag = None, None
    for (ar, ai), (br, bi), conj in terms:
        if conj:
            r, i = ar * br + ai * bi, ai * br - ar * bi
        else:
            r, i = ar * br - ai * bi, ar * bi + ai * br
        real = r if real is None else real + r
        imag = i if imag is None else imag + i
    return real, imag


def halves(x):
    high = x.astype(BF16)
    return high, (x - high.astype(F32)).astype(BF16)


def split_index():
    bl = lax.axis_index("bl")
    return lax.div(bl, NZ * NC), lax.rem(lax.div(bl, NC), NZ), lax.rem(bl, NC)


def join_index(y, z, core):
    return (y * NZ + z) * NC + core


def kernel(
    meas_h, model_h, imp_h, tally_h, one_h, two_h, gains_h, tvw_h,
    upd_ref, res,
    meas, model, imp, tally, one, two, gains, tvw,
    table, hot1, hot2, gp, gq, part, got_c, got_y, got_z, halo, halo_got,
    in_sem, zs, zr, ys, yr, cs, cr, hs, hr, rcs, rcr, rys, ryr, rzs, rzr,
):
    chan = lax.axis_index("chan")
    n_chan = lax.axis_size("chan")
    y, z, core = split_index()
    early = lax.rem(chan, 2) == 0
    chan_peers = [lax.rem(chan + 1, n_chan), lax.rem(chan + n_chan - 1, n_chan)]

    def to_bl(src, dst, send, recv, peer):
        return pltpu.make_async_remote_copy(
            src_ref=src, dst_ref=dst, send_sem=send, recv_sem=recv,
            device_id={"bl": peer}, device_id_type=MESH,
        )

    def z_peer(k):
        to = lax.rem(z + k, NZ)
        return join_index(y, to, core), to

    def y_peer(k):
        to = lax.rem(y + k, NY)
        return join_index(to, z, core), to

    other = join_index(y, z, 1 - core)

    loads = [
        pltpu.make_async_copy(src, dst, in_sem.at[i])
        for i, (src, dst) in enumerate(
            [(gains_h, gains), (one_h, one), (two_h, two), (tvw_h, tvw), (tally_h, tally),
             (imp_h, imp), (meas_h, meas), (model_h, model)]
        )
    ]
    loads[0].start()
    barrier = pltpu.get_barrier_semaphore()
    for peer in [z_peer(k)[0] for k in range(1, NZ)] + [y_peer(k)[0] for k in range(1, NY)] + [other]:
        pl.semaphore_signal(barrier, inc=1, device_id={"bl": peer}, device_id_type=MESH)

    @pl.when(early)
    def _():
        for peer in chan_peers:
            pl.semaphore_signal(barrier, inc=1, device_id={"chan": peer}, device_id_type=MESH)

    for load in loads[1:]:
        load.start()

    loads[0].wait()
    own = jnp.transpose(gains[...].reshape(LANES, 8))
    table[z, core, y] = own
    pl.semaphore_wait(barrier, 11 + 2 * lax.rem(chan, 2))

    for k in range(1, NZ):
        piece = table.at[z, core, y]
        to_bl(piece, piece, zs.at[0], zr.at[z], z_peer(k)[0]).start()

    def pass_on(v):
        piece = table.at[v, core, y]
        for k in (2, 1, 3):
            to_bl(piece, piece, ys.at[0], yr.at[v], y_peer(k)[0]).start()

    pass_on(z)

    loads[3].wait()
    lane = lax.broadcasted_iota(jnp.int32, (8, LANES), 1)
    freq, time = lane & 7, lax.shift_right_logical(lane, 3) & 3
    weight = jnp.transpose(
        jnp.broadcast_to(tvw[...][None], (8 * TIMES, CHANNELS, 8)).reshape(LANES, 8)
    )
    low, high = own[:, :128], own[:, 128:]
    freq_h = freq[:, :128]
    halo[...] = jnp.where(
        freq_h == 0, low,
        jnp.where(
            freq_h == 1, pltpu.roll(high, 1, 1),
            jnp.where(
                freq_h == 7, low,
                jnp.where(freq_h == 6, pltpu.roll(high, 127, 1), pltpu.roll(weight[:, :128], 2, 1)),
            ),
        ),
    )
    edges = [
        pltpu.make_async_remote_copy(
            src_ref=halo, dst_ref=halo_got.at[k], send_sem=hs.at[k], recv_sem=hr.at[k],
            device_id={"chan": peer}, device_id_type=MESH,
        )
        for k, peer in enumerate(chan_peers)
    ]

    @pl.when(jnp.logical_not(early))
    def _():
        for edge in edges:
            edge.start()

    loads[1].wait()
    loads[2].wait()

    def to_row(ant):
        return (
            (lax.shift_right_logical(ant, 4) & 7) * 64 + (lax.shift_right_logical(ant, 3) & 1) * 32
            + lax.shift_right_logical(ant, 7) * 8 + (ant & 7)
        )

    row1, row2 = to_row(one[...]), to_row(two[...])

    def hot_body(i, carry):
        base = pl.multiple_of(i * 32, 32)
        index = lax.broadcasted_iota(jnp.int32, (32, PAIRS), 0) + base
        hot1[pl.ds(base, 32), :] = jnp.where(index == row1, 1.0, 0.0).astype(BF16)
        hot2[pl.ds(base, 32), :] = jnp.where(index == row2, 1.0, 0.0).astype(BF16)
        return carry

    lax.fori_loop(0, 16, hot_body, 0)

    loads[4].wait()
    loads[5].wait()
    keep = lax.broadcasted_iota(jnp.int32, (CHANNELS, PAIRS), 0) < CHANNELS - tally[...]
    for t in range(TIMES):
        imp[t] = jnp.where(keep, imp[t], 0.0)
    loads[6].wait()
    loads[7].wait()

    def take_in(v, carry):
        @pl.when(v != z)
        def _():
            piece = table.at[v, core, y]
            to_bl(piece, piece, zs.at[0], zr.at[v], z_peer(1)[0]).wait_recv()
            pass_on(v)

        return carry

    def share(v, carry):
        three = table.at[v, core, pl.ds(0, 3)]
        to_bl(three, three, ys.at[0], yr.at[v], other).wait_recv()
        four = table.at[v, core]
        to_bl(four, four, cs.at[0], cr.at[v], other).start()
        return carry

    def pick(half, first):
        def arrived(v, carry):
            four = table.at[v, 1 - core]
            to_bl(four, four, cs.at[0], cr.at[v], other).wait_recv()
            return carry

        lax.fori_loop(half * 4, half * 4 + 4, arrived, 0)
        flipped = jnp.transpose(table[pl.ds(half * 4, 4)].reshape(256, LANES))
        g_high, g_low = halves(flipped)
        rows = pl.ds(half * 256, 256)
        for hot, dst in ((hot1, gp), (hot2, gq)):
            picked = jnp.dot(g_high, hot[rows, :], preferred_element_type=F32) + jnp.dot(
                g_low, hot[rows, :], preferred_element_type=F32
            )
            picked = picked.reshape(8, TIMES, CHANNELS, PAIRS)
            dst[...] = picked if first else dst[...] + picked

    lax.fori_loop(0, 8, take_in, 0)
    lax.fori_loop(0, 8, share, 0)
    pick(0, True)
    pick(1, False)

    def compute(i, carry):
        t = lax.div(i, 4)
        at = pl.ds(pl.multiple_of(lax.rem(i, 4) * 128, 128), 128)

        def matrix(ref):
            return [(ref[c, t, :, at], ref[c + 4, t, :, at]) for c in range(4)]

        jp, jq, m, d = matrix(gp), matrix(gq), matrix(model), matrix(meas)
        w = imp[t, :, at]
        a = [
            cmul_add([(jp[2 * r], m[c], False), (jp[2 * r + 1], m[c + 2], False)])
            for r in range(2) for c in range(2)
        ]
        v = [
            cmul_add([(a[2 * r], jq[2 * c], True), (a[2 * r + 1], jq[2 * c + 1], True)])
            for r in range(2) for c in range(2)
        ]
        e = [(w * (d[k][0] - v[k][0]), w * (d[k][1] - v[k][1])) for k in range(4)]
        for k in range(4):
            res[k, t, :, at] = e[k][0]
            res[k + 4, t, :, at] = e[k][1]
        b = [
            cmul_add([(jq[2 * r], m[2 * c], True), (jq[2 * r + 1], m[2 * c + 1], True)])
            for r in range(2) for c in range(2)
        ]
        first = [
            cmul_add([(e[2 * r], b[c], False), (e[2 * r + 1], b[c + 2], False)])
            for r in range(2) for c in range(2)
        ]
        second = [
            cmul_add([(a[c], e[r], True), (a[c + 2], e[r + 2], True)])
            for r in range(2) for c in range(2)
        ]
        for k in range(4):
            gp[k, t, :, at] = first[k][0]
            gp[k + 4, t, :, at] = first[k][1]
            gq[k, t, :, at] = second[k][0]
            gq[k + 4, t, :, at] = second[k][1]
        return carry

    lax.fori_loop(0, 16, compute, 0)

    p_high, p_low = halves(gp[...].reshape(LANES, PAIRS))
    q_high, q_low = halves(gq[...].reshape(LANES, PAIRS))
    nt = (((1,), (1,)), ((), ()))

    def add_up(v, count):
        rows = pl.ds(v * 64, count * 64)
        h1, h2 = hot1[rows, :], hot2[rows, :]
        total = lax.dot_general(h1, p_high, nt, preferred_element_type=F32)
        total += lax.dot_general(h1, p_low, nt, preferred_element_type=F32)
        total += lax.dot_general(h2, q_high, nt, preferred_element_type=F32)
        total += lax.dot_general(h2, q_low, nt, preferred_element_type=F32)
        part[pl.ds(v, count)] = total.reshape(count, NC, NY, 8, LANES)

    def hand_over(v, carry):
        to_bl(part.at[v, 1 - core], got_c.at[v], rcs.at[0], rcr.at[v], other).start()
        return carry

    def along_y(v, carry):
        got = got_c.at[v]
        to_bl(got, got, rcs.at[0], rcr.at[v], other).wait_recv()
        part[v, core] = part[v, core] + got_c[v]
        for k in (2, 1, 3):
            peer, to = y_peer(k)
            to_bl(part.at[v, core, to], got_y.at[v, k - 1], rys.at[0], ryr.at[v], peer).start()
        return carry

    def along_z(v, carry):
        got = got_y.at[v]
        to_bl(got, got, rys.at[0], ryr.at[v], other).wait_recv()
        part[v, core, y] = part[v, core, y] + got_y[v, 0] + (got_y[v, 1] + got_y[v, 2])

        @pl.when(v != z)
        def _():
            to_bl(
                part.at[v, core, y], got_z.at[z], rzs.at[0], rzr.at[0], join_index(y, v, core)
            ).start()

        return carry

    add_up(0, 1)
    hand_over(0, 0)
    add_up(1, 7)
    lax.fori_loop(1, 8, hand_over, 0)
    lax.fori_loop(0, 8, along_y, 0)
    lax.fori_loop(0, 8, along_z, 0)
    got_z[z] = part[z, core, y]

    for edge in edges:
        edge.wait_recv()

    @pl.when(early)
    def _():
        for edge in edges:
            edge.start()

    from_prev, from_next = halo_got[0], halo_got[1]
    x = own

    def shift(v, by):
        return pltpu.roll(v, by % LANES, 1)

    prev_edge = jnp.concatenate([pltpu.roll(from_prev, 121, 1), pltpu.roll(from_prev, 122, 1)], axis=1)
    next_edge = jnp.concatenate([pltpu.roll(from_next, 7, 1), pltpu.roll(from_next, 6, 1)], axis=1)
    next_weight = jnp.concatenate([pltpu.roll(from_next, 5, 1)] * 2, axis=1)
    is_first, is_last = freq == 0, freq == CHANNELS - 1
    not_low = jnp.where(chan > 0, 1.0, 0.0).astype(F32)
    not_high = jnp.where(chan < n_chan - 1, 1.0, 0.0).astype(F32)

    def slope(w, step):
        square = step * step
        for by in (128, 64, 32):
            square = square + shift(square, by)
        return w * step / jnp.sqrt(square + SMOOTH_EPS)

    grad = slope(
        jnp.where(is_first, weight * not_low, weight), x - jnp.where(is_first, prev_edge, shift(x, 1))
    )
    grad -= slope(
        jnp.where(is_last, next_weight * not_high, shift(weight, -1)),
        jnp.where(is_last, next_edge, shift(x, -1)) - x,
    )
    grad += slope(jnp.where(time > 0, weight, 0.0), x - shift(x, 8))
    grad -= slope(jnp.where(time < TIMES - 1, weight, 0.0), shift(x, -8) - x)
    updated = x - (STEP * TV_SCALE) * grad

    rows = got_z.at[pl.ds(0, NZ - 1)]
    to_bl(rows, rows, rzs.at[0], rzr.at[0], z_peer(1)[0]).wait_recv()
    total = got_z[0]
    for v in range(1, NZ):
        total = total + got_z[v]
    updated = updated + STEP * total
    upd_ref[...] = jnp.transpose(updated).reshape(8, TIMES, CHANNELS, 8)

    for edge in edges:
        edge.wait_send()
    to_bl(rows, rows, zs.at[0], rzr.at[0], other).wait_send()
    to_bl(rows, rows, rzs.at[0], rzr.at[0], other).wait_send()
    half = part.at[pl.ds(0, NZ), 0]
    to_bl(half, half, cs.at[0], rzr.at[0], other).wait_send()
    to_bl(half, half, rcs.at[0], rzr.at[0], other).wait_send()
    to_bl(got_y, got_y, ys.at[0], rzr.at[0], other).wait_send()
    to_bl(got_y, got_y, rys.at[0], rzr.at[0], other).wait_send()


def local(meas, model, imp, tally, one, two, gains, tvw):
    big = (8, TIMES, CHANNELS, PAIRS)
    vmem = pltpu.VMEM
    dma = pltpu.SemaphoreType.DMA
    any_spec = pl.BlockSpec(memory_space=pl.ANY)
    vmem_spec = pl.BlockSpec(memory_space=pltpu.VMEM)
    return pl.pallas_call(
        kernel,
        out_shape=(vmem((8, TIMES, CHANNELS, 8), F32), vmem(big, F32)),
        in_specs=[any_spec] * 8,
        out_specs=(vmem_spec, vmem_spec),
        scratch_shapes=[
            vmem(big, F32), vmem(big, F32), vmem((TIMES, CHANNELS, PAIRS), F32),
            vmem((1, PAIRS), jnp.int32), vmem((1, PAIRS), jnp.int32), vmem((1, PAIRS), jnp.int32),
            vmem((8, TIMES, CHANNELS, 8), F32), vmem((CHANNELS, 8), F32),
            vmem((NZ, NC, NY, 8, LANES), F32), vmem((STATIONS, PAIRS), BF16), vmem((STATIONS, PAIRS), BF16),
            vmem(big, F32), vmem(big, F32), vmem((NZ, NC, NY, 8, LANES), F32),
            vmem((NZ, NY, 8, LANES), F32), vmem((NZ, NY - 1, 8, LANES), F32), vmem((NZ, 8, LANES), F32),
            vmem((8, 128), F32), vmem((2, 8, 128), F32),
            dma((8,)), dma((1,)), dma((NZ,)), dma((1,)), dma((NZ,)), dma((1,)), dma((NZ,)), dma((2,)), dma((2,)),
            dma((1,)), dma((NZ,)), dma((1,)), dma((NZ,)), dma((1,)), dma((1,)),
        ],
        compiler_params=pltpu.CompilerParams(
            collective_id=0, has_side_effects=True, vmem_limit_bytes=58 * 1024 * 1024
        ),
    )(meas, model, imp, tally, one.reshape(1, PAIRS), two.reshape(1, PAIRS), gains, tvw)


def solution(mesh):
    placed = (
        P(None, None, "chan", "bl"),
        P(None, None, "chan", "bl"),
        P(None, "chan", "bl"),
        P("chan", "bl"),
        P("bl"),
        P("bl"),
        P(None, None, "chan", "bl"),
        P("chan", "bl"),
    )
    return jax.shard_map(
        local,
        mesh=mesh,
        in_specs=placed,
        out_specs=(P(None, None, "chan", "bl"), P(None, None, "chan", "bl")),
        check_vma=False,
    )
```

```python
import functools

import jax
import jax.numpy as jnp
from jax import lax
from jax.experimental import pallas as pl
from jax.experimental.pallas import tpu as pltpu
from jax.sharding import PartitionSpec as P

MESH = pl.DeviceIdType.MESH
STATIONS = 512
BASELINES = 32768
TIMES = 4
CHANNELS = 8
PAIRS = 512
LANES = 8 * TIMES * CHANNELS
NY, NZ, NC = 4, 8, 2
HALF = NZ // 2
DIRECT = 2
SMOOTH_EPS = 0.01
TV_SCALE = 2.0
STEP = 2.0 * STATIONS / BASELINES
F32 = jnp.float32
BF16 = jnp.bfloat16


def cmul_add(terms):
    real, imag = None, None
    for (ar, ai), (br, bi), conj in terms:
        if conj:
            r, i = ar * br + ai * bi, ai * br - ar * bi
        else:
            r, i = ar * br - ai * bi, ar * bi + ai * br
        real = r if real is None else real + r
        imag = i if imag is None else imag + i
    return real, imag


def halves(x):
    high = x.astype(BF16)
    return high, (x - high.astype(F32)).astype(BF16)


def split_index():
    bl = lax.axis_index("bl")
    return lax.div(bl, NZ * NC), lax.rem(lax.div(bl, NC), NZ), lax.rem(bl, NC)


def join_index(y, z, core):
    return (y * NZ + z) * NC + core


def kernel(
    meas_h, model_h, imp_h, tally_h, one_h, two_h, gains_h, tvw_h,
    upd_ref, res,
    meas, model, imp, tally, one, two, gains, tvw,
    table, hot1, hot2, gp, gq, part, got_0, got_c, got_y, got_z, halo, halo_got,
    in_sem, zs, zr, ys, yr, cs, cr, hs, hr, r0s, r0r, rcs, rcr, rys, ryr, rzs, rzr,
    ready_z, ready_y, ready_c,
):
    chan = lax.axis_index("chan")
    n_chan = lax.axis_size("chan")
    odd = lax.rem(chan, 2)
    y, z, core = split_index()
    early = odd == 0
    chan_peers = [lax.rem(chan + 1, n_chan), lax.rem(chan + n_chan - 1, n_chan)]

    def to_bl(src, dst, send, recv, peer):
        return pltpu.make_async_remote_copy(
            src_ref=src, dst_ref=dst, send_sem=send, recv_sem=recv,
            device_id={"bl": peer}, device_id_type=MESH,
        )

    def z_peer(to):
        return join_index(y, to, core)

    def y_peer(k):
        to = lax.rem(y + k, NY)
        return join_index(to, z, core), to

    other = join_index(y, z, 1 - core)

    loads = [
        pltpu.make_async_copy(src, dst, in_sem.at[i])
        for i, (src, dst) in enumerate(
            [(gains_h, gains), (one_h, one), (two_h, two), (tvw_h, tvw), (tally_h, tally),
             (imp_h, imp), (meas_h, meas), (model_h, model)]
        )
    ]
    loads[0].start()
    barrier = pltpu.get_barrier_semaphore()

    def rank_of(to):
        return lax.rem(to, 2) * 2 + lax.div(to, 2)

    rank = rank_of(y)
    upper = lax.div(z, HALF)

    def announce(to, carry):
        pl.semaphore_signal(barrier, inc=1, device_id={"bl": z_peer(to)}, device_id_type=MESH)
        return carry

    lax.fori_loop(z + 1, NZ, announce, 0)
    for k in range(1, NY):
        peer, to = y_peer(k)

        @pl.when(rank_of(to) > rank)
        def _():
            pl.semaphore_signal(barrier, inc=1, device_id={"bl": peer}, device_id_type=MESH)

    @pl.when(core == 0)
    def _():
        pl.semaphore_signal(barrier, inc=1, device_id={"bl": other}, device_id_type=MESH)

    @pl.when(early)
    def _():
        for peer in chan_peers:
            pl.semaphore_signal(barrier, inc=1, device_id={"chan": peer}, device_id_type=MESH)

    earlier = z + rank + core + 2 * odd

    @pl.when(earlier > 0)
    def _():
        pl.semaphore_wait(barrier, earlier)

    def tell_z(to, carry):
        pl.semaphore_signal(ready_z.at[z], inc=1, device_id={"bl": z_peer(to)}, device_id_type=MESH)
        return carry

    lax.fori_loop(upper * (HALF - 1), z, tell_z, 0)
    for k in range(1, NY):
        peer, to = y_peer(k)

        @pl.when(rank_of(to) < rank)
        def _():
            pl.semaphore_signal(ready_y, inc=1, device_id={"bl": peer}, device_id_type=MESH)

    @pl.when(core == 1)
    def _():
        pl.semaphore_signal(ready_c, inc=1, device_id={"bl": other}, device_id_type=MESH)

    loads[0].wait()
    own = jnp.transpose(gains[...].reshape(LANES, 8))
    table[z, core, y] = own

    mine = table.at[z, core, y]

    def send_down(to, carry):
        to_bl(mine, mine, zs.at[0], zr.at[z], z_peer(to)).start()
        return carry

    lax.fori_loop(0, z, send_down, 0)
    for load in loads[1:]:
        load.start()

    loads[3].wait()
    lane = lax.broadcasted_iota(jnp.int32, (8, LANES), 1)
    freq, time = lane & 7, lax.shift_right_logical(lane, 3) & 3
    weight = jnp.transpose(
        jnp.broadcast_to(tvw[...][None], (8 * TIMES, CHANNELS, 8)).reshape(LANES, 8)
    )
    low, high = own[:, :128], own[:, 128:]
    freq_h = freq[:, :128]
    halo[...] = jnp.where(
        freq_h == 0, low,
        jnp.where(
            freq_h == 1, pltpu.roll(high, 1, 1),
            jnp.where(
                freq_h == 7, low,
                jnp.where(freq_h == 6, pltpu.roll(high, 127, 1), pltpu.roll(weight[:, :128], 2, 1)),
            ),
        ),
    )
    edges = [
        pltpu.make_async_remote_copy(
            src_ref=halo, dst_ref=halo_got.at[k], send_sem=hs.at[k], recv_sem=hr.at[k],
            device_id={"chan": peer}, device_id_type=MESH,
        )
        for k, peer in enumerate(chan_peers)
    ]

    @pl.when(jnp.logical_not(early))
    def _():
        for edge in edges:
            edge.start()

    loads[1].wait()
    loads[2].wait()

    def to_row(ant):
        return (
            (lax.shift_right_logical(ant, 4) & 7) * 64 + (lax.shift_right_logical(ant, 3) & 1) * 32
            + lax.shift_right_logical(ant, 7) * 8 + (ant & 7)
        )

    row1, row2 = to_row(one[...]), to_row(two[...])

    def hot_body(i, carry):
        base = pl.multiple_of(i * 32, 32)
        index = lax.broadcasted_iota(jnp.int32, (32, PAIRS), 0) + base
        hot1[pl.ds(base, 32), :] = jnp.where(index == row1, 1.0, 0.0).astype(BF16)
        hot2[pl.ds(base, 32), :] = jnp.where(index == row2, 1.0, 0.0).astype(BF16)
        return carry

    lax.fori_loop(0, 16, hot_body, 0)

    loads[4].wait()
    loads[5].wait()
    keep = lax.broadcasted_iota(jnp.int32, (CHANNELS, PAIRS), 0) < CHANNELS - tally[...]
    for t in range(TIMES):
        imp[t] = jnp.where(keep, imp[t], 0.0)
    loads[6].wait()
    loads[7].wait()

    def pieces(v, count):
        return table.at[v, core, y] if count == 1 else table.at[pl.ds(v, count), core, y]

    def send_up(to, v, count):
        pl.semaphore_wait(ready_z.at[to], 1)
        rows = pieces(v, count)
        to_bl(rows, rows, zs.at[1], zr.at[v], z_peer(to)).start()

    def wait_for(v, count=1):
        rows = pieces(v, count)
        to_bl(rows, rows, zs.at[1], zr.at[v], other).wait_recv()

    def pass_on(v, count=1):
        rows = pieces(v, count)
        for k in (2, 1, 3):
            to_bl(rows, rows, ys.at[0], yr.at[v // HALF], y_peer(k)[0]).start()

    def take_in(v, count=1):
        wait_for(v, count)
        pass_on(v, count)

    def share(half):
        three = table.at[pl.ds(half * HALF, HALF), core, pl.ds(0, 3)]
        to_bl(three, three, ys.at[0], yr.at[half], other).wait_recv()
        four = table.at[pl.ds(half * HALF, HALF), core]
        to_bl(four, four, cs.at[0], cr.at[half], other).start()

    def pick(half, first):
        four = table.at[pl.ds(half * HALF, HALF), 1 - core]
        to_bl(four, four, cs.at[0], cr.at[half], other).wait_recv()
        flipped = jnp.transpose(table[pl.ds(half * HALF, HALF)].reshape(256, LANES))
        g_high, g_low = halves(flipped)
        rows = pl.ds(pl.multiple_of(half * 256, 256), 256)
        for hot, dst in ((hot1, gp), (hot2, gq)):
            picked = jnp.dot(g_high, hot[rows, :], preferred_element_type=F32) + jnp.dot(
                g_low, hot[rows, :], preferred_element_type=F32
            )
            picked = picked.reshape(8, TIMES, CHANNELS, PAIRS)
            dst[...] = picked if first else dst[...] + picked

    def line(at):
        for to in range(at + 1, at // HALF * HALF + HALF):
            send_up(to, at, 1)

        @pl.when(rank < NY - 1)
        def _():
            pl.semaphore_wait(ready_y, NY - 1 - rank)

        pass_on(at)
        if at < HALF:
            for v in range(HALF):
                if v != at:
                    take_in(v)
            if at == HALF - 1:
                for to in (4, 7, 6, 5):
                    send_up(to, 0, HALF)
            for v in range(HALF, NZ):
                take_in(v)
        else:
            for v in range(HALF, NZ):
                if v != at:
                    take_in(v)
            take_in(0, HALF)

    for at in range(NZ):
        pl.when(z == at)(functools.partial(line, at))

    @pl.when(core == 0)
    def _():
        pl.semaphore_wait(ready_c, 1)

    share(upper)
    share(1 - upper)
    pick(upper, True)
    pick(1 - upper, False)

    def compute(i, carry):
        t = lax.div(i, 4)
        at = pl.ds(pl.multiple_of(lax.rem(i, 4) * 128, 128), 128)

        def matrix(ref):
            return [(ref[c, t, :, at], ref[c + 4, t, :, at]) for c in range(4)]

        jp, jq, m, d = matrix(gp), matrix(gq), matrix(model), matrix(meas)
        w = imp[t, :, at]
        a = [
            cmul_add([(jp[2 * r], m[c], False), (jp[2 * r + 1], m[c + 2], False)])
            for r in range(2) for c in range(2)
        ]
        v = [
            cmul_add([(a[2 * r], jq[2 * c], True), (a[2 * r + 1], jq[2 * c + 1], True)])
            for r in range(2) for c in range(2)
        ]
        e = [(w * (d[k][0] - v[k][0]), w * (d[k][1] - v[k][1])) for k in range(4)]
        for k in range(4):
            res[k, t, :, at] = e[k][0]
            res[k + 4, t, :, at] = e[k][1]
        b = [
            cmul_add([(jq[2 * r], m[2 * c], True), (jq[2 * r + 1], m[2 * c + 1], True)])
            for r in range(2) for c in range(2)
        ]
        first = [
            cmul_add([(e[2 * r], b[c], False), (e[2 * r + 1], b[c + 2], False)])
            for r in range(2) for c in range(2)
        ]
        second = [
            cmul_add([(a[c], e[r], True), (a[c + 2], e[r + 2], True)])
            for r in range(2) for c in range(2)
        ]
        for k in range(4):
            gp[k, t, :, at] = first[k][0]
            gp[k + 4, t, :, at] = first[k][1]
            gq[k, t, :, at] = second[k][0]
            gq[k + 4, t, :, at] = second[k][1]
        return carry

    lax.fori_loop(0, 16, compute, 0)

    p_high, p_low = halves(gp[...].reshape(LANES, PAIRS))
    q_high, q_low = halves(gq[...].reshape(LANES, PAIRS))
    nt = (((1,), (1,)), ((), ()))

    def add_up(v, count):
        rows = pl.ds(v * 64, count * 64)
        h1, h2 = hot1[rows, :], hot2[rows, :]
        total = lax.dot_general(h1, p_high, nt, preferred_element_type=F32)
        total += lax.dot_general(h1, p_low, nt, preferred_element_type=F32)
        total += lax.dot_general(h2, q_high, nt, preferred_element_type=F32)
        total += lax.dot_general(h2, q_low, nt, preferred_element_type=F32)
        part[pl.ds(v, count)] = total.reshape(count, NC, NY, 8, LANES)

    def hand_over(v, carry):
        to_bl(part.at[v, 1 - core], got_c.at[v], rcs.at[0], rcr.at[v], other).start()
        return carry

    def along_y(v, carry):
        got = got_c.at[v]
        to_bl(got, got, rcs.at[0], rcr.at[v], other).wait_recv()
        part[v, core] = part[v, core] + got_c[v]
        for k in (2, 1, 3):
            peer, to = y_peer(k)
            to_bl(part.at[v, core, to], got_y.at[v, k - 1], rys.at[0], ryr.at[v], peer).start()
        return carry

    def send_on(v):
        @pl.when(v != z)
        def _():
            to_bl(part.at[v, core, y], got_z.at[z], rzs.at[0], rzr.at[0], z_peer(v)).start()

    def along_z(v, carry):
        got = got_y.at[v]
        to_bl(got, got, rys.at[0], ryr.at[v], other).wait_recv()
        part[v, core, y] = part[v, core, y] + got_y[v, 0] + (got_y[v, 1] + got_y[v, 2])
        send_on(v)
        return carry

    add_up(0, DIRECT)
    for v in range(DIRECT):
        for slot, (dy, dc) in enumerate(((2, 0), (2, 1), (1, 0), (1, 1), (3, 0), (3, 1), (0, 1))):
            to_y, to_core = lax.rem(y + dy, NY), lax.rem(core + dc, NC)
            to_bl(
                part.at[v, to_core, to_y], got_0.at[v, slot], r0s.at[0], r0r.at[v],
                join_index(to_y, z, to_core),
            ).start()
    add_up(DIRECT, NZ - DIRECT)
    lax.fori_loop(DIRECT, NZ, hand_over, 0)
    lax.fori_loop(DIRECT, NZ, along_y, 0)
    for v in range(DIRECT):
        got = got_0.at[v]
        to_bl(got, got, r0s.at[0], r0r.at[v], other).wait_recv()
        total = part[v, core, y]
        for slot in range(7):
            total = total + got_0[v, slot]
        part[v, core, y] = total
        send_on(v)
    lax.fori_loop(DIRECT, NZ, along_z, 0)
    got_z[z] = part[z, core, y]

    for edge in edges:
        edge.wait_recv()

    @pl.when(early)
    def _():
        for edge in edges:
            edge.start()

    from_prev, from_next = halo_got[0], halo_got[1]
    x = own

    def shift(v, by):
        return pltpu.roll(v, by % LANES, 1)

    prev_edge = jnp.concatenate([pltpu.roll(from_prev, 121, 1), pltpu.roll(from_prev, 122, 1)], axis=1)
    next_edge = jnp.concatenate([pltpu.roll(from_next, 7, 1), pltpu.roll(from_next, 6, 1)], axis=1)
    next_weight = jnp.concatenate([pltpu.roll(from_next, 5, 1)] * 2, axis=1)
    is_first, is_last = freq == 0, freq == CHANNELS - 1
    not_low = jnp.where(chan > 0, 1.0, 0.0).astype(F32)
    not_high = jnp.where(chan < n_chan - 1, 1.0, 0.0).astype(F32)

    def slope(w, step):
        square = step * step
        for by in (128, 64, 32):
            square = square + shift(square, by)
        return w * step / jnp.sqrt(square + SMOOTH_EPS)

    grad = slope(
        jnp.where(is_first, weight * not_low, weight), x - jnp.where(is_first, prev_edge, shift(x, 1))
    )
    grad -= slope(
        jnp.where(is_last, next_weight * not_high, shift(weight, -1)),
        jnp.where(is_last, next_edge, shift(x, -1)) - x,
    )
    grad += slope(jnp.where(time > 0, weight, 0.0), x - shift(x, 8))
    grad -= slope(jnp.where(time < TIMES - 1, weight, 0.0), shift(x, -8) - x)
    updated = x - (STEP * TV_SCALE) * grad

    rows = got_z.at[pl.ds(0, NZ - 1)]
    to_bl(rows, rows, rzs.at[0], rzr.at[0], other).wait_recv()
    total = got_z[0]
    for v in range(1, NZ):
        total = total + got_z[v]
    updated = updated + STEP * total
    upd_ref[...] = jnp.transpose(updated).reshape(8, TIMES, CHANNELS, 8)

    for edge in edges:
        edge.wait_send()

    def left(at):
        for sem, count in ((0, at), (1, (3, 2, 1, 16, 3, 2, 1, 0)[at])):
            if count:
                sent = part.at[pl.ds(0, count), 0, 0] if count <= NZ else part.at[pl.ds(0, count // NY), 0]
                to_bl(sent, sent, zs.at[sem], rzr.at[0], other).wait_send()

    for at in range(NZ):
        pl.when(z == at)(functools.partial(left, at))

    to_bl(rows, rows, rzs.at[0], rzr.at[0], other).wait_send()
    half = part.at[pl.ds(0, NZ), 0]
    to_bl(half, half, cs.at[0], rzr.at[0], other).wait_send()
    seven = part.at[pl.ds(0, NZ - DIRECT), 0]
    to_bl(seven, seven, rcs.at[0], rzr.at[0], other).wait_send()
    to_bl(got_0, got_0, r0s.at[0], rzr.at[0], other).wait_send()
    to_bl(got_y, got_y, ys.at[0], rzr.at[0], other).wait_send()
    most = got_y.at[pl.ds(0, NZ - DIRECT)]
    to_bl(most, most, rys.at[0], rzr.at[0], other).wait_send()


def local(meas, model, imp, tally, one, two, gains, tvw):
    big = (8, TIMES, CHANNELS, PAIRS)
    vmem = pltpu.VMEM
    dma = pltpu.SemaphoreType.DMA
    flag = pltpu.SemaphoreType.REGULAR
    any_spec = pl.BlockSpec(memory_space=pl.ANY)
    vmem_spec = pl.BlockSpec(memory_space=pltpu.VMEM)
    return pl.pallas_call(
        kernel,
        out_shape=(vmem((8, TIMES, CHANNELS, 8), F32), vmem(big, F32)),
        in_specs=[any_spec] * 8,
        out_specs=(vmem_spec, vmem_spec),
        scratch_shapes=[
            vmem(big, F32), vmem(big, F32), vmem((TIMES, CHANNELS, PAIRS), F32),
            vmem((1, PAIRS), jnp.int32), vmem((1, PAIRS), jnp.int32), vmem((1, PAIRS), jnp.int32),
            vmem((8, TIMES, CHANNELS, 8), F32), vmem((CHANNELS, 8), F32),
            vmem((NZ, NC, NY, 8, LANES), F32), vmem((STATIONS, PAIRS), BF16), vmem((STATIONS, PAIRS), BF16),
            vmem(big, F32), vmem(big, F32), vmem((NZ, NC, NY, 8, LANES), F32),
            vmem((DIRECT, 7, 8, LANES), F32), vmem((NZ, NY, 8, LANES), F32), vmem((NZ, NY - 1, 8, LANES), F32), vmem((NZ, 8, LANES), F32),
            vmem((8, 128), F32), vmem((2, 8, 128), F32),
            dma((8,)), dma((2,)), dma((NZ,)), dma((1,)), dma((2,)), dma((1,)), dma((2,)), dma((2,)), dma((2,)),
            dma((1,)), dma((DIRECT,)), dma((1,)), dma((NZ,)), dma((1,)), dma((NZ,)), dma((1,)), dma((1,)),
            flag((NZ,)), flag, flag,
        ],
        compiler_params=pltpu.CompilerParams(
            collective_id=0, has_side_effects=True, vmem_limit_bytes=58 * 1024 * 1024
        ),
    )(meas, model, imp, tally, one.reshape(1, PAIRS), two.reshape(1, PAIRS), gains, tvw)


def solution(mesh):
    placed = (
        P(None, None, "chan", "bl"),
        P(None, None, "chan", "bl"),
        P(None, "chan", "bl"),
        P("chan", "bl"),
        P("bl"),
        P("bl"),
        P(None, None, "chan", "bl"),
        P("chan", "bl"),
    )
    return jax.shard_map(
        local,
        mesh=mesh,
        in_specs=placed,
        out_specs=(P(None, None, "chan", "bl"), P(None, None, "chan", "bl")),
        check_vma=False,
    )
```

```python
import functools

import jax
import jax.numpy as jnp
from jax import lax
from jax.experimental import pallas as pl
from jax.experimental.pallas import tpu as pltpu
from jax.sharding import PartitionSpec as P

MESH = pl.DeviceIdType.MESH
STATIONS = 512
BASELINES = 32768
TIMES = 4
CHANNELS = 8
PAIRS = 512
LANES = 8 * TIMES * CHANNELS
NY, NZ, NC = 4, 8, 2
HALF = NZ // 2
DIRECT = 2
SMOOTH_EPS = 0.01
TV_SCALE = 2.0
STEP = 2.0 * STATIONS / BASELINES
F32 = jnp.float32
BF16 = jnp.bfloat16


def cmul_add(terms):
    real, imag = None, None
    for (ar, ai), (br, bi), conj in terms:
        if conj:
            r, i = ar * br + ai * bi, ai * br - ar * bi
        else:
            r, i = ar * br - ai * bi, ar * bi + ai * br
        real = r if real is None else real + r
        imag = i if imag is None else imag + i
    return real, imag


def halves(x):
    high = x.astype(BF16)
    return high, (x - high.astype(F32)).astype(BF16)


def split_index():
    bl = lax.axis_index("bl")
    return lax.div(bl, NZ * NC), lax.rem(lax.div(bl, NC), NZ), lax.rem(bl, NC)


def join_index(y, z, core):
    return (y * NZ + z) * NC + core


def kernel(
    meas_h, model_h, imp_h, tally_h, one_h, two_h, gains_h, tvw_h,
    upd_ref, res,
    meas, model, imp, tally, one, two, gains, tvw,
    table, hot1, hot2, gp, gq, part, got_0, got_c, got_y, got_z, halo, halo_got,
    in_sem, zs, zr, ys, yr, cs, cr, hs, hr, r0s, r0r, rcs, rcr, rys, ryr, rzs, rzr,
    ready_z, ready_y, ready_c, hub,
):
    chan = lax.axis_index("chan")
    n_chan = lax.axis_size("chan")
    odd = lax.rem(chan, 2)
    y, z, core = split_index()
    early = odd == 0
    chan_peers = [lax.rem(chan + 1, n_chan), lax.rem(chan + n_chan - 1, n_chan)]

    def to_bl(src, dst, send, recv, peer):
        return pltpu.make_async_remote_copy(
            src_ref=src, dst_ref=dst, send_sem=send, recv_sem=recv,
            device_id={"bl": peer}, device_id_type=MESH,
        )

    def z_peer(to):
        return join_index(y, to, core)

    def y_peer(k):
        to = lax.rem(y + k, NY)
        return join_index(to, z, core), to

    other = join_index(y, z, 1 - core)

    loads = [
        pltpu.make_async_copy(src, dst, in_sem.at[i])
        for i, (src, dst) in enumerate(
            [(gains_h, gains), (one_h, one), (two_h, two), (tvw_h, tvw), (tally_h, tally),
             (imp_h, imp), (meas_h, meas), (model_h, model)]
        )
    ]
    loads[0].start()
    barrier = pltpu.get_barrier_semaphore()

    second = lax.rem(y + core, 2)
    upper = lax.div(z, HALF)
    beside = [y_peer(1)[0], y_peer(3)[0], other]

    def tell_beside(sem):
        for peer in beside:
            pl.semaphore_signal(sem, inc=1, device_id={"bl": peer}, device_id_type=MESH)

    def announce(to, carry):
        pl.semaphore_signal(barrier, inc=1, device_id={"bl": z_peer(to)}, device_id_type=MESH)
        return carry

    lax.fori_loop(jnp.where(z == 0, NZ, z + 1), NZ, announce, 0)

    @pl.when((z > 0) & (upper == 0))
    def _():
        announce(0, 0)

    pl.when((upper == 0) & (second == 0))(lambda: tell_beside(barrier))

    @pl.when((upper == 1) & (core == 0))
    def _():
        pl.semaphore_signal(barrier, inc=1, device_id={"bl": other}, device_id_type=MESH)

    @pl.when(early)
    def _():
        for peer in chan_peers:
            pl.semaphore_signal(barrier, inc=1, device_id={"chan": peer}, device_id_type=MESH)

    earlier = jnp.where(z == 0, HALF - 1, z - 1) + (1 - upper) * 3 * second + upper * core + 2 * odd

    @pl.when(earlier > 0)
    def _():
        pl.semaphore_wait(barrier, earlier)

    def tell_z(to, carry):
        pl.semaphore_signal(ready_z.at[z], inc=1, device_id={"bl": z_peer(to)}, device_id_type=MESH)
        return carry

    lax.fori_loop(1 + upper * (HALF - 2), z, tell_z, 0)
    pl.when((upper == 0) & (second == 1))(lambda: tell_beside(ready_y))

    @pl.when((upper == 1) & (core == 1))
    def _():
        pl.semaphore_signal(ready_c, inc=1, device_id={"bl": other}, device_id_type=MESH)

    loads[0].wait()
    own = jnp.transpose(gains[...].reshape(LANES, 8))
    table[z, core, y] = own

    mine = table.at[z, core, y]

    def send_down(to, carry):
        to_bl(mine, mine, zs.at[0], zr.at[z], z_peer(to)).start()
        return carry

    lax.fori_loop(1, jnp.where(z == 0, HALF, z), send_down, 0)
    for load in loads[1:]:
        load.start()

    @pl.when((upper == 0) & (second == 0))
    def _():
        pl.semaphore_wait(ready_y, 3)
        tell_beside(ready_y)


    loads[3].wait()
    lane = lax.broadcasted_iota(jnp.int32, (8, LANES), 1)
    freq, time = lane & 7, lax.shift_right_logical(lane, 3) & 3
    weight = jnp.transpose(
        jnp.broadcast_to(tvw[...][None], (8 * TIMES, CHANNELS, 8)).reshape(LANES, 8)
    )
    low, high = own[:, :128], own[:, 128:]
    freq_h = freq[:, :128]
    halo[...] = jnp.where(
        freq_h == 0, low,
        jnp.where(
            freq_h == 1, pltpu.roll(high, 1, 1),
            jnp.where(
                freq_h == 7, low,
                jnp.where(freq_h == 6, pltpu.roll(high, 127, 1), pltpu.roll(weight[:, :128], 2, 1)),
            ),
        ),
    )
    edges = [
        pltpu.make_async_remote_copy(
            src_ref=halo, dst_ref=halo_got.at[k], send_sem=hs.at[k], recv_sem=hr.at[k],
            device_id={"chan": peer}, device_id_type=MESH,
        )
        for k, peer in enumerate(chan_peers)
    ]

    @pl.when(jnp.logical_not(early))
    def _():
        for edge in edges:
            edge.start()

    loads[1].wait()
    loads[2].wait()

    def to_row(ant):
        return (
            (lax.shift_right_logical(ant, 4) & 7) * 64 + (lax.shift_right_logical(ant, 3) & 1) * 32
            + lax.shift_right_logical(ant, 7) * 8 + (ant & 7)
        )

    row1, row2 = to_row(one[...]), to_row(two[...])

    def hot_body(i, carry):
        base = pl.multiple_of(i * 32, 32)
        index = lax.broadcasted_iota(jnp.int32, (32, PAIRS), 0) + base
        hot1[pl.ds(base, 32), :] = jnp.where(index == row1, 1.0, 0.0).astype(BF16)
        hot2[pl.ds(base, 32), :] = jnp.where(index == row2, 1.0, 0.0).astype(BF16)
        return carry

    lax.fori_loop(0, 16, hot_body, 0)

    loads[4].wait()
    loads[5].wait()
    keep = lax.broadcasted_iota(jnp.int32, (CHANNELS, PAIRS), 0) < CHANNELS - tally[...]
    for t in range(TIMES):
        imp[t] = jnp.where(keep, imp[t], 0.0)
    loads[6].wait()
    loads[7].wait()

    def pieces(v, count):
        return table.at[v, core, y] if count == 1 else table.at[pl.ds(v, count), core, y]

    def send_up(to, v, count):
        pl.semaphore_wait(ready_z.at[to], 1)
        rows = pieces(v, count)
        to_bl(rows, rows, zs.at[1], zr.at[v], z_peer(to)).start()

    def wait_for(v, count=1):
        rows = pieces(v, count)
        to_bl(rows, rows, zs.at[1], zr.at[v], other).wait_recv()

    def pass_on(v, count=1):
        rows = pieces(v, count)
        for k in (2, 1, 3):
            to_bl(rows, rows, ys.at[0], yr.at[v // HALF], y_peer(k)[0]).start()

    def take_in(v, count=1):
        wait_for(v, count)
        pass_on(v, count)

    def share(half):
        three = table.at[pl.ds(half * HALF, HALF), core, pl.ds(0, 3)]
        to_bl(three, three, ys.at[0], yr.at[half], other).wait_recv()
        four = table.at[pl.ds(half * HALF, HALF), core]
        to_bl(four, four, cs.at[0], cr.at[half], other).start()

    def pick(half, first):
        four = table.at[pl.ds(half * HALF, HALF), 1 - core]
        to_bl(four, four, cs.at[0], cr.at[half], other).wait_recv()
        flipped = jnp.transpose(table[pl.ds(half * HALF, HALF)].reshape(256, LANES))
        g_high, g_low = halves(flipped)
        rows = pl.ds(pl.multiple_of(half * 256, 256), 256)
        for hot, dst in ((hot1, gp), (hot2, gq)):
            picked = jnp.dot(g_high, hot[rows, :], preferred_element_type=F32) + jnp.dot(
                g_low, hot[rows, :], preferred_element_type=F32
            )
            picked = picked.reshape(8, TIMES, CHANNELS, PAIRS)
            dst[...] = picked if first else dst[...] + picked

    def line(at):
        for to in range(at + 1, at // HALF * HALF + HALF) if at else ():
            send_up(to, at, 1)
        if at < HALF:

            @pl.when(second == 1)
            def _():
                pl.semaphore_wait(ready_y, 3)

        else:
            pl.semaphore_wait(ready_y, 1)
        if at == HALF - 1:
            pl.semaphore_wait(ready_z.at[HALF], 1)
        if at in (HALF - 1, HALF):
            for k in (2, 1, 3):
                pl.semaphore_signal(hub, inc=1, device_id={"bl": y_peer(k)[0]}, device_id_type=MESH)
        if at == HALF:
            pl.semaphore_wait(hub, NY - 1)
            for to in (7, 6, 5):
                pl.semaphore_signal(ready_y, inc=1, device_id={"bl": z_peer(to)}, device_id_type=MESH)
        pass_on(at)
        if at < HALF:
            for v in (1, 2, 3, 0):
                if v != at:
                    take_in(v)
            if at:
                send_down(0, 0)
            if at == HALF - 1:
                pl.semaphore_wait(hub, NY - 1)
                pl.semaphore_signal(ready_y, inc=1, device_id={"bl": z_peer(HALF)}, device_id_type=MESH)
                lower = pieces(0, HALF)
                to_bl(lower, lower, zs.at[1], zr.at[0], z_peer(HALF)).start()
                for to in (7, 6, 5):
                    send_up(to, 0, HALF)
            for v in range(HALF, NZ):
                take_in(v)
                if at == 1:
                    piece = pieces(v, 1)
                    to_bl(piece, piece, zs.at[1], zr.at[v], z_peer(0)).start()
        else:
            for v in range(HALF, NZ):
                if v != at:
                    take_in(v)
            take_in(0, HALF)

    for at in range(NZ):
        pl.when(z == at)(functools.partial(line, at))

    @pl.when((upper == 1) & (core == 0))
    def _():
        pl.semaphore_wait(ready_c, 1)

    share(upper)
    share(1 - upper)
    pick(upper, True)
    pick(1 - upper, False)

    def compute(i, carry):
        t = lax.div(i, 4)
        at = pl.ds(pl.multiple_of(lax.rem(i, 4) * 128, 128), 128)

        def matrix(ref):
            return [(ref[c, t, :, at], ref[c + 4, t, :, at]) for c in range(4)]

        jp, jq, m, d = matrix(gp), matrix(gq), matrix(model), matrix(meas)
        w = imp[t, :, at]
        a = [
            cmul_add([(jp[2 * r], m[c], False), (jp[2 * r + 1], m[c + 2], False)])
            for r in range(2) for c in range(2)
        ]
        v = [
            cmul_add([(a[2 * r], jq[2 * c], True), (a[2 * r + 1], jq[2 * c + 1], True)])
            for r in range(2) for c in range(2)
        ]
        e = [(w * (d[k][0] - v[k][0]), w * (d[k][1] - v[k][1])) for k in range(4)]
        for k in range(4):
            res[k, t, :, at] = e[k][0]
            res[k + 4, t, :, at] = e[k][1]
        b = [
            cmul_add([(jq[2 * r], m[2 * c], True), (jq[2 * r + 1], m[2 * c + 1], True)])
            for r in range(2) for c in range(2)
        ]
        first = [
            cmul_add([(e[2 * r], b[c], False), (e[2 * r + 1], b[c + 2], False)])
            for r in range(2) for c in range(2)
        ]
        second = [
            cmul_add([(a[c], e[r], True), (a[c + 2], e[r + 2], True)])
            for r in range(2) for c in range(2)
        ]
        for k in range(4):
            gp[k, t, :, at] = first[k][0]
            gp[k + 4, t, :, at] = first[k][1]
            gq[k, t, :, at] = second[k][0]
            gq[k + 4, t, :, at] = second[k][1]
        return carry

    lax.fori_loop(0, 16, compute, 0)

    p_high, p_low = halves(gp[...].reshape(LANES, PAIRS))
    q_high, q_low = halves(gq[...].reshape(LANES, PAIRS))
    nt = (((1,), (1,)), ((), ()))

    def add_up(v, count):
        rows = pl.ds(v * 64, count * 64)
        h1, h2 = hot1[rows, :], hot2[rows, :]
        total = lax.dot_general(h1, p_high, nt, preferred_element_type=F32)
        total += lax.dot_general(h1, p_low, nt, preferred_element_type=F32)
        total += lax.dot_general(h2, q_high, nt, preferred_element_type=F32)
        total += lax.dot_general(h2, q_low, nt, preferred_element_type=F32)
        part[pl.ds(v, count)] = total.reshape(count, NC, NY, 8, LANES)

    def hand_over(v, carry):
        to_bl(part.at[v, 1 - core], got_c.at[v], rcs.at[0], rcr.at[v], other).start()
        return carry

    def along_y(v, carry):
        got = got_c.at[v]
        to_bl(got, got, rcs.at[0], rcr.at[v], other).wait_recv()
        part[v, core] = part[v, core] + got_c[v]
        for k in (2, 1, 3):
            peer, to = y_peer(k)
            to_bl(part.at[v, core, to], got_y.at[v, k - 1], rys.at[0], ryr.at[v], peer).start()
        return carry

    def send_on(v):
        @pl.when(v != z)
        def _():
            to_bl(part.at[v, core, y], got_z.at[z], rzs.at[0], rzr.at[0], z_peer(v)).start()

    def along_z(v, carry):
        got = got_y.at[v]
        to_bl(got, got, rys.at[0], ryr.at[v], other).wait_recv()
        part[v, core, y] = part[v, core, y] + got_y[v, 0] + (got_y[v, 1] + got_y[v, 2])
        send_on(v)
        return carry

    add_up(0, DIRECT)
    for v in range(DIRECT):
        for slot, (dy, dc) in enumerate(((2, 0), (2, 1), (1, 0), (1, 1), (3, 0), (3, 1), (0, 1))):
            to_y, to_core = lax.rem(y + dy, NY), lax.rem(core + dc, NC)
            to_bl(
                part.at[v, to_core, to_y], got_0.at[v, slot], r0s.at[0], r0r.at[v],
                join_index(to_y, z, to_core),
            ).start()
    add_up(DIRECT, NZ - DIRECT)
    lax.fori_loop(DIRECT, NZ, hand_over, 0)
    lax.fori_loop(DIRECT, NZ, along_y, 0)
    for v in range(DIRECT):
        got = got_0.at[v]
        to_bl(got, got, r0s.at[0], r0r.at[v], other).wait_recv()
        total = part[v, core, y]
        for slot in range(7):
            total = total + got_0[v, slot]
        part[v, core, y] = total
        send_on(v)
    lax.fori_loop(DIRECT, NZ, along_z, 0)
    got_z[z] = part[z, core, y]

    for edge in edges:
        edge.wait_recv()

    @pl.when(early)
    def _():
        for edge in edges:
            edge.start()

    from_prev, from_next = halo_got[0], halo_got[1]
    x = own

    def shift(v, by):
        return pltpu.roll(v, by % LANES, 1)

    prev_edge = jnp.concatenate([pltpu.roll(from_prev, 121, 1), pltpu.roll(from_prev, 122, 1)], axis=1)
    next_edge = jnp.concatenate([pltpu.roll(from_next, 7, 1), pltpu.roll(from_next, 6, 1)], axis=1)
    next_weight = jnp.concatenate([pltpu.roll(from_next, 5, 1)] * 2, axis=1)
    is_first, is_last = freq == 0, freq == CHANNELS - 1
    not_low = jnp.where(chan > 0, 1.0, 0.0).astype(F32)
    not_high = jnp.where(chan < n_chan - 1, 1.0, 0.0).astype(F32)

    def slope(w, step):
        square = step * step
        for by in (128, 64, 32):
            square = square + shift(square, by)
        return w * step / jnp.sqrt(square + SMOOTH_EPS)

    grad = slope(
        jnp.where(is_first, weight * not_low, weight), x - jnp.where(is_first, prev_edge, shift(x, 1))
    )
    grad -= slope(
        jnp.where(is_last, next_weight * not_high, shift(weight, -1)),
        jnp.where(is_last, next_edge, shift(x, -1)) - x,
    )
    grad += slope(jnp.where(time > 0, weight, 0.0), x - shift(x, 8))
    grad -= slope(jnp.where(time < TIMES - 1, weight, 0.0), shift(x, -8) - x)
    updated = x - (STEP * TV_SCALE) * grad

    rows = got_z.at[pl.ds(0, NZ - 1)]
    to_bl(rows, rows, rzs.at[0], rzr.at[0], other).wait_recv()
    total = got_z[0]
    for v in range(1, NZ):
        total = total + got_z[v]
    updated = updated + STEP * total
    upd_ref[...] = jnp.transpose(updated).reshape(8, TIMES, CHANNELS, 8)

    for edge in edges:
        edge.wait_send()

    def left(at):
        for sem, count in ((0, (3, 1, 2, 3, 3, 4, 5, 6)[at]), (1, (0, 6, 1, 16, 3, 2, 1, 0)[at])):
            if count:
                sent = part.at[pl.ds(0, count), 0, 0] if count <= NZ else part.at[pl.ds(0, count // NY), 0]
                to_bl(sent, sent, zs.at[sem], rzr.at[0], other).wait_send()

    for at in range(NZ):
        pl.when(z == at)(functools.partial(left, at))

    to_bl(rows, rows, rzs.at[0], rzr.at[0], other).wait_send()
    half = part.at[pl.ds(0, NZ), 0]
    to_bl(half, half, cs.at[0], rzr.at[0], other).wait_send()
    seven = part.at[pl.ds(0, NZ - DIRECT), 0]
    to_bl(seven, seven, rcs.at[0], rzr.at[0], other).wait_send()
    to_bl(got_0, got_0, r0s.at[0], rzr.at[0], other).wait_send()
    to_bl(got_y, got_y, ys.at[0], rzr.at[0], other).wait_send()
    most = got_y.at[pl.ds(0, NZ - DIRECT)]
    to_bl(most, most, rys.at[0], rzr.at[0], other).wait_send()


def local(meas, model, imp, tally, one, two, gains, tvw):
    big = (8, TIMES, CHANNELS, PAIRS)
    vmem = pltpu.VMEM
    dma = pltpu.SemaphoreType.DMA
    flag = pltpu.SemaphoreType.REGULAR
    any_spec = pl.BlockSpec(memory_space=pl.ANY)
    vmem_spec = pl.BlockSpec(memory_space=pltpu.VMEM)
    return pl.pallas_call(
        kernel,
        out_shape=(vmem((8, TIMES, CHANNELS, 8), F32), vmem(big, F32)),
        in_specs=[any_spec] * 8,
        out_specs=(vmem_spec, vmem_spec),
        scratch_shapes=[
            vmem(big, F32), vmem(big, F32), vmem((TIMES, CHANNELS, PAIRS), F32),
            vmem((1, PAIRS), jnp.int32), vmem((1, PAIRS), jnp.int32), vmem((1, PAIRS), jnp.int32),
            vmem((8, TIMES, CHANNELS, 8), F32), vmem((CHANNELS, 8), F32),
            vmem((NZ, NC, NY, 8, LANES), F32), vmem((STATIONS, PAIRS), BF16), vmem((STATIONS, PAIRS), BF16),
            vmem(big, F32), vmem(big, F32), vmem((NZ, NC, NY, 8, LANES), F32),
            vmem((DIRECT, 7, 8, LANES), F32), vmem((NZ, NY, 8, LANES), F32), vmem((NZ, NY - 1, 8, LANES), F32), vmem((NZ, 8, LANES), F32),
            vmem((8, 128), F32), vmem((2, 8, 128), F32),
            dma((8,)), dma((2,)), dma((NZ,)), dma((1,)), dma((2,)), dma((1,)), dma((2,)), dma((2,)), dma((2,)),
            dma((1,)), dma((DIRECT,)), dma((1,)), dma((NZ,)), dma((1,)), dma((NZ,)), dma((1,)), dma((1,)),
            flag((NZ,)), flag, flag, flag,
        ],
        compiler_params=pltpu.CompilerParams(
            collective_id=0, has_side_effects=True, vmem_limit_bytes=58 * 1024 * 1024
        ),
    )(meas, model, imp, tally, one.reshape(1, PAIRS), two.reshape(1, PAIRS), gains, tvw)


def solution(mesh):
    placed = (
        P(None, None, "chan", "bl"),
        P(None, None, "chan", "bl"),
        P(None, "chan", "bl"),
        P("chan", "bl"),
        P("bl"),
        P("bl"),
        P(None, None, "chan", "bl"),
        P("chan", "bl"),
    )
    return jax.shard_map(
        local,
        mesh=mesh,
        in_specs=placed,
        out_specs=(P(None, None, "chan", "bl"), P(None, None, "chan", "bl")),
        check_vma=False,
    )
```

```python
import functools

import jax
import jax.numpy as jnp
from jax import lax
from jax.experimental import pallas as pl
from jax.experimental.pallas import tpu as pltpu
from jax.sharding import PartitionSpec as P

MESH = pl.DeviceIdType.MESH
STATIONS = 512
BASELINES = 32768
TIMES = 4
CHANNELS = 8
PAIRS = 512
LANES = 8 * TIMES * CHANNELS
NY, NZ, NC = 4, 8, 2
HALF = NZ // 2
DIRECT = 2
SMOOTH_EPS = 0.01
TV_SCALE = 2.0
STEP = 2.0 * STATIONS / BASELINES
F32 = jnp.float32
BF16 = jnp.bfloat16


def cmul_add(terms):
    real, imag = None, None
    for (ar, ai), (br, bi), conj in terms:
        if conj:
            r, i = ar * br + ai * bi, ai * br - ar * bi
        else:
            r, i = ar * br - ai * bi, ar * bi + ai * br
        real = r if real is None else real + r
        imag = i if imag is None else imag + i
    return real, imag


def halves(x):
    high = x.astype(BF16)
    return high, (x - high.astype(F32)).astype(BF16)


def split_index():
    bl = lax.axis_index("bl")
    return lax.div(bl, NZ * NC), lax.rem(lax.div(bl, NC), NZ), lax.rem(bl, NC)


def join_index(y, z, core):
    return (y * NZ + z) * NC + core


def kernel(
    meas_h, model_h, imp_h, tally_h, one_h, two_h, gains_h, tvw_h,
    upd_ref, res,
    meas, model, imp, tally, one, two, gains, tvw,
    table, hot1, hot2, gp, gq, part, got_0, got_c, got_y, got_z, halo, halo_got,
    in_sem, zs, zr, ys, yr, cs, cr, hs, hr, r0s, r0r, rcs, rcr, rys, ryr, rzs, rzr,
    ready_z, ready_y, ready_c, hub,
):
    chan = lax.axis_index("chan")
    n_chan = lax.axis_size("chan")
    odd = lax.rem(chan, 2)
    y, z, core = split_index()
    early = odd == 0
    chan_peers = [lax.rem(chan + 1, n_chan), lax.rem(chan + n_chan - 1, n_chan)]

    def to_bl(src, dst, send, recv, peer):
        return pltpu.make_async_remote_copy(
            src_ref=src, dst_ref=dst, send_sem=send, recv_sem=recv,
            device_id={"bl": peer}, device_id_type=MESH,
        )

    def z_peer(to):
        return join_index(y, to, core)

    def y_peer(k):
        to = lax.rem(y + k, NY)
        return join_index(to, z, core), to

    other = join_index(y, z, 1 - core)

    loads = [
        pltpu.make_async_copy(src, dst, in_sem.at[i])
        for i, (src, dst) in enumerate(
            [(gains_h, gains), (one_h, one), (two_h, two), (tvw_h, tvw), (tally_h, tally),
             (imp_h, imp), (meas_h, meas), (model_h, model)]
        )
    ]
    loads[0].start()
    barrier = pltpu.get_barrier_semaphore()

    second = lax.rem(y + core, 2)
    upper = lax.div(z, HALF)
    beside = [y_peer(1)[0], y_peer(3)[0], other]

    def tell_beside(sem):
        for peer in beside:
            pl.semaphore_signal(sem, inc=1, device_id={"bl": peer}, device_id_type=MESH)

    def announce(to, carry):
        pl.semaphore_signal(barrier, inc=1, device_id={"bl": z_peer(to)}, device_id_type=MESH)
        return carry

    lax.fori_loop(0, (1 - upper) * z, announce, 0)
    lax.fori_loop(jnp.where(z == 0, NZ, jnp.maximum(z + 1, HALF)), NZ, announce, 0)
    pl.when((upper == 0) & (second == 0))(lambda: tell_beside(barrier))

    @pl.when((upper == 1) & (core == 0))
    def _():
        pl.semaphore_signal(barrier, inc=1, device_id={"bl": other}, device_id_type=MESH)

    @pl.when(early)
    def _():
        for peer in chan_peers:
            pl.semaphore_signal(barrier, inc=1, device_id={"chan": peer}, device_id_type=MESH)

    earlier = upper * (z - 1) + (1 - upper) * (HALF - 1 - z) + (1 - upper) * 3 * second + upper * core + 2 * odd

    @pl.when(earlier > 0)
    def _():
        pl.semaphore_wait(barrier, earlier)

    def tell_z(to, carry):
        pl.semaphore_signal(ready_z.at[z], inc=1, device_id={"bl": z_peer(to)}, device_id_type=MESH)
        return carry

    lax.fori_loop(HALF - 1, z, tell_z, 0)
    pl.when((upper == 0) & (second == 1))(lambda: tell_beside(ready_y))

    @pl.when((upper == 1) & (core == 1))
    def _():
        pl.semaphore_signal(ready_c, inc=1, device_id={"bl": other}, device_id_type=MESH)

    loads[0].wait()
    own = jnp.transpose(gains[...].reshape(LANES, 8))
    table[z, core, y] = own

    mine = table.at[z, core, y]

    def send_own(to, carry):
        to_bl(mine, mine, zs.at[0], zr.at[z], z_peer(to)).start()
        return carry

    lax.fori_loop(1 + (1 - upper) * z, upper * z + (1 - upper) * HALF, send_own, 0)
    for load in loads[1:]:
        load.start()

    @pl.when((upper == 0) & (second == 0))
    def _():
        pl.semaphore_wait(ready_y, 3)
        tell_beside(ready_y)


    loads[3].wait()
    lane = lax.broadcasted_iota(jnp.int32, (8, LANES), 1)
    freq, time = lane & 7, lax.shift_right_logical(lane, 3) & 3
    weight = jnp.transpose(
        jnp.broadcast_to(tvw[...][None], (8 * TIMES, CHANNELS, 8)).reshape(LANES, 8)
    )
    low, high = own[:, :128], own[:, 128:]
    freq_h = freq[:, :128]
    halo[...] = jnp.where(
        freq_h == 0, low,
        jnp.where(
            freq_h == 1, pltpu.roll(high, 1, 1),
            jnp.where(
                freq_h == 7, low,
                jnp.where(freq_h == 6, pltpu.roll(high, 127, 1), pltpu.roll(weight[:, :128], 2, 1)),
            ),
        ),
    )
    edges = [
        pltpu.make_async_remote_copy(
            src_ref=halo, dst_ref=halo_got.at[k], send_sem=hs.at[k], recv_sem=hr.at[k],
            device_id={"chan": peer}, device_id_type=MESH,
        )
        for k, peer in enumerate(chan_peers)
    ]

    @pl.when(jnp.logical_not(early))
    def _():
        for edge in edges:
            edge.start()

    loads[1].wait()
    loads[2].wait()

    def to_row(ant):
        return (
            (lax.shift_right_logical(ant, 4) & 7) * 64 + (lax.shift_right_logical(ant, 3) & 1) * 32
            + lax.shift_right_logical(ant, 7) * 8 + (ant & 7)
        )

    row1, row2 = to_row(one[...]), to_row(two[...])

    def hot_body(i, carry):
        index = lax.broadcasted_iota(jnp.int32, (32, PAIRS), 0) + i * 32
        v, half = lax.div(i, NC), lax.rem(i, NC)
        hot1[v, half] = jnp.where(index == row1, 1.0, 0.0).astype(BF16)
        hot2[v, half] = jnp.where(index == row2, 1.0, 0.0).astype(BF16)
        return carry

    lax.fori_loop(0, 16, hot_body, 0)

    loads[4].wait()
    loads[5].wait()
    keep = lax.broadcasted_iota(jnp.int32, (CHANNELS, PAIRS), 0) < CHANNELS - tally[...]
    for t in range(TIMES):
        imp[t] = jnp.where(keep, imp[t], 0.0)
    loads[6].wait()
    loads[7].wait()

    def pieces(v, count):
        return table.at[v, core, y] if count == 1 else table.at[pl.ds(v, count), core, y]

    def send_up(to, v, count):
        pl.semaphore_wait(ready_z.at[to], 1)
        rows = pieces(v, count)
        to_bl(rows, rows, zs.at[1], zr.at[v], z_peer(to)).start()

    def wait_for(v, count=1):
        rows = pieces(v, count)
        to_bl(rows, rows, zs.at[1], zr.at[v], other).wait_recv()

    def pass_on(v, count=1):
        rows = pieces(v, count)
        for k in (2, 1, 3):
            to_bl(rows, rows, ys.at[0], yr.at[v // HALF], y_peer(k)[0]).start()

    def take_in(v, count=1):
        wait_for(v, count)
        pass_on(v, count)

    def share(half):
        three = table.at[pl.ds(half * HALF, HALF), core, pl.ds(0, 3)]
        to_bl(three, three, ys.at[0], yr.at[half], other).wait_recv()
        four = table.at[pl.ds(half * HALF, HALF), core]
        to_bl(four, four, cs.at[0], cr.at[half], other).start()

    def pick(half, first):
        flipped = jnp.transpose(table[:, half].reshape(256, LANES))
        g_high, g_low = halves(flipped)
        for hot, dst in ((hot1, gp), (hot2, gq)):
            rows = hot[:, half].reshape(256, PAIRS)
            picked = jnp.dot(g_high, rows, preferred_element_type=F32) + jnp.dot(
                g_low, rows, preferred_element_type=F32
            )
            picked = picked.reshape(8, TIMES, CHANNELS, PAIRS)
            dst[...] = picked if first else dst[...] + picked

    def line(at):
        for to in range(at + 1, NZ) if at >= HALF else ():
            send_up(to, at, 1)
        if at < HALF:

            @pl.when(second == 1)
            def _():
                pl.semaphore_wait(ready_y, 3)

        else:
            pl.semaphore_wait(ready_y, 1)
        if at == HALF - 1:
            pl.semaphore_wait(ready_z.at[HALF], 1)
        if at in (HALF - 1, HALF):
            for k in (2, 1, 3):
                pl.semaphore_signal(hub, inc=1, device_id={"bl": y_peer(k)[0]}, device_id_type=MESH)
        if at == HALF:
            pl.semaphore_wait(hub, NY - 1)
            for to in (7, 6, 5):
                pl.semaphore_signal(ready_y, inc=1, device_id={"bl": z_peer(to)}, device_id_type=MESH)
        pass_on(at)
        if at < HALF:
            for v in (3, 2, 1, 0):
                if v != at:
                    take_in(v)
                if v < at:
                    send_own(v, 0)
            if at == HALF - 1:
                pl.semaphore_wait(hub, NY - 1)
                pl.semaphore_signal(ready_y, inc=1, device_id={"bl": z_peer(HALF)}, device_id_type=MESH)
                lower = pieces(0, HALF)
                to_bl(lower, lower, zs.at[1], zr.at[0], z_peer(HALF)).start()
                for to in (5, 6, 7):
                    send_up(to, 0, HALF)
            for v in range(HALF, NZ):
                take_in(v)
                if at == 1:
                    piece = pieces(v, 1)
                    to_bl(piece, piece, zs.at[1], zr.at[v], z_peer(0)).start()
        else:
            for v in range(HALF, NZ):
                if v != at:
                    take_in(v)
            take_in(0, HALF)

    for at in range(NZ):
        pl.when(z == at)(functools.partial(line, at))

    @pl.when((upper == 1) & (core == 0))
    def _():
        pl.semaphore_wait(ready_c, 1)

    share(upper)
    share(1 - upper)
    pick(core, True)
    for half in range(2):
        four = table.at[pl.ds(half * HALF, HALF), 1 - core]
        to_bl(four, four, cs.at[0], cr.at[half], other).wait_recv()
    pick(1 - core, False)

    def compute(i, carry):
        t = lax.div(i, 4)
        at = pl.ds(pl.multiple_of(lax.rem(i, 4) * 128, 128), 128)

        def matrix(ref):
            return [(ref[c, t, :, at], ref[c + 4, t, :, at]) for c in range(4)]

        jp, jq, m, d = matrix(gp), matrix(gq), matrix(model), matrix(meas)
        w = imp[t, :, at]
        a = [
            cmul_add([(jp[2 * r], m[c], False), (jp[2 * r + 1], m[c + 2], False)])
            for r in range(2) for c in range(2)
        ]
        v = [
            cmul_add([(a[2 * r], jq[2 * c], True), (a[2 * r + 1], jq[2 * c + 1], True)])
            for r in range(2) for c in range(2)
        ]
        e = [(w * (d[k][0] - v[k][0]), w * (d[k][1] - v[k][1])) for k in range(4)]
        for k in range(4):
            res[k, t, :, at] = e[k][0]
            res[k + 4, t, :, at] = e[k][1]
        b = [
            cmul_add([(jq[2 * r], m[2 * c], True), (jq[2 * r + 1], m[2 * c + 1], True)])
            for r in range(2) for c in range(2)
        ]
        first = [
            cmul_add([(e[2 * r], b[c], False), (e[2 * r + 1], b[c + 2], False)])
            for r in range(2) for c in range(2)
        ]
        second = [
            cmul_add([(a[c], e[r], True), (a[c + 2], e[r + 2], True)])
            for r in range(2) for c in range(2)
        ]
        for k in range(4):
            gp[k, t, :, at] = first[k][0]
            gp[k + 4, t, :, at] = first[k][1]
            gq[k, t, :, at] = second[k][0]
            gq[k + 4, t, :, at] = second[k][1]
        return carry

    lax.fori_loop(0, 16, compute, 0, unroll=2)

    p_high, p_low = halves(gp[...].reshape(LANES, PAIRS))
    q_high, q_low = halves(gq[...].reshape(LANES, PAIRS))
    nt = (((1,), (1,)), ((), ()))

    def add_up(v, count):
        h1, h2 = (hot[pl.ds(v, count)].reshape(count * 64, PAIRS) for hot in (hot1, hot2))
        total = lax.dot_general(h1, p_high, nt, preferred_element_type=F32)
        total += lax.dot_general(h1, p_low, nt, preferred_element_type=F32)
        total += lax.dot_general(h2, q_high, nt, preferred_element_type=F32)
        total += lax.dot_general(h2, q_low, nt, preferred_element_type=F32)
        part[pl.ds(v, count)] = total.reshape(count, NC, NY, 8, LANES)

    def from_end(v):
        return v + odd * (NZ - 1 - 2 * v)

    def hand_over(step, carry):
        v = from_end(step)
        to_bl(part.at[v, 1 - core], got_c.at[v], rcs.at[0], rcr.at[v], other).start()
        return carry

    def along_y(step, carry):
        v = from_end(step)
        got = got_c.at[v]
        to_bl(got, got, rcs.at[0], rcr.at[v], other).wait_recv()
        part[v, core] = part[v, core] + got_c[v]
        for k in (2, 1, 3):
            peer, to = y_peer(k)
            to_bl(part.at[v, core, to], got_y.at[v, k - 1], rys.at[0], ryr.at[v], peer).start()
        return carry

    def send_on(v):
        @pl.when(v != z)
        def _():
            to_bl(part.at[v, core, y], got_z.at[z], rzs.at[0], rzr.at[0], z_peer(v)).start()

    def along_z(step, carry):
        v = from_end(step)
        got = got_y.at[v]
        to_bl(got, got, rys.at[0], ryr.at[v], other).wait_recv()
        part[v, core, y] = part[v, core, y] + got_y[v, 0] + (got_y[v, 1] + got_y[v, 2])
        send_on(v)
        return carry

    add_up(odd * (NZ - DIRECT), DIRECT)
    for v in range(DIRECT):
        at_v = from_end(v)
        for slot, (dy, dc) in enumerate(((2, 0), (2, 1), (1, 0), (1, 1), (3, 0), (3, 1), (0, 1))):
            to_y, to_core = lax.rem(y + dy, NY), lax.rem(core + dc, NC)
            to_bl(
                part.at[at_v, to_core, to_y], got_0.at[v, slot], r0s.at[0], r0r.at[v],
                join_index(to_y, z, to_core),
            ).start()
    add_up((1 - odd) * DIRECT, NZ - DIRECT)
    lax.fori_loop(DIRECT, NZ, hand_over, 0)
    lax.fori_loop(DIRECT, NZ, along_y, 0)
    for v in range(DIRECT):
        got = got_0.at[v]
        to_bl(got, got, r0s.at[0], r0r.at[v], other).wait_recv()
        at_v = from_end(v)
        total = part[at_v, core, y]
        for slot in range(7):
            total = total + got_0[v, slot]
        part[at_v, core, y] = total
        send_on(at_v)
    lax.fori_loop(DIRECT, NZ, along_z, 0)
    got_z[z] = part[z, core, y]

    for edge in edges:
        edge.wait_recv()

    @pl.when(early)
    def _():
        for edge in edges:
            edge.start()

    from_prev, from_next = halo_got[0], halo_got[1]
    x = own

    def shift(v, by):
        return pltpu.roll(v, by % LANES, 1)

    prev_edge = jnp.concatenate([pltpu.roll(from_prev, 121, 1), pltpu.roll(from_prev, 122, 1)], axis=1)
    next_edge = jnp.concatenate([pltpu.roll(from_next, 7, 1), pltpu.roll(from_next, 6, 1)], axis=1)
    next_weight = jnp.concatenate([pltpu.roll(from_next, 5, 1)] * 2, axis=1)
    is_first, is_last = freq == 0, freq == CHANNELS - 1
    not_low = jnp.where(chan > 0, 1.0, 0.0).astype(F32)
    not_high = jnp.where(chan < n_chan - 1, 1.0, 0.0).astype(F32)

    def slope(w, step):
        square = step * step
        for by in (128, 64, 32):
            square = square + shift(square, by)
        return w * step / jnp.sqrt(square + SMOOTH_EPS)

    grad = slope(
        jnp.where(is_first, weight * not_low, weight), x - jnp.where(is_first, prev_edge, shift(x, 1))
    )
    grad -= slope(
        jnp.where(is_last, next_weight * not_high, shift(weight, -1)),
        jnp.where(is_last, next_edge, shift(x, -1)) - x,
    )
    grad += slope(jnp.where(time > 0, weight, 0.0), x - shift(x, 8))
    grad -= slope(jnp.where(time < TIMES - 1, weight, 0.0), shift(x, -8) - x)
    updated = x - (STEP * TV_SCALE) * grad

    rows = got_z.at[pl.ds(0, NZ - 1)]
    to_bl(rows, rows, rzs.at[0], rzr.at[0], other).wait_recv()
    total = got_z[0]
    for v in range(1, NZ):
        total = total + got_z[v]
    updated = updated + STEP * total
    upd_ref[...] = jnp.transpose(updated).reshape(8, TIMES, CHANNELS, 8)

    for edge in edges:
        edge.wait_send()

    def left(at):
        for sem, count in ((0, (3, 3, 3, 3, 3, 4, 5, 6)[at]), (1, (0, 4, 0, 16, 3, 2, 1, 0)[at])):
            if count:
                sent = part.at[pl.ds(0, count), 0, 0] if count <= NZ else part.at[pl.ds(0, count // NY), 0]
                to_bl(sent, sent, zs.at[sem], rzr.at[0], other).wait_send()

    for at in range(NZ):
        pl.when(z == at)(functools.partial(left, at))

    to_bl(rows, rows, rzs.at[0], rzr.at[0], other).wait_send()
    half = part.at[pl.ds(0, NZ), 0]
    to_bl(half, half, cs.at[0], rzr.at[0], other).wait_send()
    seven = part.at[pl.ds(0, NZ - DIRECT), 0]
    to_bl(seven, seven, rcs.at[0], rzr.at[0], other).wait_send()
    to_bl(got_0, got_0, r0s.at[0], rzr.at[0], other).wait_send()
    to_bl(got_y, got_y, ys.at[0], rzr.at[0], other).wait_send()
    most = got_y.at[pl.ds(0, NZ - DIRECT)]
    to_bl(most, most, rys.at[0], rzr.at[0], other).wait_send()


def hand_out(updated, residual, updated_h, residual_h, sem):
    copies = [
        pltpu.make_async_copy(residual, residual_h, sem.at[0]),
        pltpu.make_async_copy(updated, updated_h, sem.at[1]),
    ]
    for copy in copies:
        copy.start()
    for copy in copies:
        copy.wait()


def local(meas, model, imp, tally, one, two, gains, tvw):
    big = (8, TIMES, CHANNELS, PAIRS)
    vmem = pltpu.VMEM
    dma = pltpu.SemaphoreType.DMA
    flag = pltpu.SemaphoreType.REGULAR
    any_spec = pl.BlockSpec(memory_space=pl.ANY)
    vmem_spec = pl.BlockSpec(memory_space=pltpu.VMEM)
    updated, residual = pl.pallas_call(
        kernel,
        out_shape=(vmem((8, TIMES, CHANNELS, 8), F32), vmem(big, F32)),
        in_specs=[any_spec] * 8,
        out_specs=(vmem_spec, vmem_spec),
        scratch_shapes=[
            vmem(big, F32), vmem(big, F32), vmem((TIMES, CHANNELS, PAIRS), F32),
            vmem((1, PAIRS), jnp.int32), vmem((1, PAIRS), jnp.int32), vmem((1, PAIRS), jnp.int32),
            vmem((8, TIMES, CHANNELS, 8), F32), vmem((CHANNELS, 8), F32),
            vmem((NZ, NC, NY, 8, LANES), F32), vmem((NZ, NC, 32, PAIRS), BF16), vmem((NZ, NC, 32, PAIRS), BF16),
            vmem(big, F32), vmem(big, F32), vmem((NZ, NC, NY, 8, LANES), F32),
            vmem((DIRECT, 7, 8, LANES), F32), vmem((NZ, NY, 8, LANES), F32), vmem((NZ, NY - 1, 8, LANES), F32), vmem((NZ, 8, LANES), F32),
            vmem((8, 128), F32), vmem((2, 8, 128), F32),
            dma((8,)), dma((2,)), dma((NZ,)), dma((1,)), dma((2,)), dma((1,)), dma((2,)), dma((2,)), dma((2,)),
            dma((1,)), dma((DIRECT,)), dma((1,)), dma((NZ,)), dma((1,)), dma((NZ,)), dma((1,)), dma((1,)),
            flag((NZ,)), flag, flag, flag,
        ],
        compiler_params=pltpu.CompilerParams(
            collective_id=0, has_side_effects=True, vmem_limit_bytes=58 * 1024 * 1024
        ),
    )(meas, model, imp, tally, one.reshape(1, PAIRS), two.reshape(1, PAIRS), gains, tvw)
    held = [pltpu.with_memory_space_constraint(x, pltpu.VMEM) for x in (updated, residual)]
    return pl.pallas_call(
        hand_out,
        out_shape=(jax.ShapeDtypeStruct(updated.shape, F32), jax.ShapeDtypeStruct(residual.shape, F32)),
        in_specs=[vmem_spec, vmem_spec],
        out_specs=(any_spec, any_spec),
        scratch_shapes=[dma((2,))],
    )(*held)


def solution(mesh):
    placed = (
        P(None, None, "chan", "bl"),
        P(None, None, "chan", "bl"),
        P(None, "chan", "bl"),
        P("chan", "bl"),
        P("bl"),
        P("bl"),
        P(None, None, "chan", "bl"),
        P("chan", "bl"),
    )
    return jax.shard_map(
        local,
        mesh=mesh,
        in_specs=placed,
        out_specs=(P(None, None, "chan", "bl"), P(None, None, "chan", "bl")),
        check_vma=False,
    )
```

```python
import functools

import jax
import jax.numpy as jnp
from jax import lax
from jax.experimental import pallas as pl
from jax.experimental.pallas import tpu as pltpu
from jax.sharding import PartitionSpec as P

MESH = pl.DeviceIdType.MESH
STATIONS = 512
BASELINES = 32768
TIMES = 4
CHANNELS = 8
PAIRS = 512
LANES = 8 * TIMES * CHANNELS
NY, NZ, NC = 4, 8, 2
HALF = NZ // 2
DIRECT = 2
SMOOTH_EPS = 0.01
TV_SCALE = 2.0
STEP = 2.0 * STATIONS / BASELINES
F32 = jnp.float32
BF16 = jnp.bfloat16


def cmul_add(terms):
    real, imag = None, None
    for (ar, ai), (br, bi), conj in terms:
        if conj:
            r, i = ar * br + ai * bi, ai * br - ar * bi
        else:
            r, i = ar * br - ai * bi, ar * bi + ai * br
        real = r if real is None else real + r
        imag = i if imag is None else imag + i
    return real, imag


def halves(x):
    high = x.astype(BF16)
    return high, (x - high.astype(F32)).astype(BF16)


def split_index():
    bl = lax.axis_index("bl")
    return lax.div(bl, NZ * NC), lax.rem(lax.div(bl, NC), NZ), lax.rem(bl, NC)


def join_index(y, z, core):
    return (y * NZ + z) * NC + core


def kernel(
    meas_h, model_h, imp_h, tally_h, one_h, two_h, gains_h, tvw_h,
    upd_ref, res,
    meas, model, imp, tally, one, two, gains, tvw,
    table, hot1, hot2, gp, gq, part, got_0, got_c, got_y, got_z, halo, halo_got,
    in_sem, zs, zr, ys, yr, cs, cr, hs, hr, r0s, r0r, rcs, rcr, rys, ryr, rzs, rzr,
    ready_z, ready_y, ready_c, hub,
):
    chan = lax.axis_index("chan")
    n_chan = lax.axis_size("chan")
    odd = lax.rem(chan, 2)
    y, z, core = split_index()
    early = odd == 0
    chan_peers = [lax.rem(chan + 1, n_chan), lax.rem(chan + n_chan - 1, n_chan)]

    def to_bl(src, dst, send, recv, peer):
        return pltpu.make_async_remote_copy(
            src_ref=src, dst_ref=dst, send_sem=send, recv_sem=recv,
            device_id={"bl": peer}, device_id_type=MESH,
        )

    def z_peer(to):
        return join_index(y, to, core)

    def y_peer(k):
        to = lax.rem(y + k, NY)
        return join_index(to, z, core), to

    other = join_index(y, z, 1 - core)

    loads = [
        pltpu.make_async_copy(src, dst, in_sem.at[i])
        for i, (src, dst) in enumerate(
            [(gains_h, gains), (one_h, one), (two_h, two), (tvw_h, tvw), (tally_h, tally),
             (imp_h, imp), (meas_h, meas), (model_h, model)]
        )
    ]
    loads[0].start()
    barrier = pltpu.get_barrier_semaphore()

    second = lax.rem(y + core, 2)
    upper = lax.div(z, HALF)
    beside = [y_peer(1)[0], y_peer(3)[0], other]

    def tell_beside(sem):
        for peer in beside:
            pl.semaphore_signal(sem, inc=1, device_id={"bl": peer}, device_id_type=MESH)

    def announce(to, carry):
        pl.semaphore_signal(barrier, inc=1, device_id={"bl": z_peer(to)}, device_id_type=MESH)
        return carry

    lax.fori_loop(0, (1 - upper) * z, announce, 0)
    lax.fori_loop(jnp.where(z == 0, NZ, jnp.maximum(z + 1, HALF)), NZ, announce, 0)
    pl.when((upper == 0) & (second == 0))(lambda: tell_beside(barrier))

    @pl.when((upper == 1) & (core == 0))
    def _():
        pl.semaphore_signal(barrier, inc=1, device_id={"bl": other}, device_id_type=MESH)

    @pl.when(early)
    def _():
        for peer in chan_peers:
            pl.semaphore_signal(barrier, inc=1, device_id={"chan": peer}, device_id_type=MESH)

    earlier = upper * (z - 1) + (1 - upper) * (HALF - 1 - z) + (1 - upper) * 3 * second + upper * core + 2 * odd

    @pl.when(earlier > 0)
    def _():
        pl.semaphore_wait(barrier, earlier)

    def tell_z(to, carry):
        pl.semaphore_signal(ready_z.at[z], inc=1, device_id={"bl": z_peer(to)}, device_id_type=MESH)
        return carry

    lax.fori_loop(HALF - 1, z, tell_z, 0)
    pl.when((upper == 0) & (second == 1))(lambda: tell_beside(ready_y))

    @pl.when((upper == 1) & (core == 1))
    def _():
        pl.semaphore_signal(ready_c, inc=1, device_id={"bl": other}, device_id_type=MESH)

    loads[0].wait()
    own = jnp.transpose(gains[...].reshape(LANES, 8))
    table[z, core, y] = own

    mine = table.at[z, core, y]

    def send_own(to, carry):
        to_bl(mine, mine, zs.at[0], zr.at[z], z_peer(to)).start()
        return carry

    lax.fori_loop(1 + (1 - upper) * z, upper * z + (1 - upper) * HALF, send_own, 0)
    for load in loads[1:]:
        load.start()

    @pl.when((upper == 0) & (second == 0))
    def _():
        pl.semaphore_wait(ready_y, 3)
        tell_beside(ready_y)


    loads[3].wait()
    lane = lax.broadcasted_iota(jnp.int32, (8, LANES), 1)
    freq, time = lane & 7, lax.shift_right_logical(lane, 3) & 3
    weight = jnp.transpose(
        jnp.broadcast_to(tvw[...][None], (8 * TIMES, CHANNELS, 8)).reshape(LANES, 8)
    )
    low, high = own[:, :128], own[:, 128:]
    freq_h = freq[:, :128]
    halo[...] = jnp.where(
        freq_h == 0, low,
        jnp.where(
            freq_h == 1, pltpu.roll(high, 1, 1),
            jnp.where(
                freq_h == 7, low,
                jnp.where(freq_h == 6, pltpu.roll(high, 127, 1), pltpu.roll(weight[:, :128], 2, 1)),
            ),
        ),
    )
    edges = [
        pltpu.make_async_remote_copy(
            src_ref=halo, dst_ref=halo_got.at[k], send_sem=hs.at[k], recv_sem=hr.at[k],
            device_id={"chan": peer}, device_id_type=MESH,
        )
        for k, peer in enumerate(chan_peers)
    ]

    @pl.when(jnp.logical_not(early))
    def _():
        for edge in edges:
            edge.start()

    loads[1].wait()
    loads[2].wait()

    def to_row(ant):
        return (
            (lax.shift_right_logical(ant, 4) & 7) * 64 + (lax.shift_right_logical(ant, 3) & 1) * 32
            + lax.shift_right_logical(ant, 7) * 8 + (ant & 7)
        )

    row1, row2 = to_row(one[...]), to_row(two[...])

    def hot_body(i, carry):
        index = lax.broadcasted_iota(jnp.int32, (32, PAIRS), 0) + i * 32
        v, half = lax.div(i, NC), lax.rem(i, NC)
        hot1[v, half] = jnp.where(index == row1, 1.0, 0.0).astype(BF16)
        hot2[v, half] = jnp.where(index == row2, 1.0, 0.0).astype(BF16)
        return carry

    lax.fori_loop(0, 16, hot_body, 0)

    loads[4].wait()
    loads[5].wait()
    keep = lax.broadcasted_iota(jnp.int32, (CHANNELS, PAIRS), 0) < CHANNELS - tally[...]
    for t in range(TIMES):
        imp[t] = jnp.where(keep, imp[t], 0.0)
    loads[6].wait()
    loads[7].wait()

    def pieces(v, count):
        return table.at[v, core, y] if count == 1 else table.at[pl.ds(v, count), core, y]

    def send_up(to, v, count):
        pl.semaphore_wait(ready_z.at[to], 1)
        rows = pieces(v, count)
        to_bl(rows, rows, zs.at[1], zr.at[v], z_peer(to)).start()

    def wait_for(v, count=1):
        rows = pieces(v, count)
        to_bl(rows, rows, zs.at[1], zr.at[v], other).wait_recv()

    def pass_on(v, count=1):
        rows = pieces(v, count)
        for k in (2, 1, 3):
            to_bl(rows, rows, ys.at[0], yr.at[v // HALF], y_peer(k)[0]).start()

    def take_in(v, count=1):
        wait_for(v, count)
        pass_on(v, count)

    def share(half):
        three = table.at[pl.ds(half * HALF, HALF), core, pl.ds(0, 3)]
        to_bl(three, three, ys.at[0], yr.at[half], other).wait_recv()
        four = table.at[pl.ds(half * HALF, HALF), core]
        to_bl(four, four, cs.at[0], cr.at[half], other).start()

    def pick(half, first):
        flipped = jnp.transpose(table[:, half].reshape(256, LANES))
        g_high, g_low = halves(flipped)
        for hot, dst in ((hot1, gp), (hot2, gq)):
            rows = hot[:, half].reshape(256, PAIRS)
            picked = jnp.dot(g_high, rows, preferred_element_type=F32) + jnp.dot(
                g_low, rows, preferred_element_type=F32
            )
            picked = picked.reshape(8, TIMES, CHANNELS, PAIRS)
            dst[...] = picked if first else dst[...] + picked

    def line(at):
        for to in range(at + 1, NZ) if at >= HALF else ():
            send_up(to, at, 1)
        if at < HALF:

            @pl.when(second == 1)
            def _():
                pl.semaphore_wait(ready_y, 3)

        else:
            pl.semaphore_wait(ready_y, 1)
        if at == HALF - 1:
            pl.semaphore_wait(ready_z.at[HALF], 1)
        if at in (HALF - 1, HALF):
            for k in (2, 1, 3):
                pl.semaphore_signal(hub, inc=1, device_id={"bl": y_peer(k)[0]}, device_id_type=MESH)
        if at == HALF:
            pl.semaphore_wait(hub, NY - 1)
            for to in (7, 6, 5):
                pl.semaphore_signal(ready_y, inc=1, device_id={"bl": z_peer(to)}, device_id_type=MESH)
        pass_on(at)
        if at < HALF:
            for v in (3, 2, 1, 0):
                if v != at:
                    take_in(v)
                if v < at:
                    send_own(v, 0)
            if at == HALF - 1:
                pl.semaphore_wait(hub, NY - 1)
                pl.semaphore_signal(ready_y, inc=1, device_id={"bl": z_peer(HALF)}, device_id_type=MESH)
                lower = pieces(0, HALF)
                to_bl(lower, lower, zs.at[1], zr.at[0], z_peer(HALF)).start()
                for to in (5, 6, 7):
                    send_up(to, 0, HALF)
            for v in range(HALF, NZ):
                take_in(v)
                if at == 1:
                    piece = pieces(v, 1)
                    to_bl(piece, piece, zs.at[1], zr.at[v], z_peer(0)).start()
        else:
            for v in range(HALF, NZ):
                if v != at:
                    take_in(v)
            take_in(0, HALF)

    for at in range(NZ):
        pl.when(z == at)(functools.partial(line, at))

    @pl.when((upper == 1) & (core == 0))
    def _():
        pl.semaphore_wait(ready_c, 1)

    share(upper)
    share(1 - upper)
    pick(core, True)
    for half in range(2):
        four = table.at[pl.ds(half * HALF, HALF), 1 - core]
        to_bl(four, four, cs.at[0], cr.at[half], other).wait_recv()
    pick(1 - core, False)

    def compute(i, carry):
        t = lax.div(i, 4)
        at = pl.ds(pl.multiple_of(lax.rem(i, 4) * 128, 128), 128)

        def matrix(ref):
            return [(ref[c, t, :, at], ref[c + 4, t, :, at]) for c in range(4)]

        jp, jq, m, d = matrix(gp), matrix(gq), matrix(model), matrix(meas)
        w = imp[t, :, at]
        a = [
            cmul_add([(jp[2 * r], m[c], False), (jp[2 * r + 1], m[c + 2], False)])
            for r in range(2) for c in range(2)
        ]
        v = [
            cmul_add([(a[2 * r], jq[2 * c], True), (a[2 * r + 1], jq[2 * c + 1], True)])
            for r in range(2) for c in range(2)
        ]
        e = [(w * (d[k][0] - v[k][0]), w * (d[k][1] - v[k][1])) for k in range(4)]
        for k in range(4):
            res[k, t, :, at] = e[k][0]
            res[k + 4, t, :, at] = e[k][1]
        b = [
            cmul_add([(jq[2 * r], m[2 * c], True), (jq[2 * r + 1], m[2 * c + 1], True)])
            for r in range(2) for c in range(2)
        ]
        first = [
            cmul_add([(e[2 * r], b[c], False), (e[2 * r + 1], b[c + 2], False)])
            for r in range(2) for c in range(2)
        ]
        second = [
            cmul_add([(a[c], e[r], True), (a[c + 2], e[r + 2], True)])
            for r in range(2) for c in range(2)
        ]
        for k in range(4):
            gp[k, t, :, at] = first[k][0]
            gp[k + 4, t, :, at] = first[k][1]
            gq[k, t, :, at] = second[k][0]
            gq[k + 4, t, :, at] = second[k][1]
        return carry

    lax.fori_loop(0, 16, compute, 0, unroll=2)

    p_high, p_low = halves(gp[...].reshape(LANES, PAIRS))
    q_high, q_low = halves(gq[...].reshape(LANES, PAIRS))
    nt = (((1,), (1,)), ((), ()))

    def add_up(places):
        h1, h2 = (
            jnp.concatenate([hot[v].reshape(64, PAIRS) for v in places]) for hot in (hot1, hot2)
        )
        total = lax.dot_general(h1, p_high, nt, preferred_element_type=F32)
        total += lax.dot_general(h1, p_low, nt, preferred_element_type=F32)
        total += lax.dot_general(h2, q_high, nt, preferred_element_type=F32)
        total += lax.dot_general(h2, q_low, nt, preferred_element_type=F32)
        for i, v in enumerate(places):
            part[v] = total[i * 64 : i * 64 + 64].reshape(NC, NY, 8, LANES)

    def from_end(v):
        if isinstance(v, int):
            return v + odd * ((v // 2 if v % 2 else NZ - 1 - v // 2) - v)
        far = lax.rem(v, 2)
        return v + odd * (lax.div(v, 2) * (2 * far - 1) + (1 - far) * (NZ - 1) - v)

    def hand_over(step, carry):
        v = from_end(step)
        to_bl(part.at[v, 1 - core], got_c.at[v], rcs.at[0], rcr.at[v], other).start()
        return carry

    def along_y(step, carry):
        v = from_end(step)
        got = got_c.at[v]
        to_bl(got, got, rcs.at[0], rcr.at[v], other).wait_recv()
        part[v, core] = part[v, core] + got_c[v]
        for k in (2, 1, 3):
            peer, to = y_peer(k)
            to_bl(part.at[v, core, to], got_y.at[v, k - 1], rys.at[0], ryr.at[v], peer).start()
        return carry

    def send_on(v):
        @pl.when(v != z)
        def _():
            to_bl(part.at[v, core, y], got_z.at[z], rzs.at[0], rzr.at[0], z_peer(v)).start()

    def along_z(step, carry):
        v = from_end(step)
        got = got_y.at[v]
        to_bl(got, got, rys.at[0], ryr.at[v], other).wait_recv()
        part[v, core, y] = part[v, core, y] + got_y[v, 0] + (got_y[v, 1] + got_y[v, 2])
        send_on(v)
        return carry

    add_up([from_end(v) for v in range(DIRECT)])
    for v in range(DIRECT):
        at_v = from_end(v)
        for slot, (dy, dc) in enumerate(((2, 0), (2, 1), (1, 0), (1, 1), (3, 0), (3, 1), (0, 1))):
            to_y, to_core = lax.rem(y + dy, NY), lax.rem(core + dc, NC)
            to_bl(
                part.at[at_v, to_core, to_y], got_0.at[v, slot], r0s.at[0], r0r.at[v],
                join_index(to_y, z, to_core),
            ).start()
    add_up([DIRECT - odd + v for v in range(NZ - DIRECT)])
    lax.fori_loop(DIRECT, NZ, hand_over, 0)
    lax.fori_loop(DIRECT, NZ, along_y, 0)
    for v in range(DIRECT):
        got = got_0.at[v]
        to_bl(got, got, r0s.at[0], r0r.at[v], other).wait_recv()
        at_v = from_end(v)
        total = part[at_v, core, y]
        for slot in range(7):
            total = total + got_0[v, slot]
        part[at_v, core, y] = total
        send_on(at_v)
    lax.fori_loop(DIRECT, NZ, along_z, 0)
    got_z[z] = part[z, core, y]

    for edge in edges:
        edge.wait_recv()

    @pl.when(early)
    def _():
        for edge in edges:
            edge.start()

    from_prev, from_next = halo_got[0], halo_got[1]
    x = own

    def shift(v, by):
        return pltpu.roll(v, by % LANES, 1)

    prev_edge = jnp.concatenate([pltpu.roll(from_prev, 121, 1), pltpu.roll(from_prev, 122, 1)], axis=1)
    next_edge = jnp.concatenate([pltpu.roll(from_next, 7, 1), pltpu.roll(from_next, 6, 1)], axis=1)
    next_weight = jnp.concatenate([pltpu.roll(from_next, 5, 1)] * 2, axis=1)
    is_first, is_last = freq == 0, freq == CHANNELS - 1
    not_low = jnp.where(chan > 0, 1.0, 0.0).astype(F32)
    not_high = jnp.where(chan < n_chan - 1, 1.0, 0.0).astype(F32)

    def slope(w, step):
        square = step * step
        for by in (128, 64, 32):
            square = square + shift(square, by)
        return w * step / jnp.sqrt(square + SMOOTH_EPS)

    grad = slope(
        jnp.where(is_first, weight * not_low, weight), x - jnp.where(is_first, prev_edge, shift(x, 1))
    )
    grad -= slope(
        jnp.where(is_last, next_weight * not_high, shift(weight, -1)),
        jnp.where(is_last, next_edge, shift(x, -1)) - x,
    )
    grad += slope(jnp.where(time > 0, weight, 0.0), x - shift(x, 8))
    grad -= slope(jnp.where(time < TIMES - 1, weight, 0.0), shift(x, -8) - x)
    updated = x - (STEP * TV_SCALE) * grad

    rows = got_z.at[pl.ds(0, NZ - 1)]
    to_bl(rows, rows, rzs.at[0], rzr.at[0], other).wait_recv()
    total = got_z[0]
    for v in range(1, NZ):
        total = total + got_z[v]
    updated = updated + STEP * total
    upd_ref[...] = jnp.transpose(updated).reshape(8, TIMES, CHANNELS, 8)

    for edge in edges:
        edge.wait_send()

    def left(at):
        for sem, count in ((0, (3, 3, 3, 3, 3, 4, 5, 6)[at]), (1, (0, 4, 0, 16, 3, 2, 1, 0)[at])):
            if count:
                sent = part.at[pl.ds(0, count), 0, 0] if count <= NZ else part.at[pl.ds(0, count // NY), 0]
                to_bl(sent, sent, zs.at[sem], rzr.at[0], other).wait_send()

    for at in range(NZ):
        pl.when(z == at)(functools.partial(left, at))

    to_bl(rows, rows, rzs.at[0], rzr.at[0], other).wait_send()
    half = part.at[pl.ds(0, NZ), 0]
    to_bl(half, half, cs.at[0], rzr.at[0], other).wait_send()
    seven = part.at[pl.ds(0, NZ - DIRECT), 0]
    to_bl(seven, seven, rcs.at[0], rzr.at[0], other).wait_send()
    to_bl(got_0, got_0, r0s.at[0], rzr.at[0], other).wait_send()
    to_bl(got_y, got_y, ys.at[0], rzr.at[0], other).wait_send()
    most = got_y.at[pl.ds(0, NZ - DIRECT)]
    to_bl(most, most, rys.at[0], rzr.at[0], other).wait_send()


def hand_out(updated, residual, updated_h, residual_h, sem):
    copies = [
        pltpu.make_async_copy(residual, residual_h, sem.at[0]),
        pltpu.make_async_copy(updated, updated_h, sem.at[1]),
    ]
    for copy in copies:
        copy.start()
    for copy in copies:
        copy.wait()


def local(meas, model, imp, tally, one, two, gains, tvw):
    big = (8, TIMES, CHANNELS, PAIRS)
    vmem = pltpu.VMEM
    dma = pltpu.SemaphoreType.DMA
    flag = pltpu.SemaphoreType.REGULAR
    any_spec = pl.BlockSpec(memory_space=pl.ANY)
    vmem_spec = pl.BlockSpec(memory_space=pltpu.VMEM)
    updated, residual = pl.pallas_call(
        kernel,
        out_shape=(vmem((8, TIMES, CHANNELS, 8), F32), vmem(big, F32)),
        in_specs=[any_spec] * 8,
        out_specs=(vmem_spec, vmem_spec),
        scratch_shapes=[
            vmem(big, F32), vmem(big, F32), vmem((TIMES, CHANNELS, PAIRS), F32),
            vmem((1, PAIRS), jnp.int32), vmem((1, PAIRS), jnp.int32), vmem((1, PAIRS), jnp.int32),
            vmem((8, TIMES, CHANNELS, 8), F32), vmem((CHANNELS, 8), F32),
            vmem((NZ, NC, NY, 8, LANES), F32), vmem((NZ, NC, 32, PAIRS), BF16), vmem((NZ, NC, 32, PAIRS), BF16),
            vmem(big, F32), vmem(big, F32), vmem((NZ, NC, NY, 8, LANES), F32),
            vmem((DIRECT, 7, 8, LANES), F32), vmem((NZ, NY, 8, LANES), F32), vmem((NZ, NY - 1, 8, LANES), F32), vmem((NZ, 8, LANES), F32),
            vmem((8, 128), F32), vmem((2, 8, 128), F32),
            dma((8,)), dma((2,)), dma((NZ,)), dma((1,)), dma((2,)), dma((1,)), dma((2,)), dma((2,)), dma((2,)),
            dma((1,)), dma((DIRECT,)), dma((1,)), dma((NZ,)), dma((1,)), dma((NZ,)), dma((1,)), dma((1,)),
            flag((NZ,)), flag, flag, flag,
        ],
        compiler_params=pltpu.CompilerParams(
            collective_id=0, has_side_effects=True, vmem_limit_bytes=58 * 1024 * 1024
        ),
    )(meas, model, imp, tally, one.reshape(1, PAIRS), two.reshape(1, PAIRS), gains, tvw)
    held = [pltpu.with_memory_space_constraint(x, pltpu.VMEM) for x in (updated, residual)]
    return pl.pallas_call(
        hand_out,
        out_shape=(jax.ShapeDtypeStruct(updated.shape, F32), jax.ShapeDtypeStruct(residual.shape, F32)),
        in_specs=[vmem_spec, vmem_spec],
        out_specs=(any_spec, any_spec),
        scratch_shapes=[dma((2,))],
    )(*held)


def solution(mesh):
    placed = (
        P(None, None, "chan", "bl"),
        P(None, None, "chan", "bl"),
        P(None, "chan", "bl"),
        P("chan", "bl"),
        P("bl"),
        P("bl"),
        P(None, None, "chan", "bl"),
        P("chan", "bl"),
    )
    return jax.shard_map(
        local,
        mesh=mesh,
        in_specs=placed,
        out_specs=(P(None, None, "chan", "bl"), P(None, None, "chan", "bl")),
        check_vma=False,
    )
```

```python
import functools

import jax
import jax.numpy as jnp
from jax import lax
from jax.experimental import pallas as pl
from jax.experimental.pallas import tpu as pltpu
from jax.sharding import PartitionSpec as P

MESH = pl.DeviceIdType.MESH
STATIONS = 512
BASELINES = 32768
TIMES = 4
CHANNELS = 8
PAIRS = 512
LANES = 8 * TIMES * CHANNELS
NY, NZ, NC = 4, 8, 2
HALF = NZ // 2
DIRECT = 2
SMOOTH_EPS = 0.01
TV_SCALE = 2.0
STEP = 2.0 * STATIONS / BASELINES
F32 = jnp.float32
BF16 = jnp.bfloat16


def cmul_add(terms):
    real, imag = None, None
    for (ar, ai), (br, bi), conj in terms:
        if conj:
            r, i = ar * br + ai * bi, ai * br - ar * bi
        else:
            r, i = ar * br - ai * bi, ar * bi + ai * br
        real = r if real is None else real + r
        imag = i if imag is None else imag + i
    return real, imag


def halves(x):
    high = x.astype(BF16)
    return high, (x - high.astype(F32)).astype(BF16)


def split_index():
    bl = lax.axis_index("bl")
    return lax.div(bl, NZ * NC), lax.rem(lax.div(bl, NC), NZ), lax.rem(bl, NC)


def join_index(y, z, core):
    return (y * NZ + z) * NC + core


def kernel(
    meas_h, model_h, imp_h, tally_h, one_h, two_h, gains_h, tvw_h,
    upd_ref, res,
    meas, model, imp, tally, one, two, gains, tvw,
    table, hot1, hot2, gp, gq, part, got_0, got_c, got_y, got_z, halo, halo_got,
    in_sem, zs, zr, ys, yr, cs, cr, hs, hr, r0s, r0r, rcs, rcr, rys, ryr, rzs, rzr,
    ready_z, ready_y, ready_c, hub,
):
    chan = lax.axis_index("chan")
    n_chan = lax.axis_size("chan")
    odd = lax.rem(chan, 2)
    y, z, core = split_index()
    early = odd == 0
    chan_peers = [lax.rem(chan + 1, n_chan), lax.rem(chan + n_chan - 1, n_chan)]

    def to_bl(src, dst, send, recv, peer):
        return pltpu.make_async_remote_copy(
            src_ref=src, dst_ref=dst, send_sem=send, recv_sem=recv,
            device_id={"bl": peer}, device_id_type=MESH,
        )

    def z_peer(to):
        return join_index(y, to, core)

    def y_peer(k):
        to = lax.rem(y + k, NY)
        return join_index(to, z, core), to

    other = join_index(y, z, 1 - core)

    loads = [
        pltpu.make_async_copy(src, dst, in_sem.at[i])
        for i, (src, dst) in enumerate(
            [(gains_h, gains), (one_h, one), (two_h, two), (tvw_h, tvw), (tally_h, tally),
             (imp_h, imp), (meas_h, meas), (model_h, model)]
        )
    ]
    loads[0].start()
    barrier = pltpu.get_barrier_semaphore()

    second = lax.rem(y + core, 2)
    upper = lax.div(z, HALF)
    beside = [y_peer(1)[0], y_peer(3)[0], other]

    def tell_beside(sem):
        for peer in beside:
            pl.semaphore_signal(sem, inc=1, device_id={"bl": peer}, device_id_type=MESH)

    def announce(to, carry):
        pl.semaphore_signal(barrier, inc=1, device_id={"bl": z_peer(to)}, device_id_type=MESH)
        return carry

    lax.fori_loop(0, (1 - upper) * z, announce, 0)
    lax.fori_loop(jnp.where(z == 0, NZ, jnp.maximum(z + 1, HALF)), NZ, announce, 0)
    pl.when((upper == 0) & (second == 0))(lambda: tell_beside(barrier))

    @pl.when((upper == 1) & (core == 0))
    def _():
        pl.semaphore_signal(barrier, inc=1, device_id={"bl": other}, device_id_type=MESH)

    @pl.when(early)
    def _():
        for peer in chan_peers:
            pl.semaphore_signal(barrier, inc=1, device_id={"chan": peer}, device_id_type=MESH)

    earlier = upper * (z - 1) + (1 - upper) * (HALF - 1 - z) + (1 - upper) * 3 * second + upper * core + 2 * odd

    @pl.when(earlier > 0)
    def _():
        pl.semaphore_wait(barrier, earlier)

    def tell_z(to, carry):
        pl.semaphore_signal(ready_z.at[z], inc=1, device_id={"bl": z_peer(to)}, device_id_type=MESH)
        return carry

    lax.fori_loop(HALF - 1, z, tell_z, 0)
    pl.when((upper == 0) & (second == 1))(lambda: tell_beside(ready_y))

    @pl.when((upper == 1) & (core == 1))
    def _():
        pl.semaphore_signal(ready_c, inc=1, device_id={"bl": other}, device_id_type=MESH)

    loads[0].wait()
    own = jnp.transpose(gains[...].reshape(LANES, 8))
    table[z, core, y] = own

    mine = table.at[z, core, y]

    def send_own(to, carry):
        to_bl(mine, mine, zs.at[0], zr.at[z], z_peer(to)).start()
        return carry

    lax.fori_loop(1 + (1 - upper) * z, upper * z + (1 - upper) * HALF, send_own, 0)
    for load in loads[1:]:
        load.start()

    @pl.when((upper == 0) & (second == 0))
    def _():
        pl.semaphore_wait(ready_y, 3)
        tell_beside(ready_y)


    loads[3].wait()
    lane = lax.broadcasted_iota(jnp.int32, (8, LANES), 1)
    freq, time = lane & 7, lax.shift_right_logical(lane, 3) & 3
    weight = jnp.transpose(
        jnp.broadcast_to(tvw[...][None], (8 * TIMES, CHANNELS, 8)).reshape(LANES, 8)
    )
    low, high = own[:, :128], own[:, 128:]
    freq_h = freq[:, :128]
    halo[...] = jnp.where(
        freq_h == 0, low,
        jnp.where(
            freq_h == 1, pltpu.roll(high, 1, 1),
            jnp.where(
                freq_h == 7, low,
                jnp.where(freq_h == 6, pltpu.roll(high, 127, 1), pltpu.roll(weight[:, :128], 2, 1)),
            ),
        ),
    )
    edges = [
        pltpu.make_async_remote_copy(
            src_ref=halo, dst_ref=halo_got.at[k], send_sem=hs.at[k], recv_sem=hr.at[k],
            device_id={"chan": peer}, device_id_type=MESH,
        )
        for k, peer in enumerate(chan_peers)
    ]

    @pl.when(jnp.logical_not(early))
    def _():
        for edge in edges:
            edge.start()

    loads[1].wait()
    loads[2].wait()

    def to_row(ant):
        return (
            (lax.shift_right_logical(ant, 4) & 7) * 64 + (lax.shift_right_logical(ant, 3) & 1) * 32
            + lax.shift_right_logical(ant, 7) * 8 + (ant & 7)
        )

    row1, row2 = to_row(one[...]), to_row(two[...])

    def hot_body(i, carry):
        index = lax.broadcasted_iota(jnp.int32, (32, PAIRS), 0) + i * 32
        v, half = lax.div(i, NC), lax.rem(i, NC)
        hot1[v, half] = jnp.where(index == row1, 1.0, 0.0).astype(BF16)
        hot2[v, half] = jnp.where(index == row2, 1.0, 0.0).astype(BF16)
        return carry

    lax.fori_loop(0, 16, hot_body, 0)

    loads[4].wait()
    loads[5].wait()
    keep = lax.broadcasted_iota(jnp.int32, (CHANNELS, PAIRS), 0) < CHANNELS - tally[...]
    for t in range(TIMES):
        imp[t] = jnp.where(keep, imp[t], 0.0)
    loads[6].wait()
    loads[7].wait()

    def pieces(v, count):
        return table.at[v, core, y] if count == 1 else table.at[pl.ds(v, count), core, y]

    def send_up(to, v, count):
        pl.semaphore_wait(ready_z.at[to], 1)
        rows = pieces(v, count)
        to_bl(rows, rows, zs.at[1], zr.at[v], z_peer(to)).start()

    def wait_for(v, count=1):
        rows = pieces(v, count)
        to_bl(rows, rows, zs.at[1], zr.at[v], other).wait_recv()

    def pass_on(v, count=1):
        rows = pieces(v, count)
        for k in (2, 1, 3):
            to_bl(rows, rows, ys.at[0], yr.at[v // HALF], y_peer(k)[0]).start()

    def take_in(v, count=1):
        wait_for(v, count)
        pass_on(v, count)

    def share(half):
        three = table.at[pl.ds(half * HALF, HALF), core, pl.ds(0, 3)]
        to_bl(three, three, ys.at[0], yr.at[half], other).wait_recv()
        four = table.at[pl.ds(half * HALF, HALF), core]
        to_bl(four, four, cs.at[0], cr.at[half], other).start()

    def pick(half, first):
        flipped = jnp.transpose(table[:, half].reshape(256, LANES))
        g_high, g_low = halves(flipped)
        for hot, dst in ((hot1, gp), (hot2, gq)):
            rows = hot[:, half].reshape(256, PAIRS)
            picked = jnp.dot(g_high, rows, preferred_element_type=F32) + jnp.dot(
                g_low, rows, preferred_element_type=F32
            )
            picked = picked.reshape(8, TIMES, CHANNELS, PAIRS)
            dst[...] = picked if first else dst[...] + picked

    def tell_plane():
        pl.semaphore_wait(hub, NY - 1)
        pl.semaphore_signal(ready_y, inc=1, device_id={"bl": z_peer(HALF)}, device_id_type=MESH)

    def line(at):
        for to in range(at + 1, NZ) if at >= HALF else ():
            send_up(to, at, 1)
        if at < HALF:

            @pl.when(second == 1)
            def _():
                pl.semaphore_wait(ready_y, 3)

        else:
            pl.semaphore_wait(ready_y, 1)
        if at == HALF - 1:
            pl.semaphore_wait(ready_z.at[HALF], 1)
        if at in (HALF - 1, HALF):
            for k in (2, 1, 3):
                pl.semaphore_signal(hub, inc=1, device_id={"bl": y_peer(k)[0]}, device_id_type=MESH)
        if at == HALF:
            pl.semaphore_wait(hub, NY - 1)
            for to in (7, 6, 5):
                pl.semaphore_signal(ready_y, inc=1, device_id={"bl": z_peer(to)}, device_id_type=MESH)
        pass_on(at)
        if at < HALF:
            for v in (3, 2, 1, 0):
                if at == HALF - 1 and v == 0:
                    pl.when(early)(tell_plane)
                if v != at:
                    take_in(v)
                if v < at:
                    send_own(v, 0)
            if at == HALF - 1:
                pl.when(jnp.logical_not(early))(tell_plane)
                lower = pieces(0, HALF)
                to_bl(lower, lower, zs.at[1], zr.at[0], z_peer(HALF)).start()
                for to in (5, 6, 7):
                    send_up(to, 0, HALF)
            for v in range(HALF, NZ):
                take_in(v)
                if at == 1:
                    piece = pieces(v, 1)
                    to_bl(piece, piece, zs.at[1], zr.at[v], z_peer(0)).start()
        else:
            for v in range(HALF, NZ):
                if v != at:
                    take_in(v)
            take_in(0, HALF)

    for at in range(NZ):
        pl.when(z == at)(functools.partial(line, at))

    @pl.when((upper == 1) & (core == 0))
    def _():
        pl.semaphore_wait(ready_c, 1)

    share(upper)
    share(1 - upper)
    pick(core, True)
    for half in range(2):
        four = table.at[pl.ds(half * HALF, HALF), 1 - core]
        to_bl(four, four, cs.at[0], cr.at[half], other).wait_recv()
    pick(1 - core, False)

    def compute(i, carry):
        t = lax.div(i, 4)
        at = pl.ds(pl.multiple_of(lax.rem(i, 4) * 128, 128), 128)

        def matrix(ref):
            return [(ref[c, t, :, at], ref[c + 4, t, :, at]) for c in range(4)]

        jp, jq, m, d = matrix(gp), matrix(gq), matrix(model), matrix(meas)
        w = imp[t, :, at]
        a = [
            cmul_add([(jp[2 * r], m[c], False), (jp[2 * r + 1], m[c + 2], False)])
            for r in range(2) for c in range(2)
        ]
        v = [
            cmul_add([(a[2 * r], jq[2 * c], True), (a[2 * r + 1], jq[2 * c + 1], True)])
            for r in range(2) for c in range(2)
        ]
        e = [(w * (d[k][0] - v[k][0]), w * (d[k][1] - v[k][1])) for k in range(4)]
        for k in range(4):
            res[k, t, :, at] = e[k][0]
            res[k + 4, t, :, at] = e[k][1]
        b = [
            cmul_add([(jq[2 * r], m[2 * c], True), (jq[2 * r + 1], m[2 * c + 1], True)])
            for r in range(2) for c in range(2)
        ]
        first = [
            cmul_add([(e[2 * r], b[c], False), (e[2 * r + 1], b[c + 2], False)])
            for r in range(2) for c in range(2)
        ]
        second = [
            cmul_add([(a[c], e[r], True), (a[c + 2], e[r + 2], True)])
            for r in range(2) for c in range(2)
        ]
        for k in range(4):
            gp[k, t, :, at] = first[k][0]
            gp[k + 4, t, :, at] = first[k][1]
            gq[k, t, :, at] = second[k][0]
            gq[k + 4, t, :, at] = second[k][1]
        return carry

    lax.fori_loop(0, 16, compute, 0, unroll=2)

    p_high, p_low = halves(gp[...].reshape(LANES, PAIRS))
    q_high, q_low = halves(gq[...].reshape(LANES, PAIRS))
    nt = (((1,), (1,)), ((), ()))

    def add_up(places):
        h1, h2 = (
            jnp.concatenate([hot[v].reshape(64, PAIRS) for v in places]) for hot in (hot1, hot2)
        )
        total = lax.dot_general(h1, p_high, nt, preferred_element_type=F32)
        total += lax.dot_general(h1, p_low, nt, preferred_element_type=F32)
        total += lax.dot_general(h2, q_high, nt, preferred_element_type=F32)
        total += lax.dot_general(h2, q_low, nt, preferred_element_type=F32)
        for i, v in enumerate(places):
            part[v] = total[i * 64 : i * 64 + 64].reshape(NC, NY, 8, LANES)

    def from_end(v):
        if isinstance(v, int):
            return v + odd * ((v // 2 if v % 2 else NZ - 1 - v // 2) - v)
        far = lax.rem(v, 2)
        return v + odd * (lax.div(v, 2) * (2 * far - 1) + (1 - far) * (NZ - 1) - v)

    def hand_over(step, carry):
        v = from_end(step)
        to_bl(part.at[v, 1 - core], got_c.at[v], rcs.at[0], rcr.at[v], other).start()
        return carry

    def along_y(step, carry):
        v = from_end(step)
        got = got_c.at[v]
        to_bl(got, got, rcs.at[0], rcr.at[v], other).wait_recv()
        part[v, core] = part[v, core] + got_c[v]
        for k in (2, 1, 3):
            peer, to = y_peer(k)
            to_bl(part.at[v, core, to], got_y.at[v, k - 1], rys.at[0], ryr.at[v], peer).start()
        return carry

    def send_on(v):
        @pl.when(v != z)
        def _():
            to_bl(part.at[v, core, y], got_z.at[z], rzs.at[0], rzr.at[0], z_peer(v)).start()

    def along_z(step, carry):
        v = from_end(step)
        got = got_y.at[v]
        to_bl(got, got, rys.at[0], ryr.at[v], other).wait_recv()
        part[v, core, y] = part[v, core, y] + got_y[v, 0] + (got_y[v, 1] + got_y[v, 2])
        send_on(v)
        return carry

    add_up([from_end(v) for v in range(DIRECT)])
    for v in range(DIRECT):
        at_v = from_end(v)
        for slot, (dy, dc) in enumerate(((2, 0), (2, 1), (1, 0), (1, 1), (3, 0), (3, 1), (0, 1))):
            to_y, to_core = lax.rem(y + dy, NY), lax.rem(core + dc, NC)
            to_bl(
                part.at[at_v, to_core, to_y], got_0.at[v, slot], r0s.at[0], r0r.at[v],
                join_index(to_y, z, to_core),
            ).start()
    add_up([DIRECT - odd + v for v in range(NZ - DIRECT)])
    lax.fori_loop(DIRECT, NZ, hand_over, 0)
    lax.fori_loop(DIRECT, NZ, along_y, 0)
    for v in range(DIRECT):
        got = got_0.at[v]
        to_bl(got, got, r0s.at[0], r0r.at[v], other).wait_recv()
        at_v = from_end(v)
        total = part[at_v, core, y]
        for slot in range(7):
            total = total + got_0[v, slot]
        part[at_v, core, y] = total
        send_on(at_v)
    lax.fori_loop(DIRECT, NZ, along_z, 0)
    got_z[z] = part[z, core, y]

    for edge in edges:
        edge.wait_recv()

    @pl.when(early)
    def _():
        for edge in edges:
            edge.start()

    from_prev, from_next = halo_got[0], halo_got[1]
    x = own

    def shift(v, by):
        return pltpu.roll(v, by % LANES, 1)

    prev_edge = jnp.concatenate([pltpu.roll(from_prev, 121, 1), pltpu.roll(from_prev, 122, 1)], axis=1)
    next_edge = jnp.concatenate([pltpu.roll(from_next, 7, 1), pltpu.roll(from_next, 6, 1)], axis=1)
    next_weight = jnp.concatenate([pltpu.roll(from_next, 5, 1)] * 2, axis=1)
    is_first, is_last = freq == 0, freq == CHANNELS - 1
    not_low = jnp.where(chan > 0, 1.0, 0.0).astype(F32)
    not_high = jnp.where(chan < n_chan - 1, 1.0, 0.0).astype(F32)

    def slope(w, step):
        square = step * step
        for by in (128, 64, 32):
            square = square + shift(square, by)
        return w * step / jnp.sqrt(square + SMOOTH_EPS)

    grad = slope(
        jnp.where(is_first, weight * not_low, weight), x - jnp.where(is_first, prev_edge, shift(x, 1))
    )
    grad -= slope(
        jnp.where(is_last, next_weight * not_high, shift(weight, -1)),
        jnp.where(is_last, next_edge, shift(x, -1)) - x,
    )
    grad += slope(jnp.where(time > 0, weight, 0.0), x - shift(x, 8))
    grad -= slope(jnp.where(time < TIMES - 1, weight, 0.0), shift(x, -8) - x)
    updated = x - (STEP * TV_SCALE) * grad

    rows = got_z.at[pl.ds(0, NZ - 1)]
    to_bl(rows, rows, rzs.at[0], rzr.at[0], other).wait_recv()
    total = got_z[0]
    for v in range(1, NZ):
        total = total + got_z[v]
    updated = updated + STEP * total
    upd_ref[...] = jnp.transpose(updated).reshape(8, TIMES, CHANNELS, 8)

    for edge in edges:
        edge.wait_send()

    def left(at):
        for sem, count in ((0, (3, 3, 3, 3, 3, 4, 5, 6)[at]), (1, (0, 4, 0, 16, 3, 2, 1, 0)[at])):
            if count:
                sent = part.at[pl.ds(0, count), 0, 0] if count <= NZ else part.at[pl.ds(0, count // NY), 0]
                to_bl(sent, sent, zs.at[sem], rzr.at[0], other).wait_send()

    for at in range(NZ):
        pl.when(z == at)(functools.partial(left, at))

    to_bl(rows, rows, rzs.at[0], rzr.at[0], other).wait_send()
    half = part.at[pl.ds(0, NZ), 0]
    to_bl(half, half, cs.at[0], rzr.at[0], other).wait_send()
    seven = part.at[pl.ds(0, NZ - DIRECT), 0]
    to_bl(seven, seven, rcs.at[0], rzr.at[0], other).wait_send()
    to_bl(got_0, got_0, r0s.at[0], rzr.at[0], other).wait_send()
    to_bl(got_y, got_y, ys.at[0], rzr.at[0], other).wait_send()
    most = got_y.at[pl.ds(0, NZ - DIRECT)]
    to_bl(most, most, rys.at[0], rzr.at[0], other).wait_send()


def hand_out(updated, residual, updated_h, residual_h, sem):
    copies = [
        pltpu.make_async_copy(residual, residual_h, sem.at[0]),
        pltpu.make_async_copy(updated, updated_h, sem.at[1]),
    ]
    for copy in copies:
        copy.start()
    for copy in copies:
        copy.wait()


def local(meas, model, imp, tally, one, two, gains, tvw):
    big = (8, TIMES, CHANNELS, PAIRS)
    vmem = pltpu.VMEM
    dma = pltpu.SemaphoreType.DMA
    flag = pltpu.SemaphoreType.REGULAR
    any_spec = pl.BlockSpec(memory_space=pl.ANY)
    vmem_spec = pl.BlockSpec(memory_space=pltpu.VMEM)
    updated, residual = pl.pallas_call(
        kernel,
        out_shape=(vmem((8, TIMES, CHANNELS, 8), F32), vmem(big, F32)),
        in_specs=[any_spec] * 8,
        out_specs=(vmem_spec, vmem_spec),
        scratch_shapes=[
            vmem(big, F32), vmem(big, F32), vmem((TIMES, CHANNELS, PAIRS), F32),
            vmem((1, PAIRS), jnp.int32), vmem((1, PAIRS), jnp.int32), vmem((1, PAIRS), jnp.int32),
            vmem((8, TIMES, CHANNELS, 8), F32), vmem((CHANNELS, 8), F32),
            vmem((NZ, NC, NY, 8, LANES), F32), vmem((NZ, NC, 32, PAIRS), BF16), vmem((NZ, NC, 32, PAIRS), BF16),
            vmem(big, F32), vmem(big, F32), vmem((NZ, NC, NY, 8, LANES), F32),
            vmem((DIRECT, 7, 8, LANES), F32), vmem((NZ, NY, 8, LANES), F32), vmem((NZ, NY - 1, 8, LANES), F32), vmem((NZ, 8, LANES), F32),
            vmem((8, 128), F32), vmem((2, 8, 128), F32),
            dma((8,)), dma((2,)), dma((NZ,)), dma((1,)), dma((2,)), dma((1,)), dma((2,)), dma((2,)), dma((2,)),
            dma((1,)), dma((DIRECT,)), dma((1,)), dma((NZ,)), dma((1,)), dma((NZ,)), dma((1,)), dma((1,)),
            flag((NZ,)), flag, flag, flag,
        ],
        compiler_params=pltpu.CompilerParams(
            collective_id=0, has_side_effects=True, vmem_limit_bytes=58 * 1024 * 1024
        ),
    )(meas, model, imp, tally, one.reshape(1, PAIRS), two.reshape(1, PAIRS), gains, tvw)
    held = [pltpu.with_memory_space_constraint(x, pltpu.VMEM) for x in (updated, residual)]
    return pl.pallas_call(
        hand_out,
        out_shape=(jax.ShapeDtypeStruct(updated.shape, F32), jax.ShapeDtypeStruct(residual.shape, F32)),
        in_specs=[vmem_spec, vmem_spec],
        out_specs=(any_spec, any_spec),
        scratch_shapes=[dma((2,))],
    )(*held)


def solution(mesh):
    placed = (
        P(None, None, "chan", "bl"),
        P(None, None, "chan", "bl"),
        P(None, "chan", "bl"),
        P("chan", "bl"),
        P("bl"),
        P("bl"),
        P(None, None, "chan", "bl"),
        P("chan", "bl"),
    )
    return jax.shard_map(
        local,
        mesh=mesh,
        in_specs=placed,
        out_specs=(P(None, None, "chan", "bl"), P(None, None, "chan", "bl")),
        check_vma=False,
    )
```

```python
import functools

import jax
import jax.numpy as jnp
from jax import lax
from jax.experimental import pallas as pl
from jax.experimental.pallas import tpu as pltpu
from jax.sharding import PartitionSpec as P

MESH = pl.DeviceIdType.MESH
STATIONS = 512
BASELINES = 32768
TIMES = 4
CHANNELS = 8
PAIRS = 512
LANES = 8 * TIMES * CHANNELS
NY, NZ, NC = 4, 8, 2
HALF = NZ // 2
DIRECT = 2
SMOOTH_EPS = 0.01
TV_SCALE = 2.0
STEP = 2.0 * STATIONS / BASELINES
F32 = jnp.float32
BF16 = jnp.bfloat16


def cmul_add(terms):
    real, imag = None, None
    for (ar, ai), (br, bi), conj in terms:
        if conj:
            r, i = ar * br + ai * bi, ai * br - ar * bi
        else:
            r, i = ar * br - ai * bi, ar * bi + ai * br
        real = r if real is None else real + r
        imag = i if imag is None else imag + i
    return real, imag


def halves(x):
    high = x.astype(BF16)
    return high, (x - high.astype(F32)).astype(BF16)


def split_index():
    bl = lax.axis_index("bl")
    return lax.div(bl, NZ * NC), lax.rem(lax.div(bl, NC), NZ), lax.rem(bl, NC)


def join_index(y, z, core):
    return (y * NZ + z) * NC + core


def kernel(
    meas_h, model_h, imp_h, tally_h, one_h, two_h, gains_h, tvw_h,
    upd_ref, res,
    meas, model, imp, tally, one, two, gains, tvw,
    table, hot1, hot2, gp, gq, part, got_0, got_c, got_y, got_z, halo, halo_got,
    in_sem, zs, zr, ys, yr, cs, cr, hs, hr, r0s, r0r, rcs, rcr, rys, ryr, rzs, rzr,
    ready_z, ready_y, ready_c, hub,
):
    chan = lax.axis_index("chan")
    n_chan = lax.axis_size("chan")
    odd = lax.rem(chan, 2)
    y, z, core = split_index()
    early = odd == 0
    chan_peers = [lax.rem(chan + 1, n_chan), lax.rem(chan + n_chan - 1, n_chan)]

    def to_bl(src, dst, send, recv, peer):
        return pltpu.make_async_remote_copy(
            src_ref=src, dst_ref=dst, send_sem=send, recv_sem=recv,
            device_id={"bl": peer}, device_id_type=MESH,
        )

    def z_peer(to):
        return join_index(y, to, core)

    def y_peer(k):
        to = lax.rem(y + k, NY)
        return join_index(to, z, core), to

    other = join_index(y, z, 1 - core)

    loads = [
        pltpu.make_async_copy(src, dst, in_sem.at[i])
        for i, (src, dst) in enumerate(
            [(gains_h, gains), (one_h, one), (two_h, two), (tvw_h, tvw), (tally_h, tally),
             (imp_h, imp), (meas_h, meas), (model_h, model)]
        )
    ]
    loads[0].start()
    barrier = pltpu.get_barrier_semaphore()

    second = lax.rem(y + core, 2)
    upper = lax.div(z, HALF)
    beside = [y_peer(1)[0], y_peer(3)[0], other]

    def tell_beside(sem):
        for peer in beside:
            pl.semaphore_signal(sem, inc=1, device_id={"bl": peer}, device_id_type=MESH)

    def announce(to, carry):
        pl.semaphore_signal(barrier, inc=1, device_id={"bl": z_peer(to)}, device_id_type=MESH)
        return carry

    lax.fori_loop(0, (1 - upper) * z, announce, 0)
    lax.fori_loop(jnp.where(z == 0, NZ, jnp.maximum(z + 1, HALF)), NZ, announce, 0)
    pl.when((upper == 0) & (second == 0))(lambda: tell_beside(barrier))

    @pl.when((upper == 1) & (core == 0))
    def _():
        pl.semaphore_signal(barrier, inc=1, device_id={"bl": other}, device_id_type=MESH)

    @pl.when(early)
    def _():
        for peer in chan_peers:
            pl.semaphore_signal(barrier, inc=1, device_id={"chan": peer}, device_id_type=MESH)

    earlier = upper * (z - 1) + (1 - upper) * (HALF - 1 - z) + (1 - upper) * 3 * second + upper * core + 2 * odd

    @pl.when(earlier > 0)
    def _():
        pl.semaphore_wait(barrier, earlier)

    def tell_z(to, carry):
        pl.semaphore_signal(ready_z.at[z], inc=1, device_id={"bl": z_peer(to)}, device_id_type=MESH)
        return carry

    lax.fori_loop(HALF - 1, z, tell_z, 0)
    pl.when((upper == 0) & (second == 1))(lambda: tell_beside(ready_y))

    @pl.when((upper == 1) & (core == 1))
    def _():
        pl.semaphore_signal(ready_c, inc=1, device_id={"bl": other}, device_id_type=MESH)

    loads[0].wait()
    own = jnp.transpose(gains[...].reshape(LANES, 8))
    table[z, core, y] = own

    mine = table.at[z, core, y]

    def send_own(to, carry):
        to_bl(mine, mine, zs.at[0], zr.at[z], z_peer(to)).start()
        return carry

    lax.fori_loop(1 + (1 - upper) * z, upper * z + (1 - upper) * HALF, send_own, 0)
    for load in loads[1:]:
        load.start()

    @pl.when((upper == 0) & (second == 0))
    def _():
        pl.semaphore_wait(ready_y, 3)
        tell_beside(ready_y)


    loads[3].wait()
    lane = lax.broadcasted_iota(jnp.int32, (8, LANES), 1)
    freq, time = lane & 7, lax.shift_right_logical(lane, 3) & 3
    weight = jnp.transpose(
        jnp.broadcast_to(tvw[...][None], (8 * TIMES, CHANNELS, 8)).reshape(LANES, 8)
    )
    low, high = own[:, :128], own[:, 128:]
    freq_h = freq[:, :128]
    halo[...] = jnp.where(
        freq_h == 0, low,
        jnp.where(
            freq_h == 1, pltpu.roll(high, 1, 1),
            jnp.where(
                freq_h == 7, low,
                jnp.where(freq_h == 6, pltpu.roll(high, 127, 1), pltpu.roll(weight[:, :128], 2, 1)),
            ),
        ),
    )
    edges = [
        pltpu.make_async_remote_copy(
            src_ref=halo, dst_ref=halo_got.at[k], send_sem=hs.at[k], recv_sem=hr.at[k],
            device_id={"chan": peer}, device_id_type=MESH,
        )
        for k, peer in enumerate(chan_peers)
    ]

    @pl.when(jnp.logical_not(early))
    def _():
        for edge in edges:
            edge.start()

    loads[1].wait()
    loads[2].wait()

    def to_row(ant):
        return (
            (lax.shift_right_logical(ant, 4) & 7) * 64 + (lax.shift_right_logical(ant, 3) & 1) * 32
            + lax.shift_right_logical(ant, 7) * 8 + (ant & 7)
        )

    row1, row2 = to_row(one[...]), to_row(two[...])

    def hot_body(i, carry):
        index = lax.broadcasted_iota(jnp.int32, (32, PAIRS), 0) + i * 32
        v, half = lax.div(i, NC), lax.rem(i, NC)
        hot1[v, half] = jnp.where(index == row1, 1.0, 0.0).astype(BF16)
        hot2[v, half] = jnp.where(index == row2, 1.0, 0.0).astype(BF16)
        return carry

    lax.fori_loop(0, 16, hot_body, 0)

    loads[4].wait()
    loads[5].wait()
    keep = lax.broadcasted_iota(jnp.int32, (CHANNELS, PAIRS), 0) < CHANNELS - tally[...]
    for t in range(TIMES):
        imp[t] = jnp.where(keep, imp[t], 0.0)
    def pieces(v, count):
        return table.at[v, core, y] if count == 1 else table.at[pl.ds(v, count), core, y]

    def send_up(to, v, count):
        pl.semaphore_wait(ready_z.at[to], 1)
        rows = pieces(v, count)
        to_bl(rows, rows, zs.at[1], zr.at[v], z_peer(to)).start()

    def wait_for(v, count=1):
        rows = pieces(v, count)
        to_bl(rows, rows, zs.at[1], zr.at[v], other).wait_recv()

    def pass_on(v, count=1):
        rows = pieces(v, count)
        for k in (2, 1, 3):
            to_bl(rows, rows, ys.at[0], yr.at[v // HALF], y_peer(k)[0]).start()

    def take_in(v, count=1):
        wait_for(v, count)
        pass_on(v, count)

    def share(half):
        three = table.at[pl.ds(half * HALF, HALF), core, pl.ds(0, 3)]
        to_bl(three, three, ys.at[0], yr.at[half], other).wait_recv()
        four = table.at[pl.ds(half * HALF, HALF), core]
        to_bl(four, four, cs.at[0], cr.at[half], other).start()

    def pick(half, first):
        flipped = jnp.transpose(table[:, half].reshape(256, LANES))
        g_high, g_low = halves(flipped)
        for hot, dst in ((hot1, gp), (hot2, gq)):
            rows = hot[:, half].reshape(256, PAIRS)
            picked = jnp.dot(g_high, rows, preferred_element_type=F32) + jnp.dot(
                g_low, rows, preferred_element_type=F32
            )
            picked = picked.reshape(8, TIMES, CHANNELS, PAIRS)
            dst[...] = picked if first else dst[...] + picked

    def tell_plane():
        pl.semaphore_wait(hub, NY - 1)
        pl.semaphore_signal(ready_y, inc=1, device_id={"bl": z_peer(HALF)}, device_id_type=MESH)

    def line(at):
        for to in range(at + 1, NZ) if at >= HALF else ():
            send_up(to, at, 1)
        if at < HALF:

            @pl.when(second == 1)
            def _():
                pl.semaphore_wait(ready_y, 3)

        else:
            pl.semaphore_wait(ready_y, 1)
        if at == HALF - 1:
            pl.semaphore_wait(ready_z.at[HALF], 1)
        if at in (HALF - 1, HALF):
            for k in (2, 1, 3):
                pl.semaphore_signal(hub, inc=1, device_id={"bl": y_peer(k)[0]}, device_id_type=MESH)
        if at == HALF:
            pl.semaphore_wait(hub, NY - 1)
            for to in (7, 6, 5):
                pl.semaphore_signal(ready_y, inc=1, device_id={"bl": z_peer(to)}, device_id_type=MESH)
        pass_on(at)
        if at < HALF:
            for v in (3, 2, 1, 0):
                if at == HALF - 1 and v == 0:
                    pl.when(early)(tell_plane)
                if v != at:
                    take_in(v)
                if v < at:
                    send_own(v, 0)
            if at == HALF - 1:
                pl.when(jnp.logical_not(early))(tell_plane)
                lower = pieces(0, HALF)
                to_bl(lower, lower, zs.at[1], zr.at[0], z_peer(HALF)).start()
                for to in (5, 6, 7):
                    send_up(to, 0, HALF)
            for v in range(HALF, NZ):
                take_in(v)
                if at == 1:
                    piece = pieces(v, 1)
                    to_bl(piece, piece, zs.at[1], zr.at[v], z_peer(0)).start()
        else:
            for v in range(HALF, NZ):
                if v != at:
                    take_in(v)
            take_in(0, HALF)

    for at in range(NZ):
        pl.when(z == at)(functools.partial(line, at))

    @pl.when((upper == 1) & (core == 0))
    def _():
        pl.semaphore_wait(ready_c, 1)

    share(upper)
    share(1 - upper)
    pick(core, True)
    for half in range(2):
        four = table.at[pl.ds(half * HALF, HALF), 1 - core]
        to_bl(four, four, cs.at[0], cr.at[half], other).wait_recv()
    pick(1 - core, False)

    def compute(i, carry):
        t = lax.div(i, 4)
        at = pl.ds(pl.multiple_of(lax.rem(i, 4) * 128, 128), 128)

        def matrix(ref):
            return [(ref[c, t, :, at], ref[c + 4, t, :, at]) for c in range(4)]

        jp, jq, m, d = matrix(gp), matrix(gq), matrix(model), matrix(meas)
        w = imp[t, :, at]
        a = [
            cmul_add([(jp[2 * r], m[c], False), (jp[2 * r + 1], m[c + 2], False)])
            for r in range(2) for c in range(2)
        ]
        v = [
            cmul_add([(a[2 * r], jq[2 * c], True), (a[2 * r + 1], jq[2 * c + 1], True)])
            for r in range(2) for c in range(2)
        ]
        e = [(w * (d[k][0] - v[k][0]), w * (d[k][1] - v[k][1])) for k in range(4)]
        for k in range(4):
            res[k, t, :, at] = e[k][0]
            res[k + 4, t, :, at] = e[k][1]
        b = [
            cmul_add([(jq[2 * r], m[2 * c], True), (jq[2 * r + 1], m[2 * c + 1], True)])
            for r in range(2) for c in range(2)
        ]
        first = [
            cmul_add([(e[2 * r], b[c], False), (e[2 * r + 1], b[c + 2], False)])
            for r in range(2) for c in range(2)
        ]
        second = [
            cmul_add([(a[c], e[r], True), (a[c + 2], e[r + 2], True)])
            for r in range(2) for c in range(2)
        ]
        for k in range(4):
            gp[k, t, :, at] = first[k][0]
            gp[k + 4, t, :, at] = first[k][1]
            gq[k, t, :, at] = second[k][0]
            gq[k + 4, t, :, at] = second[k][1]
        return carry

    loads[6].wait()
    loads[7].wait()
    lax.fori_loop(0, 16, compute, 0, unroll=2)

    p_high, p_low = halves(gp[...].reshape(LANES, PAIRS))
    q_high, q_low = halves(gq[...].reshape(LANES, PAIRS))
    nt = (((1,), (1,)), ((), ()))

    def add_up(places):
        h1, h2 = (
            jnp.concatenate([hot[v].reshape(64, PAIRS) for v in places]) for hot in (hot1, hot2)
        )
        total = lax.dot_general(h1, p_high, nt, preferred_element_type=F32)
        total += lax.dot_general(h1, p_low, nt, preferred_element_type=F32)
        total += lax.dot_general(h2, q_high, nt, preferred_element_type=F32)
        total += lax.dot_general(h2, q_low, nt, preferred_element_type=F32)
        for i, v in enumerate(places):
            part[v] = total[i * 64 : i * 64 + 64].reshape(NC, NY, 8, LANES)

    def from_end(v):
        if isinstance(v, int):
            return v + odd * ((v // 2 if v % 2 else NZ - 1 - v // 2) - v)
        far = lax.rem(v, 2)
        return v + odd * (lax.div(v, 2) * (2 * far - 1) + (1 - far) * (NZ - 1) - v)

    def hand_over(step, carry):
        v = from_end(step)
        to_bl(part.at[v, 1 - core], got_c.at[v], rcs.at[0], rcr.at[v], other).start()
        return carry

    def along_y(step, carry):
        v = from_end(step)
        got = got_c.at[v]
        to_bl(got, got, rcs.at[0], rcr.at[v], other).wait_recv()
        part[v, core] = part[v, core] + got_c[v]
        for k in (2, 1, 3):
            peer, to = y_peer(k)
            to_bl(part.at[v, core, to], got_y.at[v, k - 1], rys.at[0], ryr.at[v], peer).start()
        return carry

    def send_on(v):
        @pl.when(v != z)
        def _():
            to_bl(part.at[v, core, y], got_z.at[z], rzs.at[0], rzr.at[0], z_peer(v)).start()

    def along_z(step, carry):
        v = from_end(step)
        got = got_y.at[v]
        to_bl(got, got, rys.at[0], ryr.at[v], other).wait_recv()
        part[v, core, y] = part[v, core, y] + got_y[v, 0] + (got_y[v, 1] + got_y[v, 2])
        send_on(v)
        return carry

    add_up([from_end(v) for v in range(DIRECT)])
    for v in range(DIRECT):
        at_v = from_end(v)
        for slot, (dy, dc) in enumerate(((2, 0), (2, 1), (1, 0), (1, 1), (3, 0), (3, 1), (0, 1))):
            to_y, to_core = lax.rem(y + dy, NY), lax.rem(core + dc, NC)
            to_bl(
                part.at[at_v, to_core, to_y], got_0.at[v, slot], r0s.at[0], r0r.at[v],
                join_index(to_y, z, to_core),
            ).start()
    add_up([DIRECT - odd + v for v in range(NZ - DIRECT)])
    lax.fori_loop(DIRECT, NZ, hand_over, 0)
    lax.fori_loop(DIRECT, NZ, along_y, 0)
    for v in range(DIRECT):
        got = got_0.at[v]
        to_bl(got, got, r0s.at[0], r0r.at[v], other).wait_recv()
        at_v = from_end(v)
        total = part[at_v, core, y]
        for slot in range(7):
            total = total + got_0[v, slot]
        part[at_v, core, y] = total
        send_on(at_v)
    lax.fori_loop(DIRECT, NZ, along_z, 0)
    got_z[z] = part[z, core, y]

    for edge in edges:
        edge.wait_recv()

    @pl.when(early)
    def _():
        for edge in edges:
            edge.start()

    from_prev, from_next = halo_got[0], halo_got[1]
    x = own

    def shift(v, by):
        return pltpu.roll(v, by % LANES, 1)

    prev_edge = jnp.concatenate([pltpu.roll(from_prev, 121, 1), pltpu.roll(from_prev, 122, 1)], axis=1)
    next_edge = jnp.concatenate([pltpu.roll(from_next, 7, 1), pltpu.roll(from_next, 6, 1)], axis=1)
    next_weight = jnp.concatenate([pltpu.roll(from_next, 5, 1)] * 2, axis=1)
    is_first, is_last = freq == 0, freq == CHANNELS - 1
    not_low = jnp.where(chan > 0, 1.0, 0.0).astype(F32)
    not_high = jnp.where(chan < n_chan - 1, 1.0, 0.0).astype(F32)

    def slope(w, step):
        square = step * step
        for by in (128, 64, 32):
            square = square + shift(square, by)
        return w * step / jnp.sqrt(square + SMOOTH_EPS)

    grad = slope(
        jnp.where(is_first, weight * not_low, weight), x - jnp.where(is_first, prev_edge, shift(x, 1))
    )
    grad -= slope(
        jnp.where(is_last, next_weight * not_high, shift(weight, -1)),
        jnp.where(is_last, next_edge, shift(x, -1)) - x,
    )
    grad += slope(jnp.where(time > 0, weight, 0.0), x - shift(x, 8))
    grad -= slope(jnp.where(time < TIMES - 1, weight, 0.0), shift(x, -8) - x)
    updated = x - (STEP * TV_SCALE) * grad

    rows = got_z.at[pl.ds(0, NZ - 1)]
    to_bl(rows, rows, rzs.at[0], rzr.at[0], other).wait_recv()
    total = got_z[0]
    for v in range(1, NZ):
        total = total + got_z[v]
    updated = updated + STEP * total
    upd_ref[...] = jnp.transpose(updated).reshape(8, TIMES, CHANNELS, 8)

    for edge in edges:
        edge.wait_send()

    def left(at):
        for sem, count in ((0, (3, 3, 3, 3, 3, 4, 5, 6)[at]), (1, (0, 4, 0, 16, 3, 2, 1, 0)[at])):
            if count:
                sent = part.at[pl.ds(0, count), 0, 0] if count <= NZ else part.at[pl.ds(0, count // NY), 0]
                to_bl(sent, sent, zs.at[sem], rzr.at[0], other).wait_send()

    for at in range(NZ):
        pl.when(z == at)(functools.partial(left, at))

    to_bl(rows, rows, rzs.at[0], rzr.at[0], other).wait_send()
    half = part.at[pl.ds(0, NZ), 0]
    to_bl(half, half, cs.at[0], rzr.at[0], other).wait_send()
    seven = part.at[pl.ds(0, NZ - DIRECT), 0]
    to_bl(seven, seven, rcs.at[0], rzr.at[0], other).wait_send()
    to_bl(got_0, got_0, r0s.at[0], rzr.at[0], other).wait_send()
    to_bl(got_y, got_y, ys.at[0], rzr.at[0], other).wait_send()
    most = got_y.at[pl.ds(0, NZ - DIRECT)]
    to_bl(most, most, rys.at[0], rzr.at[0], other).wait_send()


def hand_out(updated, residual, updated_h, residual_h, sem):
    copies = [
        pltpu.make_async_copy(updated, updated_h, sem.at[0]),
        pltpu.make_async_copy(residual, residual_h, sem.at[1]),
    ]
    for copy in copies:
        copy.start()
    for copy in copies:
        copy.wait()


def local(meas, model, imp, tally, one, two, gains, tvw):
    big = (8, TIMES, CHANNELS, PAIRS)
    vmem = pltpu.VMEM
    dma = pltpu.SemaphoreType.DMA
    flag = pltpu.SemaphoreType.REGULAR
    any_spec = pl.BlockSpec(memory_space=pl.ANY)
    vmem_spec = pl.BlockSpec(memory_space=pltpu.VMEM)
    updated, residual = pl.pallas_call(
        kernel,
        out_shape=(vmem((8, TIMES, CHANNELS, 8), F32), vmem(big, F32)),
        in_specs=[any_spec] * 8,
        out_specs=(vmem_spec, vmem_spec),
        scratch_shapes=[
            vmem(big, F32), vmem(big, F32), vmem((TIMES, CHANNELS, PAIRS), F32),
            vmem((1, PAIRS), jnp.int32), vmem((1, PAIRS), jnp.int32), vmem((1, PAIRS), jnp.int32),
            vmem((8, TIMES, CHANNELS, 8), F32), vmem((CHANNELS, 8), F32),
            vmem((NZ, NC, NY, 8, LANES), F32), vmem((NZ, NC, 32, PAIRS), BF16), vmem((NZ, NC, 32, PAIRS), BF16),
            vmem(big, F32), vmem(big, F32), vmem((NZ, NC, NY, 8, LANES), F32),
            vmem((DIRECT, 7, 8, LANES), F32), vmem((NZ, NY, 8, LANES), F32), vmem((NZ, NY - 1, 8, LANES), F32), vmem((NZ, 8, LANES), F32),
            vmem((8, 128), F32), vmem((2, 8, 128), F32),
            dma((8,)), dma((2,)), dma((NZ,)), dma((1,)), dma((2,)), dma((1,)), dma((2,)), dma((2,)), dma((2,)),
            dma((1,)), dma((DIRECT,)), dma((1,)), dma((NZ,)), dma((1,)), dma((NZ,)), dma((1,)), dma((1,)),
            flag((NZ,)), flag, flag, flag,
        ],
        compiler_params=pltpu.CompilerParams(
            collective_id=0, has_side_effects=True, vmem_limit_bytes=58 * 1024 * 1024
        ),
    )(meas, model, imp, tally, one.reshape(1, PAIRS), two.reshape(1, PAIRS), gains, tvw)
    held = [pltpu.with_memory_space_constraint(x, pltpu.VMEM) for x in (updated, residual)]
    return pl.pallas_call(
        hand_out,
        out_shape=(jax.ShapeDtypeStruct(updated.shape, F32), jax.ShapeDtypeStruct(residual.shape, F32)),
        in_specs=[vmem_spec, vmem_spec],
        out_specs=(any_spec, any_spec),
        scratch_shapes=[dma((2,))],
    )(*held)


def solution(mesh):
    placed = (
        P(None, None, "chan", "bl"),
        P(None, None, "chan", "bl"),
        P(None, "chan", "bl"),
        P("chan", "bl"),
        P("bl"),
        P("bl"),
        P(None, None, "chan", "bl"),
        P("chan", "bl"),
    )
    return jax.shard_map(
        local,
        mesh=mesh,
        in_specs=placed,
        out_specs=(P(None, None, "chan", "bl"), P(None, None, "chan", "bl")),
        check_vma=False,
    )
```

```python
import functools

import jax
import jax.numpy as jnp
from jax import lax
from jax.experimental import pallas as pl
from jax.experimental.pallas import tpu as pltpu
from jax.sharding import PartitionSpec as P

MESH = pl.DeviceIdType.MESH
STATIONS = 512
BASELINES = 32768
TIMES = 4
CHANNELS = 8
PAIRS = 512
LANES = 8 * TIMES * CHANNELS
NY, NZ, NC = 4, 8, 2
HALF = NZ // 2
DIRECT = 2
SMOOTH_EPS = 0.01
TV_SCALE = 2.0
STEP = 2.0 * STATIONS / BASELINES
F32 = jnp.float32
BF16 = jnp.bfloat16


def cmul_add(terms):
    real, imag = None, None
    for (ar, ai), (br, bi), conj in terms:
        if conj:
            r, i = ar * br + ai * bi, ai * br - ar * bi
        else:
            r, i = ar * br - ai * bi, ar * bi + ai * br
        real = r if real is None else real + r
        imag = i if imag is None else imag + i
    return real, imag


def halves(x):
    high = x.astype(BF16)
    return high, (x - high.astype(F32)).astype(BF16)


def split_index():
    bl = lax.axis_index("bl")
    return lax.div(bl, NZ * NC), lax.rem(lax.div(bl, NC), NZ), lax.rem(bl, NC)


def join_index(y, z, core):
    return (y * NZ + z) * NC + core


def kernel(
    meas_h, model_h, imp_h, tally_h, one_h, two_h, gains_h, tvw_h,
    upd_ref, res,
    meas, model, imp, tally, one, two, gains, tvw,
    table, hot1, hot2, gp, gq, part, got_0, got_c, got_y, got_z, halo, halo_got,
    in_sem, zs, zr, ys, yr, cs, cr, hs, hr, r0s, r0r, rcs, rcr, rys, ryr, rzs, rzr,
    ready_z, ready_y, ready_c, hub,
):
    chan = lax.axis_index("chan")
    n_chan = lax.axis_size("chan")
    odd = lax.rem(chan, 2)
    y, z, core = split_index()
    early = odd == 0
    chan_peers = [lax.rem(chan + 1, n_chan), lax.rem(chan + n_chan - 1, n_chan)]

    def to_bl(src, dst, send, recv, peer):
        return pltpu.make_async_remote_copy(
            src_ref=src, dst_ref=dst, send_sem=send, recv_sem=recv,
            device_id={"bl": peer}, device_id_type=MESH,
        )

    def z_peer(to):
        return join_index(y, to, core)

    def y_peer(k):
        to = lax.rem(y + k, NY)
        return join_index(to, z, core), to

    other = join_index(y, z, 1 - core)

    loads = [
        pltpu.make_async_copy(src, dst, in_sem.at[i])
        for i, (src, dst) in enumerate(
            [(gains_h, gains), (one_h, one), (two_h, two), (tvw_h, tvw), (tally_h, tally),
             (imp_h, imp), (meas_h, meas), (model_h, model)]
        )
    ]
    loads[0].start()
    barrier = pltpu.get_barrier_semaphore()

    second = lax.rem(y + core, 2)
    upper = lax.div(z, HALF)
    beside = [y_peer(1)[0], y_peer(3)[0], other]

    def tell_beside(sem):
        for peer in beside:
            pl.semaphore_signal(sem, inc=1, device_id={"bl": peer}, device_id_type=MESH)

    def announce(to, carry):
        pl.semaphore_signal(barrier, inc=1, device_id={"bl": z_peer(to)}, device_id_type=MESH)
        return carry

    lax.fori_loop(0, (1 - upper) * z, announce, 0)
    lax.fori_loop(jnp.where(z == 0, NZ, jnp.maximum(z + 1, HALF)), NZ, announce, 0)
    pl.when((upper == 0) & (second == 0))(lambda: tell_beside(barrier))

    @pl.when((upper == 1) & (core == 0))
    def _():
        pl.semaphore_signal(barrier, inc=1, device_id={"bl": other}, device_id_type=MESH)

    @pl.when(early)
    def _():
        for peer in chan_peers:
            pl.semaphore_signal(barrier, inc=1, device_id={"chan": peer}, device_id_type=MESH)

    earlier = upper * (z - 1) + (1 - upper) * (HALF - 1 - z) + (1 - upper) * 3 * second + upper * core + 2 * odd

    @pl.when(earlier > 0)
    def _():
        pl.semaphore_wait(barrier, earlier)

    def tell_z(to, carry):
        pl.semaphore_signal(ready_z.at[z], inc=1, device_id={"bl": z_peer(to)}, device_id_type=MESH)
        return carry

    lax.fori_loop(HALF - 1, z, tell_z, 0)
    pl.when((upper == 0) & (second == 1))(lambda: tell_beside(ready_y))

    @pl.when((upper == 1) & (core == 1))
    def _():
        pl.semaphore_signal(ready_c, inc=1, device_id={"bl": other}, device_id_type=MESH)

    loads[0].wait()
    own = jnp.transpose(gains[...].reshape(LANES, 8))
    table[z, core, y] = own

    mine = table.at[z, core, y]

    def send_own(to, carry):
        to_bl(mine, mine, zs.at[0], zr.at[z], z_peer(to)).start()
        return carry

    lax.fori_loop(1 + (1 - upper) * z, upper * z + (1 - upper) * HALF, send_own, 0)
    for load in loads[1:]:
        load.start()

    @pl.when((upper == 0) & (second == 0))
    def _():
        pl.semaphore_wait(ready_y, 3)
        tell_beside(ready_y)


    loads[3].wait()
    lane = lax.broadcasted_iota(jnp.int32, (8, LANES), 1)
    freq, time = lane & 7, lax.shift_right_logical(lane, 3) & 3
    weight = jnp.transpose(
        jnp.broadcast_to(tvw[...][None], (8 * TIMES, CHANNELS, 8)).reshape(LANES, 8)
    )
    low, high = own[:, :128], own[:, 128:]
    freq_h = freq[:, :128]
    halo[...] = jnp.where(
        freq_h == 0, low,
        jnp.where(
            freq_h == 1, pltpu.roll(high, 1, 1),
            jnp.where(
                freq_h == 7, low,
                jnp.where(freq_h == 6, pltpu.roll(high, 127, 1), pltpu.roll(weight[:, :128], 2, 1)),
            ),
        ),
    )
    edges = [
        pltpu.make_async_remote_copy(
            src_ref=halo, dst_ref=halo_got.at[k], send_sem=hs.at[k], recv_sem=hr.at[k],
            device_id={"chan": peer}, device_id_type=MESH,
        )
        for k, peer in enumerate(chan_peers)
    ]

    @pl.when(jnp.logical_not(early))
    def _():
        for edge in edges:
            edge.start()

    loads[1].wait()
    loads[2].wait()

    def to_row(ant):
        return (
            (lax.shift_right_logical(ant, 4) & 7) * 64 + (lax.shift_right_logical(ant, 3) & 1) * 32
            + lax.shift_right_logical(ant, 7) * 8 + (ant & 7)
        )

    row1, row2 = to_row(one[...]), to_row(two[...])

    def hot_body(i, carry):
        index = lax.broadcasted_iota(jnp.int32, (32, PAIRS), 0) + i * 32
        v, half = lax.div(i, NC), lax.rem(i, NC)
        hot1[v, half] = jnp.where(index == row1, 1.0, 0.0).astype(BF16)
        hot2[v, half] = jnp.where(index == row2, 1.0, 0.0).astype(BF16)
        return carry

    lax.fori_loop(0, 16, hot_body, 0)

    loads[4].wait()
    loads[5].wait()
    keep = lax.broadcasted_iota(jnp.int32, (CHANNELS, PAIRS), 0) < CHANNELS - tally[...]
    for t in range(TIMES):
        imp[t] = jnp.where(keep, imp[t], 0.0)
    loads[6].wait()
    loads[7].wait()

    def pieces(v, count):
        return table.at[v, core, y] if count == 1 else table.at[pl.ds(v, count), core, y]

    def send_up(to, v, count):
        pl.semaphore_wait(ready_z.at[to], 1)
        rows = pieces(v, count)
        to_bl(rows, rows, zs.at[1], zr.at[v], z_peer(to)).start()

    def wait_for(v, count=1):
        rows = pieces(v, count)
        to_bl(rows, rows, zs.at[1], zr.at[v], other).wait_recv()

    def pass_on(v, count=1):
        rows = pieces(v, count)
        for k in (2, 1, 3):
            to_bl(rows, rows, ys.at[0], yr.at[v // HALF], y_peer(k)[0]).start()

    def take_in(v, count=1):
        wait_for(v, count)
        pass_on(v, count)

    def share(half):
        three = table.at[pl.ds(half * HALF, HALF), core, pl.ds(0, 3)]
        to_bl(three, three, ys.at[0], yr.at[half], other).wait_recv()
        four = table.at[pl.ds(half * HALF, HALF), core]
        to_bl(four, four, cs.at[0], cr.at[half], other).start()

    def pick(half, first):
        flipped = jnp.transpose(table[:, half].reshape(256, LANES))
        g_high, g_low = halves(flipped)
        for hot, dst in ((hot1, gp), (hot2, gq)):
            rows = hot[:, half].reshape(256, PAIRS)
            picked = jnp.dot(g_high, rows, preferred_element_type=F32) + jnp.dot(
                g_low, rows, preferred_element_type=F32
            )
            picked = picked.reshape(8, TIMES, CHANNELS, PAIRS)
            dst[...] = picked if first else dst[...] + picked

    def tell_plane():
        pl.semaphore_wait(hub, NY - 1)
        pl.semaphore_signal(ready_y, inc=1, device_id={"bl": z_peer(HALF)}, device_id_type=MESH)

    def line(at):
        for to in range(at + 1, NZ) if at >= HALF else ():
            send_up(to, at, 1)
        if at < HALF:

            @pl.when(second == 1)
            def _():
                pl.semaphore_wait(ready_y, 3)

        else:
            pl.semaphore_wait(ready_y, 1)
        if at == HALF - 1:
            pl.semaphore_wait(ready_z.at[HALF], 1)
        if at in (HALF - 1, HALF):
            for k in (2, 1, 3):
                pl.semaphore_signal(hub, inc=1, device_id={"bl": y_peer(k)[0]}, device_id_type=MESH)
        if at == HALF:
            pl.semaphore_wait(hub, NY - 1)
            for to in (7, 6, 5):
                pl.semaphore_signal(ready_y, inc=1, device_id={"bl": z_peer(to)}, device_id_type=MESH)
        pass_on(at)
        if at < HALF:
            for v in (3, 2, 1, 0):
                if at == HALF - 1 and v == 0:
                    pl.when(early)(tell_plane)
                if v != at:
                    take_in(v)
                if v < at:
                    send_own(v, 0)
            if at == HALF - 1:
                pl.when(jnp.logical_not(early))(tell_plane)
                lower = pieces(0, HALF)
                to_bl(lower, lower, zs.at[1], zr.at[0], z_peer(HALF)).start()
                for to in (5, 6, 7):
                    send_up(to, 0, HALF)
            for v in range(HALF, NZ):
                take_in(v)
                if at == 1:
                    piece = pieces(v, 1)
                    to_bl(piece, piece, zs.at[1], zr.at[v], z_peer(0)).start()
        else:
            for v in range(HALF, NZ):
                if v != at:
                    take_in(v)
            take_in(0, HALF)

    for at in range(NZ):
        pl.when(z == at)(functools.partial(line, at))

    @pl.when((upper == 1) & (core == 0))
    def _():
        pl.semaphore_wait(ready_c, 1)

    share(upper)
    share(1 - upper)
    pick(core, True)
    for half in range(2):
        four = table.at[pl.ds(half * HALF, HALF), 1 - core]
        to_bl(four, four, cs.at[0], cr.at[half], other).wait_recv()
    pick(1 - core, False)

    def compute(i, carry):
        t = lax.div(i, 4)
        at = pl.ds(pl.multiple_of(lax.rem(i, 4) * 128, 128), 128)

        def matrix(ref):
            return [(ref[c, t, :, at], ref[c + 4, t, :, at]) for c in range(4)]

        jp, jq, m, d = matrix(gp), matrix(gq), matrix(model), matrix(meas)
        w = imp[t, :, at]
        a = [
            cmul_add([(jp[2 * r], m[c], False), (jp[2 * r + 1], m[c + 2], False)])
            for r in range(2) for c in range(2)
        ]
        v = [
            cmul_add([(a[2 * r], jq[2 * c], True), (a[2 * r + 1], jq[2 * c + 1], True)])
            for r in range(2) for c in range(2)
        ]
        e = [(w * (d[k][0] - v[k][0]), w * (d[k][1] - v[k][1])) for k in range(4)]
        for k in range(4):
            res[k, t, :, at] = e[k][0]
            res[k + 4, t, :, at] = e[k][1]
        b = [
            cmul_add([(jq[2 * r], m[2 * c], True), (jq[2 * r + 1], m[2 * c + 1], True)])
            for r in range(2) for c in range(2)
        ]
        first = [
            cmul_add([(e[2 * r], b[c], False), (e[2 * r + 1], b[c + 2], False)])
            for r in range(2) for c in range(2)
        ]
        second = [
            cmul_add([(a[c], e[r], True), (a[c + 2], e[r + 2], True)])
            for r in range(2) for c in range(2)
        ]
        for k in range(4):
            gp[k, t, :, at] = first[k][0]
            gp[k + 4, t, :, at] = first[k][1]
            gq[k, t, :, at] = second[k][0]
            gq[k + 4, t, :, at] = second[k][1]
        return carry

    lax.fori_loop(0, 16, compute, 0, unroll=2)

    p_high, p_low = halves(gp[...].reshape(LANES, PAIRS))
    q_high, q_low = halves(gq[...].reshape(LANES, PAIRS))
    nt = (((1,), (1,)), ((), ()))

    def add_up(places):
        h1, h2 = (
            jnp.concatenate([hot[v].reshape(64, PAIRS) for v in places]) for hot in (hot1, hot2)
        )
        total = lax.dot_general(h1, p_high, nt, preferred_element_type=F32)
        total += lax.dot_general(h1, p_low, nt, preferred_element_type=F32)
        total += lax.dot_general(h2, q_high, nt, preferred_element_type=F32)
        total += lax.dot_general(h2, q_low, nt, preferred_element_type=F32)
        for i, v in enumerate(places):
            part[v] = total[i * 64 : i * 64 + 64].reshape(NC, NY, 8, LANES)

    def from_end(v):
        if isinstance(v, int):
            return v + odd * ((v // 2 if v % 2 else NZ - 1 - v // 2) - v)
        far = lax.rem(v, 2)
        return v + odd * (lax.div(v, 2) * (2 * far - 1) + (1 - far) * (NZ - 1) - v)

    def hand_over(step, carry):
        v = from_end(step)
        to_bl(part.at[v, 1 - core], got_c.at[v], rcs.at[0], rcr.at[v], other).start()
        return carry

    def along_y(step, carry):
        v = from_end(step)
        got = got_c.at[v]
        to_bl(got, got, rcs.at[0], rcr.at[v], other).wait_recv()
        part[v, core] = part[v, core] + got_c[v]
        for k in (2, 1, 3):
            peer, to = y_peer(k)
            to_bl(part.at[v, core, to], got_y.at[v, k - 1], rys.at[0], ryr.at[v], peer).start()
        return carry

    def send_on(v):
        @pl.when(v != z)
        def _():
            to_bl(part.at[v, core, y], got_z.at[z], rzs.at[0], rzr.at[0], z_peer(v)).start()

    def along_z(step, carry):
        v = from_end(step)
        got = got_y.at[v]
        to_bl(got, got, rys.at[0], ryr.at[v], other).wait_recv()
        part[v, core, y] = part[v, core, y] + got_y[v, 0] + (got_y[v, 1] + got_y[v, 2])
        send_on(v)
        return carry

    add_up([from_end(v) for v in range(DIRECT)])
    for v in range(DIRECT):
        at_v = from_end(v)
        for slot, (dy, dc) in enumerate(((2, 0), (2, 1), (1, 0), (1, 1), (3, 0), (3, 1), (0, 1))):
            to_y, to_core = lax.rem(y + dy, NY), lax.rem(core + dc, NC)
            to_bl(
                part.at[at_v, to_core, to_y], got_0.at[v, slot], r0s.at[0], r0r.at[v],
                join_index(to_y, z, to_core),
            ).start()
    add_up([DIRECT - odd + v for v in range(NZ - DIRECT)])
    lax.fori_loop(DIRECT, NZ, hand_over, 0)
    lax.fori_loop(DIRECT, NZ - 3, along_y, 0)
    for v in range(DIRECT):
        got = got_0.at[v]
        to_bl(got, got, r0s.at[0], r0r.at[v], other).wait_recv()
        at_v = from_end(v)
        total = part[at_v, core, y]
        for slot in range(7):
            total = total + got_0[v, slot]
        part[at_v, core, y] = total
        send_on(at_v)
    lax.fori_loop(NZ - 3, NZ, along_y, 0)
    lax.fori_loop(DIRECT, NZ, along_z, 0)
    got_z[z] = part[z, core, y]

    for edge in edges:
        edge.wait_recv()

    @pl.when(early)
    def _():
        for edge in edges:
            edge.start()

    from_prev, from_next = halo_got[0], halo_got[1]
    x = own

    def shift(v, by):
        return pltpu.roll(v, by % LANES, 1)

    prev_edge = jnp.concatenate([pltpu.roll(from_prev, 121, 1), pltpu.roll(from_prev, 122, 1)], axis=1)
    next_edge = jnp.concatenate([pltpu.roll(from_next, 7, 1), pltpu.roll(from_next, 6, 1)], axis=1)
    next_weight = jnp.concatenate([pltpu.roll(from_next, 5, 1)] * 2, axis=1)
    is_first, is_last = freq == 0, freq == CHANNELS - 1
    not_low = jnp.where(chan > 0, 1.0, 0.0).astype(F32)
    not_high = jnp.where(chan < n_chan - 1, 1.0, 0.0).astype(F32)

    def slope(w, step):
        square = step * step
        for by in (128, 64, 32):
            square = square + shift(square, by)
        return w * step / jnp.sqrt(square + SMOOTH_EPS)

    grad = slope(
        jnp.where(is_first, weight * not_low, weight), x - jnp.where(is_first, prev_edge, shift(x, 1))
    )
    grad -= slope(
        jnp.where(is_last, next_weight * not_high, shift(weight, -1)),
        jnp.where(is_last, next_edge, shift(x, -1)) - x,
    )
    grad += slope(jnp.where(time > 0, weight, 0.0), x - shift(x, 8))
    grad -= slope(jnp.where(time < TIMES - 1, weight, 0.0), shift(x, -8) - x)
    updated = x - (STEP * TV_SCALE) * grad

    rows = got_z.at[pl.ds(0, NZ - 1)]
    to_bl(rows, rows, rzs.at[0], rzr.at[0], other).wait_recv()
    total = got_z[0]
    for v in range(1, NZ):
        total = total + got_z[v]
    updated = updated + STEP * total
    upd_ref[...] = jnp.transpose(updated).reshape(8, TIMES, CHANNELS, 8)

    for edge in edges:
        edge.wait_send()

    def left(at):
        for sem, count in ((0, (3, 3, 3, 3, 3, 4, 5, 6)[at]), (1, (0, 4, 0, 16, 3, 2, 1, 0)[at])):
            if count:
                sent = part.at[pl.ds(0, count), 0, 0] if count <= NZ else part.at[pl.ds(0, count // NY), 0]
                to_bl(sent, sent, zs.at[sem], rzr.at[0], other).wait_send()

    for at in range(NZ):
        pl.when(z == at)(functools.partial(left, at))

    to_bl(rows, rows, rzs.at[0], rzr.at[0], other).wait_send()
    half = part.at[pl.ds(0, NZ), 0]
    to_bl(half, half, cs.at[0], rzr.at[0], other).wait_send()
    seven = part.at[pl.ds(0, NZ - DIRECT), 0]
    to_bl(seven, seven, rcs.at[0], rzr.at[0], other).wait_send()
    to_bl(got_0, got_0, r0s.at[0], rzr.at[0], other).wait_send()
    to_bl(got_y, got_y, ys.at[0], rzr.at[0], other).wait_send()
    most = got_y.at[pl.ds(0, NZ - DIRECT)]
    to_bl(most, most, rys.at[0], rzr.at[0], other).wait_send()


def hand_out(updated, residual, updated_h, residual_h, sem):
    copies = [
        pltpu.make_async_copy(residual, residual_h, sem.at[0]),
        pltpu.make_async_copy(updated, updated_h, sem.at[1]),
    ]
    for copy in copies:
        copy.start()
    for copy in copies:
        copy.wait()


def local(meas, model, imp, tally, one, two, gains, tvw):
    big = (8, TIMES, CHANNELS, PAIRS)
    vmem = pltpu.VMEM
    dma = pltpu.SemaphoreType.DMA
    flag = pltpu.SemaphoreType.REGULAR
    any_spec = pl.BlockSpec(memory_space=pl.ANY)
    vmem_spec = pl.BlockSpec(memory_space=pltpu.VMEM)
    updated, residual = pl.pallas_call(
        kernel,
        out_shape=(vmem((8, TIMES, CHANNELS, 8), F32), vmem(big, F32)),
        in_specs=[any_spec] * 8,
        out_specs=(vmem_spec, vmem_spec),
        scratch_shapes=[
            vmem(big, F32), vmem(big, F32), vmem((TIMES, CHANNELS, PAIRS), F32),
            vmem((1, PAIRS), jnp.int32), vmem((1, PAIRS), jnp.int32), vmem((1, PAIRS), jnp.int32),
            vmem((8, TIMES, CHANNELS, 8), F32), vmem((CHANNELS, 8), F32),
            vmem((NZ, NC, NY, 8, LANES), F32), vmem((NZ, NC, 32, PAIRS), BF16), vmem((NZ, NC, 32, PAIRS), BF16),
            vmem(big, F32), vmem(big, F32), vmem((NZ, NC, NY, 8, LANES), F32),
            vmem((DIRECT, 7, 8, LANES), F32), vmem((NZ, NY, 8, LANES), F32), vmem((NZ, NY - 1, 8, LANES), F32), vmem((NZ, 8, LANES), F32),
            vmem((8, 128), F32), vmem((2, 8, 128), F32),
            dma((8,)), dma((2,)), dma((NZ,)), dma((1,)), dma((2,)), dma((1,)), dma((2,)), dma((2,)), dma((2,)),
            dma((1,)), dma((DIRECT,)), dma((1,)), dma((NZ,)), dma((1,)), dma((NZ,)), dma((1,)), dma((1,)),
            flag((NZ,)), flag, flag, flag,
        ],
        compiler_params=pltpu.CompilerParams(
            collective_id=0, has_side_effects=True, vmem_limit_bytes=58 * 1024 * 1024
        ),
    )(meas, model, imp, tally, one.reshape(1, PAIRS), two.reshape(1, PAIRS), gains, tvw)
    held = [pltpu.with_memory_space_constraint(x, pltpu.VMEM) for x in (updated, residual)]
    return pl.pallas_call(
        hand_out,
        out_shape=(jax.ShapeDtypeStruct(updated.shape, F32), jax.ShapeDtypeStruct(residual.shape, F32)),
        in_specs=[vmem_spec, vmem_spec],
        out_specs=(any_spec, any_spec),
        scratch_shapes=[dma((2,))],
    )(*held)


def solution(mesh):
    placed = (
        P(None, None, "chan", "bl"),
        P(None, None, "chan", "bl"),
        P(None, "chan", "bl"),
        P("chan", "bl"),
        P("bl"),
        P("bl"),
        P(None, None, "chan", "bl"),
        P("chan", "bl"),
    )
    return jax.shard_map(
        local,
        mesh=mesh,
        in_specs=placed,
        out_specs=(P(None, None, "chan", "bl"), P(None, None, "chan", "bl")),
        check_vma=False,
    )
```

```python
import functools

import jax
import jax.numpy as jnp
from jax import lax
from jax.experimental import pallas as pl
from jax.experimental.pallas import tpu as pltpu
from jax.sharding import PartitionSpec as P

MESH = pl.DeviceIdType.MESH
STATIONS = 512
BASELINES = 32768
TIMES = 4
CHANNELS = 8
PAIRS = 512
LANES = 8 * TIMES * CHANNELS
NY, NZ, NC = 4, 8, 2
HALF = NZ // 2
DIRECT = 2
SMOOTH_EPS = 0.01
TV_SCALE = 2.0
STEP = 2.0 * STATIONS / BASELINES
F32 = jnp.float32
BF16 = jnp.bfloat16


def cmul_add(terms):
    real, imag = None, None
    for (ar, ai), (br, bi), conj in terms:
        if conj:
            r, i = ar * br + ai * bi, ai * br - ar * bi
        else:
            r, i = ar * br - ai * bi, ar * bi + ai * br
        real = r if real is None else real + r
        imag = i if imag is None else imag + i
    return real, imag


def halves(x):
    high = x.astype(BF16)
    return high, (x - high.astype(F32)).astype(BF16)


def split_index():
    bl = lax.axis_index("bl")
    return lax.div(bl, NZ * NC), lax.rem(lax.div(bl, NC), NZ), lax.rem(bl, NC)


def join_index(y, z, core):
    return (y * NZ + z) * NC + core


def kernel(
    meas_h, model_h, imp_h, tally_h, one_h, two_h, gains_h, tvw_h,
    upd_ref, res,
    meas, model, imp, tally, one, two, gains, tvw,
    table, hot1, hot2, gp, gq, part, got_0, got_c, got_y, got_z, halo, halo_got,
    in_sem, zs, zr, ys, yr, cs, cr, hs, hr, r0s, r0r, rcs, rcr, rys, ryr, rzs, rzr,
    ready_z, ready_y, ready_c, hub,
):
    chan = lax.axis_index("chan")
    n_chan = lax.axis_size("chan")
    odd = lax.rem(chan, 2)
    y, z, core = split_index()
    early = odd == 0
    chan_peers = [lax.rem(chan + 1, n_chan), lax.rem(chan + n_chan - 1, n_chan)]

    def to_bl(src, dst, send, recv, peer):
        return pltpu.make_async_remote_copy(
            src_ref=src, dst_ref=dst, send_sem=send, recv_sem=recv,
            device_id={"bl": peer}, device_id_type=MESH,
        )

    def z_peer(to):
        return join_index(y, to, core)

    def y_peer(k):
        to = lax.rem(y + k, NY)
        return join_index(to, z, core), to

    other = join_index(y, z, 1 - core)

    loads = [
        pltpu.make_async_copy(src, dst, in_sem.at[i])
        for i, (src, dst) in enumerate(
            [(gains_h, gains), (one_h, one), (two_h, two), (tvw_h, tvw), (tally_h, tally),
             (imp_h, imp), (meas_h, meas), (model_h, model)]
        )
    ]
    loads[0].start()
    barrier = pltpu.get_barrier_semaphore()

    second = lax.rem(y + core, 2)
    upper = lax.div(z, HALF)
    beside = [y_peer(1)[0], y_peer(3)[0], other]

    def tell_beside(sem):
        for peer in beside:
            pl.semaphore_signal(sem, inc=1, device_id={"bl": peer}, device_id_type=MESH)

    def announce(to, carry):
        pl.semaphore_signal(barrier, inc=1, device_id={"bl": z_peer(to)}, device_id_type=MESH)
        return carry

    lax.fori_loop(0, (1 - upper) * z, announce, 0)
    lax.fori_loop(jnp.where(z == 0, NZ, jnp.maximum(z + 1, HALF)), NZ, announce, 0)
    pl.when((upper == 0) & (second == 0))(lambda: tell_beside(barrier))

    @pl.when((upper == 1) & (core == 0))
    def _():
        pl.semaphore_signal(barrier, inc=1, device_id={"bl": other}, device_id_type=MESH)

    @pl.when(early)
    def _():
        for peer in chan_peers:
            pl.semaphore_signal(barrier, inc=1, device_id={"chan": peer}, device_id_type=MESH)

    earlier = upper * (z - 1) + (1 - upper) * (HALF - 1 - z) + (1 - upper) * 3 * second + upper * core + 2 * odd

    @pl.when(earlier > 0)
    def _():
        pl.semaphore_wait(barrier, earlier)

    def tell_z(to, carry):
        pl.semaphore_signal(ready_z.at[z], inc=1, device_id={"bl": z_peer(to)}, device_id_type=MESH)
        return carry

    lax.fori_loop(HALF - 1, z, tell_z, 0)
    pl.when((upper == 0) & (second == 1))(lambda: tell_beside(ready_y))

    @pl.when((upper == 1) & (core == 1))
    def _():
        pl.semaphore_signal(ready_c, inc=1, device_id={"bl": other}, device_id_type=MESH)

    loads[0].wait()
    own = jnp.transpose(gains[...].reshape(LANES, 8))
    table[z, core, y] = own

    mine = table.at[z, core, y]

    def send_own(to, carry):
        to_bl(mine, mine, zs.at[0], zr.at[z], z_peer(to)).start()
        return carry

    lax.fori_loop(1 + (1 - upper) * z, upper * z + (1 - upper) * HALF, send_own, 0)
    for load in loads[1:]:
        load.start()

    @pl.when((upper == 0) & (second == 0))
    def _():
        pl.semaphore_wait(ready_y, 3)
        tell_beside(ready_y)


    loads[3].wait()
    lane = lax.broadcasted_iota(jnp.int32, (8, LANES), 1)
    freq, time = lane & 7, lax.shift_right_logical(lane, 3) & 3
    weight = jnp.transpose(
        jnp.broadcast_to(tvw[...][None], (8 * TIMES, CHANNELS, 8)).reshape(LANES, 8)
    )
    low, high = own[:, :128], own[:, 128:]
    freq_h = freq[:, :128]
    halo[...] = jnp.where(
        freq_h == 0, low,
        jnp.where(
            freq_h == 1, pltpu.roll(high, 1, 1),
            jnp.where(
                freq_h == 7, low,
                jnp.where(freq_h == 6, pltpu.roll(high, 127, 1), pltpu.roll(weight[:, :128], 2, 1)),
            ),
        ),
    )
    edges = [
        pltpu.make_async_remote_copy(
            src_ref=halo, dst_ref=halo_got.at[k], send_sem=hs.at[k], recv_sem=hr.at[k],
            device_id={"chan": peer}, device_id_type=MESH,
        )
        for k, peer in enumerate(chan_peers)
    ]

    @pl.when(jnp.logical_not(early))
    def _():
        for edge in edges:
            edge.start()

    loads[1].wait()
    loads[2].wait()

    def to_row(ant):
        return (
            (lax.shift_right_logical(ant, 4) & 7) * 64 + (lax.shift_right_logical(ant, 3) & 1) * 32
            + lax.shift_right_logical(ant, 7) * 8 + (ant & 7)
        )

    row1, row2 = to_row(one[...]), to_row(two[...])

    def hot_body(i, carry):
        index = lax.broadcasted_iota(jnp.int32, (32, PAIRS), 0) + i * 32
        v, half = lax.div(i, NC), lax.rem(i, NC)
        hot1[v, half] = jnp.where(index == row1, 1.0, 0.0).astype(BF16)
        hot2[v, half] = jnp.where(index == row2, 1.0, 0.0).astype(BF16)
        return carry

    lax.fori_loop(0, 16, hot_body, 0)

    loads[4].wait()
    loads[5].wait()
    keep = lax.broadcasted_iota(jnp.int32, (CHANNELS, PAIRS), 0) < CHANNELS - tally[...]
    for t in range(TIMES):
        imp[t] = jnp.where(keep, imp[t], 0.0)
    loads[6].wait()
    loads[7].wait()

    def pieces(v, count):
        return table.at[v, core, y] if count == 1 else table.at[pl.ds(v, count), core, y]

    def send_up(to, v, count):
        pl.semaphore_wait(ready_z.at[to], 1)
        rows = pieces(v, count)
        to_bl(rows, rows, zs.at[1], zr.at[v], z_peer(to)).start()

    def wait_for(v, count=1):
        rows = pieces(v, count)
        to_bl(rows, rows, zs.at[1], zr.at[v], other).wait_recv()

    def pass_on(v, count=1):
        rows = pieces(v, count)
        for k in (2, 1, 3):
            to_bl(rows, rows, ys.at[0], yr.at[v // HALF], y_peer(k)[0]).start()

    def take_in(v, count=1):
        wait_for(v, count)
        pass_on(v, count)

    def share(half):
        three = table.at[pl.ds(half * HALF, HALF), core, pl.ds(0, 3)]
        to_bl(three, three, ys.at[0], yr.at[half], other).wait_recv()
        four = table.at[pl.ds(half * HALF, HALF), core]
        to_bl(four, four, cs.at[0], cr.at[half], other).start()

    def pick(half, first):
        flipped = jnp.transpose(table[:, half].reshape(256, LANES))
        g_high, g_low = halves(flipped)
        for hot, dst in ((hot1, gp), (hot2, gq)):
            rows = hot[:, half].reshape(256, PAIRS)
            picked = jnp.dot(g_high, rows, preferred_element_type=F32) + jnp.dot(
                g_low, rows, preferred_element_type=F32
            )
            picked = picked.reshape(8, TIMES, CHANNELS, PAIRS)
            dst[...] = picked if first else dst[...] + picked

    def tell_plane():
        pl.semaphore_wait(hub, NY - 1)
        pl.semaphore_signal(ready_y, inc=1, device_id={"bl": z_peer(HALF)}, device_id_type=MESH)

    def line(at):
        for to in range(at + 1, NZ) if at >= HALF else ():
            send_up(to, at, 1)
        if at < HALF:

            @pl.when(second == 1)
            def _():
                pl.semaphore_wait(ready_y, 3)

        else:
            pl.semaphore_wait(ready_y, 1)
        if at == HALF - 1:
            pl.semaphore_wait(ready_z.at[HALF], 1)
        if at in (HALF - 1, HALF):
            for k in (2, 1, 3):
                pl.semaphore_signal(hub, inc=1, device_id={"bl": y_peer(k)[0]}, device_id_type=MESH)
        if at == HALF:
            pl.semaphore_wait(hub, NY - 1)
            for to in (7, 6, 5):
                pl.semaphore_signal(ready_y, inc=1, device_id={"bl": z_peer(to)}, device_id_type=MESH)
        pass_on(at)
        if at < HALF:
            for v in (3, 2, 1, 0):
                if at == HALF - 1 and v == 0:
                    pl.when(early)(tell_plane)
                if v != at:
                    take_in(v)
                if v < at:
                    send_own(v, 0)
            if at == HALF - 1:
                pl.when(jnp.logical_not(early))(tell_plane)
                lower = pieces(0, HALF)
                to_bl(lower, lower, zs.at[1], zr.at[0], z_peer(HALF)).start()
                for to in (5, 6, 7):
                    send_up(to, 0, HALF)
            for v in range(HALF, NZ):
                take_in(v)
                if at == 1:
                    piece = pieces(v, 1)
                    to_bl(piece, piece, zs.at[1], zr.at[v], z_peer(0)).start()
        else:
            for v in range(HALF, NZ):
                if v != at:
                    take_in(v)
            take_in(0, HALF)

    for at in range(NZ):
        pl.when(z == at)(functools.partial(line, at))

    @pl.when((upper == 1) & (core == 0))
    def _():
        pl.semaphore_wait(ready_c, 1)

    share(upper)
    share(1 - upper)
    pick(core, True)
    for half in range(2):
        four = table.at[pl.ds(half * HALF, HALF), 1 - core]
        to_bl(four, four, cs.at[0], cr.at[half], other).wait_recv()
    pick(1 - core, False)

    def compute(i, carry):
        t = lax.div(i, 4)
        at = pl.ds(pl.multiple_of(lax.rem(i, 4) * 128, 128), 128)

        def matrix(ref):
            return [(ref[c, t, :, at], ref[c + 4, t, :, at]) for c in range(4)]

        jp, jq, m, d = matrix(gp), matrix(gq), matrix(model), matrix(meas)
        w = imp[t, :, at]
        a = [
            cmul_add([(jp[2 * r], m[c], False), (jp[2 * r + 1], m[c + 2], False)])
            for r in range(2) for c in range(2)
        ]
        v = [
            cmul_add([(a[2 * r], jq[2 * c], True), (a[2 * r + 1], jq[2 * c + 1], True)])
            for r in range(2) for c in range(2)
        ]
        e = [(w * (d[k][0] - v[k][0]), w * (d[k][1] - v[k][1])) for k in range(4)]
        for k in range(4):
            res[k, t, :, at] = e[k][0]
            res[k + 4, t, :, at] = e[k][1]
        b = [
            cmul_add([(jq[2 * r], m[2 * c], True), (jq[2 * r + 1], m[2 * c + 1], True)])
            for r in range(2) for c in range(2)
        ]
        first = [
            cmul_add([(e[2 * r], b[c], False), (e[2 * r + 1], b[c + 2], False)])
            for r in range(2) for c in range(2)
        ]
        second = [
            cmul_add([(a[c], e[r], True), (a[c + 2], e[r + 2], True)])
            for r in range(2) for c in range(2)
        ]
        for k in range(4):
            gp[k, t, :, at] = first[k][0]
            gp[k + 4, t, :, at] = first[k][1]
            gq[k, t, :, at] = second[k][0]
            gq[k + 4, t, :, at] = second[k][1]
        return carry

    lax.fori_loop(0, 16, compute, 0, unroll=4)

    p_high, p_low = halves(gp[...].reshape(LANES, PAIRS))
    q_high, q_low = halves(gq[...].reshape(LANES, PAIRS))
    nt = (((1,), (1,)), ((), ()))

    def add_up(places):
        h1, h2 = (
            jnp.concatenate([hot[v].reshape(64, PAIRS) for v in places]) for hot in (hot1, hot2)
        )
        total = lax.dot_general(h1, p_high, nt, preferred_element_type=F32)
        total += lax.dot_general(h1, p_low, nt, preferred_element_type=F32)
        total += lax.dot_general(h2, q_high, nt, preferred_element_type=F32)
        total += lax.dot_general(h2, q_low, nt, preferred_element_type=F32)
        for i, v in enumerate(places):
            part[v] = total[i * 64 : i * 64 + 64].reshape(NC, NY, 8, LANES)

    def from_end(v):
        if isinstance(v, int):
            return v + odd * ((v // 2 if v % 2 else NZ - 1 - v // 2) - v)
        far = lax.rem(v, 2)
        return v + odd * (lax.div(v, 2) * (2 * far - 1) + (1 - far) * (NZ - 1) - v)

    def hand_over(step, carry):
        v = from_end(step)
        to_bl(part.at[v, 1 - core], got_c.at[v], rcs.at[0], rcr.at[v], other).start()
        return carry

    def along_y(step, carry):
        v = from_end(step)
        got = got_c.at[v]
        to_bl(got, got, rcs.at[0], rcr.at[v], other).wait_recv()
        part[v, core] = part[v, core] + got_c[v]
        for k in (2, 1, 3):
            peer, to = y_peer(k)
            to_bl(part.at[v, core, to], got_y.at[v, k - 1], rys.at[0], ryr.at[v], peer).start()
        return carry

    def send_on(v):
        @pl.when(v != z)
        def _():
            to_bl(part.at[v, core, y], got_z.at[z], rzs.at[0], rzr.at[0], z_peer(v)).start()

    def along_z(step, carry):
        v = from_end(step)
        got = got_y.at[v]
        to_bl(got, got, rys.at[0], ryr.at[v], other).wait_recv()
        part[v, core, y] = part[v, core, y] + got_y[v, 0] + (got_y[v, 1] + got_y[v, 2])
        send_on(v)
        return carry

    add_up([from_end(v) for v in range(DIRECT)])
    for v in range(DIRECT):
        at_v = from_end(v)
        for slot, (dy, dc) in enumerate(((2, 0), (2, 1), (1, 0), (1, 1), (3, 0), (3, 1), (0, 1))):
            to_y, to_core = lax.rem(y + dy, NY), lax.rem(core + dc, NC)
            to_bl(
                part.at[at_v, to_core, to_y], got_0.at[v, slot], r0s.at[0], r0r.at[v],
                join_index(to_y, z, to_core),
            ).start()
    add_up([DIRECT - odd + v for v in range(NZ - DIRECT)])
    lax.fori_loop(DIRECT, NZ, hand_over, 0)
    lax.fori_loop(DIRECT, NZ, along_y, 0)
    for v in range(DIRECT):
        got = got_0.at[v]
        to_bl(got, got, r0s.at[0], r0r.at[v], other).wait_recv()
        at_v = from_end(v)
        total = part[at_v, core, y]
        for slot in range(7):
            total = total + got_0[v, slot]
        part[at_v, core, y] = total
        send_on(at_v)
    lax.fori_loop(DIRECT, NZ, along_z, 0)
    got_z[z] = part[z, core, y]

    for edge in edges:
        edge.wait_recv()

    @pl.when(early)
    def _():
        for edge in edges:
            edge.start()

    from_prev, from_next = halo_got[0], halo_got[1]
    x = own

    def shift(v, by):
        return pltpu.roll(v, by % LANES, 1)

    prev_edge = jnp.concatenate([pltpu.roll(from_prev, 121, 1), pltpu.roll(from_prev, 122, 1)], axis=1)
    next_edge = jnp.concatenate([pltpu.roll(from_next, 7, 1), pltpu.roll(from_next, 6, 1)], axis=1)
    next_weight = jnp.concatenate([pltpu.roll(from_next, 5, 1)] * 2, axis=1)
    is_first, is_last = freq == 0, freq == CHANNELS - 1
    not_low = jnp.where(chan > 0, 1.0, 0.0).astype(F32)
    not_high = jnp.where(chan < n_chan - 1, 1.0, 0.0).astype(F32)

    def slope(w, step):
        square = step * step
        for by in (128, 64, 32):
            square = square + shift(square, by)
        return w * step / jnp.sqrt(square + SMOOTH_EPS)

    grad = slope(
        jnp.where(is_first, weight * not_low, weight), x - jnp.where(is_first, prev_edge, shift(x, 1))
    )
    grad -= slope(
        jnp.where(is_last, next_weight * not_high, shift(weight, -1)),
        jnp.where(is_last, next_edge, shift(x, -1)) - x,
    )
    grad += slope(jnp.where(time > 0, weight, 0.0), x - shift(x, 8))
    grad -= slope(jnp.where(time < TIMES - 1, weight, 0.0), shift(x, -8) - x)
    updated = x - (STEP * TV_SCALE) * grad

    rows = got_z.at[pl.ds(0, NZ - 1)]
    to_bl(rows, rows, rzs.at[0], rzr.at[0], other).wait_recv()
    total = got_z[0]
    for v in range(1, NZ):
        total = total + got_z[v]
    updated = updated + STEP * total
    upd_ref[...] = jnp.transpose(updated).reshape(8, TIMES, CHANNELS, 8)

    for edge in edges:
        edge.wait_send()

    def left(at):
        for sem, count in ((0, (3, 3, 3, 3, 3, 4, 5, 6)[at]), (1, (0, 4, 0, 16, 3, 2, 1, 0)[at])):
            if count:
                sent = part.at[pl.ds(0, count), 0, 0] if count <= NZ else part.at[pl.ds(0, count // NY), 0]
                to_bl(sent, sent, zs.at[sem], rzr.at[0], other).wait_send()

    for at in range(NZ):
        pl.when(z == at)(functools.partial(left, at))

    to_bl(rows, rows, rzs.at[0], rzr.at[0], other).wait_send()
    half = part.at[pl.ds(0, NZ), 0]
    to_bl(half, half, cs.at[0], rzr.at[0], other).wait_send()
    seven = part.at[pl.ds(0, NZ - DIRECT), 0]
    to_bl(seven, seven, rcs.at[0], rzr.at[0], other).wait_send()
    to_bl(got_0, got_0, r0s.at[0], rzr.at[0], other).wait_send()
    to_bl(got_y, got_y, ys.at[0], rzr.at[0], other).wait_send()
    most = got_y.at[pl.ds(0, NZ - DIRECT)]
    to_bl(most, most, rys.at[0], rzr.at[0], other).wait_send()


def hand_out(updated, residual, updated_h, residual_h, sem):
    copies = [
        pltpu.make_async_copy(residual, residual_h, sem.at[0]),
        pltpu.make_async_copy(updated, updated_h, sem.at[1]),
    ]
    for copy in copies:
        copy.start()
    for copy in copies:
        copy.wait()


def local(meas, model, imp, tally, one, two, gains, tvw):
    big = (8, TIMES, CHANNELS, PAIRS)
    vmem = pltpu.VMEM
    dma = pltpu.SemaphoreType.DMA
    flag = pltpu.SemaphoreType.REGULAR
    any_spec = pl.BlockSpec(memory_space=pl.ANY)
    vmem_spec = pl.BlockSpec(memory_space=pltpu.VMEM)
    updated, residual = pl.pallas_call(
        kernel,
        out_shape=(vmem((8, TIMES, CHANNELS, 8), F32), vmem(big, F32)),
        in_specs=[any_spec] * 8,
        out_specs=(vmem_spec, vmem_spec),
        scratch_shapes=[
            vmem(big, F32), vmem(big, F32), vmem((TIMES, CHANNELS, PAIRS), F32),
            vmem((1, PAIRS), jnp.int32), vmem((1, PAIRS), jnp.int32), vmem((1, PAIRS), jnp.int32),
            vmem((8, TIMES, CHANNELS, 8), F32), vmem((CHANNELS, 8), F32),
            vmem((NZ, NC, NY, 8, LANES), F32), vmem((NZ, NC, 32, PAIRS), BF16), vmem((NZ, NC, 32, PAIRS), BF16),
            vmem(big, F32), vmem(big, F32), vmem((NZ, NC, NY, 8, LANES), F32),
            vmem((DIRECT, 7, 8, LANES), F32), vmem((NZ, NY, 8, LANES), F32), vmem((NZ, NY - 1, 8, LANES), F32), vmem((NZ, 8, LANES), F32),
            vmem((8, 128), F32), vmem((2, 8, 128), F32),
            dma((8,)), dma((2,)), dma((NZ,)), dma((1,)), dma((2,)), dma((1,)), dma((2,)), dma((2,)), dma((2,)),
            dma((1,)), dma((DIRECT,)), dma((1,)), dma((NZ,)), dma((1,)), dma((NZ,)), dma((1,)), dma((1,)),
            flag((NZ,)), flag, flag, flag,
        ],
        compiler_params=pltpu.CompilerParams(
            collective_id=0, has_side_effects=True, vmem_limit_bytes=58 * 1024 * 1024
        ),
    )(meas, model, imp, tally, one.reshape(1, PAIRS), two.reshape(1, PAIRS), gains, tvw)
    held = [pltpu.with_memory_space_constraint(x, pltpu.VMEM) for x in (updated, residual)]
    return pl.pallas_call(
        hand_out,
        out_shape=(jax.ShapeDtypeStruct(updated.shape, F32), jax.ShapeDtypeStruct(residual.shape, F32)),
        in_specs=[vmem_spec, vmem_spec],
        out_specs=(any_spec, any_spec),
        scratch_shapes=[dma((2,))],
    )(*held)


def solution(mesh):
    placed = (
        P(None, None, "chan", "bl"),
        P(None, None, "chan", "bl"),
        P(None, "chan", "bl"),
        P("chan", "bl"),
        P("bl"),
        P("bl"),
        P(None, None, "chan", "bl"),
        P("chan", "bl"),
    )
    return jax.shard_map(
        local,
        mesh=mesh,
        in_specs=placed,
        out_specs=(P(None, None, "chan", "bl"), P(None, None, "chan", "bl")),
        check_vma=False,
    )
```
